32 devices in a mesh: groups: 2 (over x), tensor: 16 (over z, y, core).
Axes of the slice: x: 2, y: 2, z: 4, core: 2. Of those that a mesh axis runs over, the one named last changes fastest.
Arguments:
- activations: bfloat16 [256, 26624], P('groups', 'tensor'), parts along dimension 0, may hold values from -6 to 6
- rotation_small: float32 [52, 52], replicated, may hold values from -0.875 to 0.875
- down_weight: bfloat16 [26624, 8192], P('tensor'), may hold values from -0.0546875 to 0.0546875
Outputs:
- projected: bfloat16 [256, 8192], P('groups', 'tensor'), parts along dimension 0
The draws below stay inside these ranges and needn't reach their ends.
There are 2 independent parts, one for each index of `groups`. The reference program is written for one: setup_inputs(seed, part) draws one part's arguments, and reference() takes and returns one part's arrays. A program takes and returns all parts, laid end to end along the dimension named above; an argument that names none is the same for every part. Nothing has to cross between parts.
All inputs are finite; a program needn't handle non-finite values.
Results may differ from the reference program's by a relative error of at most 0.005.
Values sent between devices are 32-bit elements; how exact they have to be, the bound alone decides.
No kernel may reach another device: no remote copies, remote signals or barrier semaphores. Data moves between devices by JAX's collectives and lax.ppermute only.
A program may use at most 128 MiB of HBM per device.

```python
import jax
import jax.numpy as jnp
from jax import lax

D = 8192
FF = 26624
BLOCK = 52
TOK = 128


def with_spikes(entries, rng, source, target, blocks, factor):
    def block_of(dim):
        return (jnp.arange(entries.shape[dim]) // (entries.shape[dim] // blocks)).reshape((-1,) + (1,) * (entries.ndim - 1 - dim))

    near = jax.random.permutation(rng, blocks)[block_of(target)]
    second = (block_of(target) + blocks // 2) % blocks
    return jnp.where((block_of(source) == near) | (block_of(source) == second), factor * entries, entries)


def block_scale(stream_key, dims, shards, smallest, top_value):
    level, own = 1.0, jax.random.fold_in(stream_key, 6)
    for axis_at, shards_of in shards:
        draws = jnp.exp(jax.random.uniform(jax.random.fold_in(own, axis_at), (shards_of,), jnp.float32, smallest / len(shards), top_value / len(shards)))
        level = level * jnp.repeat(draws, dims[axis_at] // shards_of).reshape([-1 if axis == axis_at else 1 for axis in range(len(dims))])
    return level


def bell_draw(key, extent, deviation, reach, pieces=(), kind=jnp.bfloat16):
    values = deviation * jax.random.normal(key, extent, jnp.float32)
    if pieces:
        values = values * block_scale(key, extent, pieces, -0.22, 0.18)
    return jnp.clip(values, -reach, reach).astype(kind)


def heavy_noise(own_key, extent, deviation, reach, pieces, heavy, kind=jnp.bfloat16):
    entries = deviation * jax.random.normal(own_key, extent, jnp.float32)
    if pieces:
        entries = entries * block_scale(own_key, extent, pieces, -0.22, 0.18)
    return jnp.clip(with_spikes(entries, jax.random.fold_in(own_key, 3), *heavy), -reach, reach).astype(kind)


def setup_inputs(seed: int = 0, part: int = 0) -> dict:
    arg_keys = jax.random.split(jax.random.key(seed), 4)
    part_keys = jax.random.split(jax.random.fold_in(arg_keys[3], part), 4)
    activations = bell_draw(part_keys[0], (TOK, FF), 1.0, 6.0, ((1, 16),))
    rotation_small = bell_draw(arg_keys[1], (BLOCK, BLOCK), BLOCK ** -0.5, 0.875, (), jnp.float32)
    down_weight = heavy_noise(arg_keys[2], (FF, D), FF ** -0.5, 0.0546875, ((0, 16),), (0, 1, 16, 2.0))
    return {"activations": activations, "rotation_small": rotation_small, "down_weight": down_weight}


def sylvester(order):
    index = jnp.arange(order, dtype=jnp.int32)
    common = jnp.zeros((order, order), jnp.int32)
    for place in range(max(order.bit_length(), 1)):
        common = common + ((index[:, None] >> place) & 1) * ((index[None, :] >> place) & 1)
    return (1 - 2 * (common % 2)).astype(jnp.float32)


def reference(activations, rotation_small, down_weight):
    power = FF // BLOCK
    values = activations.astype(jnp.float32).reshape(TOK, power, BLOCK)
    hadamard = sylvester(power)
    mixed = jnp.einsum("tpq,pa->taq", values, hadamard, precision=lax.Precision.HIGHEST)
    mixed = jnp.einsum("taq,qb->tab", mixed, rotation_small.astype(jnp.float32), precision=lax.Precision.HIGHEST)
    rotated = (mixed * (power ** -0.5)).reshape(TOK, FF).astype(jnp.bfloat16)
    return jnp.dot(rotated, down_weight, preferred_element_type=jnp.float32).astype(jnp.bfloat16)
```

```python
import functools

import jax
import jax.numpy as jnp
import numpy as np
from jax import lax
from jax.experimental import pallas as pl
from jax.experimental.pallas import tpu as pltpu
from jax.sharding import PartitionSpec as P

LANES = 128
F32 = jnp.float32
BF16 = jnp.bfloat16


def quotient(index, divisor, limit):
    shift = 16
    scale = -(-(1 << shift) // divisor)
    numbers = np.arange(limit, dtype=np.int64)
    assert np.array_equal((numbers * scale) >> shift, numbers // divisor)
    assert limit * scale < 2**31
    return (index * scale) >> shift


def sign_of(common, count):
    parity = common
    for place in range(1, count):
        parity = parity ^ (common >> place)
    return (1 - 2 * (parity & 1)).astype(F32)


def mix_kernel(start, group, activations, small, out):
    tokens, local = activations.shape
    block = small.shape[0]
    cols = out.shape[1]
    rows = group * block
    span = local // block
    low = group.bit_length() - 1
    high = span.bit_length() - 1 - low
    full = small[...]
    head = full.astype(BF16)
    tail = (full - head.astype(F32)).astype(BF16)

    row = lax.broadcasted_iota(jnp.int32, (rows, block), 0)
    unit = lax.broadcasted_iota(jnp.int32, (rows, block), 1)
    spread_rows = (row - quotient(row, block, rows) * block == unit).astype(F32).astype(BF16)
    col = lax.broadcasted_iota(jnp.int32, (block, cols), 1) + start
    unit = lax.broadcasted_iota(jnp.int32, (block, cols), 0)
    spread_cols = (col - quotient(col, block, local) * block == unit).astype(F32).astype(BF16)
    at_row = quotient(lax.broadcasted_iota(jnp.int32, (rows, cols), 0), block, rows)
    at_col = quotient(lax.broadcasted_iota(jnp.int32, (rows, cols), 1) + start, block, local)
    sign = sign_of(at_row & at_col, max(low, 1))

    def tiled(part):
        tall = jnp.dot(spread_rows, part, preferred_element_type=F32).astype(BF16)
        return (jnp.dot(tall, spread_cols, preferred_element_type=F32) * sign).astype(BF16)

    head, tail = tiled(head), tiled(tail)
    owner = quotient(lax.broadcasted_iota(jnp.int32, (8, cols), 1) + start, block, local) >> low
    total = jnp.zeros((tokens, cols), F32)
    for piece in range(span // group):
        values = activations[:, piece * rows:(piece + 1) * rows]
        term = jnp.dot(values, head, preferred_element_type=F32)
        term = term + jnp.dot(values, tail, preferred_element_type=F32)
        total = total + term * sign_of(owner & piece, max(high, 1))[0:1]
    out[...] = total


def mix(activations, small, start, cols):
    tokens, local = activations.shape
    block = small.shape[0]
    span = local // block
    group = min(4, span)
    return pl.pallas_call(
        functools.partial(mix_kernel, start, group),
        out_shape=jax.ShapeDtypeStruct((tokens, cols), F32),
        in_specs=[pl.BlockSpec(memory_space=pltpu.VMEM)] * 2,
        out_specs=pl.BlockSpec(memory_space=pltpu.VMEM),
        cost_estimate=pl.CostEstimate(
            flops=4 * tokens * local * cols, bytes_accessed=tokens * (2 * local + 4 * cols), transcendentals=0
        ),
        compiler_params=pltpu.CompilerParams(vmem_limit_bytes=24 * 2**20),
        name="mix",
    )(activations, small)


def product_kernel(edges, order, *refs):
    chunks, weight, out = refs[:-2], refs[-2], refs[-1]
    total = None
    for chunk, begin, end in zip(chunks, edges[:-1], edges[1:]):
        term = jnp.dot(chunk[...], weight[begin:end, :], preferred_element_type=F32)
        total = term if total is None else total + term
    out[0] = total


def product(chunks, weight, me, edges, order, width, part, parts):
    tokens = chunks[0].shape[0]
    local = weight.shape[0]
    blocks = len(order)
    table = jnp.asarray(np.array(order, np.int32)) ^ me

    def kernel(table_ref, *refs):
        product_kernel(edges, order, *refs)

    return pl.pallas_call(
        kernel,
        grid_spec=pltpu.PrefetchScalarGridSpec(
            num_scalar_prefetch=1,
            grid=(blocks,),
            in_specs=[pl.BlockSpec(chunk.shape, lambda i, t: (0, 0)) for chunk in chunks]
            + [pl.BlockSpec((local, width), lambda i, t: (0, t[i] * parts + part))],
            out_specs=pl.BlockSpec((1, tokens, width), lambda i, t: (i, 0, 0)),
        ),
        out_shape=jax.ShapeDtypeStruct((blocks, tokens, width), F32),
        cost_estimate=pl.CostEstimate(
            flops=2 * tokens * local * width * blocks,
            bytes_accessed=blocks * width * (2 * local + 4 * tokens),
            transcendentals=0,
        ),
        compiler_params=pltpu.CompilerParams(vmem_limit_bytes=24 * 2**20),
        name="product",
    )(table, *chunks, weight)


def relative_owners(bits):
    found = [0]
    for bit in bits:
        found = [value | extra for value in found for extra in (0, bit)]
    return found


def body(activations, rotation_small, down_weight):
    shards = lax.axis_size("tensor")
    me = lax.axis_index("tensor")
    tokens, local = activations.shape
    block = rotation_small.shape[0]
    features = down_weight.shape[1]
    factor = (local // block * shards) ** (-0.5)
    bits = [1 << place for place in range(shards.bit_length() - 1)]

    def swap(x, bit):
        return lax.ppermute(x, "tensor", [(d, d ^ bit) for d in range(shards)])

    tiles = -(-local // LANES)
    count = max(1, min(len(bits), tiles))
    edges = [min(local, (tiles * c // count) * LANES) for c in range(count)] + [local]
    chunks = [mix(activations, rotation_small, a, b - a) for a, b in zip(edges[:-1], edges[1:])]
    cycle = bits[::-1][:1] + bits[1:-1] + bits[:1] if len(bits) > 1 else bits
    for phase in range(len(bits)):
        for c in range(count):
            bit = cycle[(phase - c) % len(bits)]
            sign = jnp.where(me & bit, -1.0, 1.0).astype(F32)
            chunks[c] = swap(chunks[c], bit) + sign * chunks[c]
    chunks = [(chunk * factor).astype(BF16) for chunk in chunks]

    share = features // shards
    parts = 2 if share % (2 * LANES) == 0 else 1
    width = share // parts
    results = []
    for part in range(parts):
        order = list(bits)
        if part and len(bits) > 2:
            order[1], order[2] = order[2], order[1]
        owners = relative_owners(order)
        half = len(owners) // 2
        send = product(chunks, down_weight, me, edges, owners[half:], width, part, parts)
        keep = product(chunks, down_weight, me, edges, owners[:half], width, part, parts)
        for bit in order:
            keep = keep + swap(send, bit)
            half = keep.shape[0] // 2
            if half:
                keep, send = keep[:half], keep[half:]
        results.append(keep[0])
    return jnp.concatenate(results, axis=1).astype(BF16)


def solution(mesh):
    placed = (P("groups", "tensor"), P(), P("tensor", None))
    return jax.shard_map(
        body, mesh=mesh, in_specs=placed, out_specs=P("groups", "tensor"), check_vma=False
    )
```

```python
import functools

import jax
import jax.numpy as jnp
import numpy as np
from jax import lax
from jax.experimental import pallas as pl
from jax.experimental.pallas import tpu as pltpu
from jax.sharding import PartitionSpec as P

LANES = 128
F32 = jnp.float32
BF16 = jnp.bfloat16


def quotient(index, divisor, limit):
    shift = 16
    scale = -(-(1 << shift) // divisor)
    numbers = np.arange(limit, dtype=np.int64)
    assert np.array_equal((numbers * scale) >> shift, numbers // divisor)
    assert limit * scale < 2**31
    return (index * scale) >> shift


def sign_of(common, count):
    parity = common
    for place in range(1, count):
        parity = parity ^ (common >> place)
    return (1 - 2 * (parity & 1)).astype(F32)


def mix_kernel(start, group, activations, small, *refs):
    out = refs[-1]
    tokens, local = activations.shape
    block = small.shape[0]
    cols = out.shape[1]
    rows = group * block
    span = local // block
    low = group.bit_length() - 1
    high = span.bit_length() - 1 - low
    full = small[...]
    head = full.astype(BF16)
    tail = (full - head.astype(F32)).astype(BF16)

    row = lax.broadcasted_iota(jnp.int32, (rows, block), 0)
    unit = lax.broadcasted_iota(jnp.int32, (rows, block), 1)
    spread_rows = (row - quotient(row, block, rows) * block == unit).astype(F32).astype(BF16)
    col = lax.broadcasted_iota(jnp.int32, (block, cols), 1) + start
    unit = lax.broadcasted_iota(jnp.int32, (block, cols), 0)
    spread_cols = (col - quotient(col, block, local) * block == unit).astype(F32).astype(BF16)
    at_row = quotient(lax.broadcasted_iota(jnp.int32, (rows, cols), 0), block, rows)
    at_col = quotient(lax.broadcasted_iota(jnp.int32, (rows, cols), 1) + start, block, local)
    sign = sign_of(at_row & at_col, max(low, 1))

    def tiled(part):
        tall = jnp.dot(spread_rows, part, preferred_element_type=F32).astype(BF16)
        return (jnp.dot(tall, spread_cols, preferred_element_type=F32) * sign).astype(BF16)

    head, tail = tiled(head), tiled(tail)
    owner = quotient(lax.broadcasted_iota(jnp.int32, (8, cols), 1) + start, block, local) >> low
    total = jnp.zeros((tokens, cols), F32)
    for piece in range(span // group):
        values = activations[:, piece * rows:(piece + 1) * rows]
        term = jnp.dot(values, head, preferred_element_type=F32)
        term = term + jnp.dot(values, tail, preferred_element_type=F32)
        total = total + term * sign_of(owner & piece, max(high, 1))[0:1]
    out[...] = total


VMEM = pl.BlockSpec(memory_space=pltpu.VMEM)
SMEM = pl.BlockSpec(memory_space=pltpu.SMEM)
UNREAD = pl.BlockSpec(memory_space=pl.ANY)
PARAMS = pltpu.CompilerParams(vmem_limit_bytes=24 * 2**20)


def mix(activations, small, start, cols, after):
    tokens, local = activations.shape
    block = small.shape[0]
    group = min(4, local // block)
    return pl.pallas_call(
        functools.partial(mix_kernel, start, group),
        out_shape=jax.ShapeDtypeStruct((tokens, cols), F32),
        in_specs=[VMEM] * 2 + [UNREAD] * len(after),
        out_specs=VMEM,
        cost_estimate=pl.CostEstimate(
            flops=4 * tokens * local * cols, bytes_accessed=tokens * (2 * local + 4 * cols), transcendentals=0
        ),
        compiler_params=PARAMS,
        name="mix",
    )(activations, small, *after)


def fold(me, own, got, bit, after, factor=None):
    sign = jnp.where((me[0] & bit) != 0, -1.0, 1.0).astype(F32)
    if after:
        own, *_ = lax.optimization_barrier((own, *after))
    total = got + sign * own
    return total if factor is None else (total * factor).astype(BF16)


def product(chunks, weight, me, edges, distances, width, part, parts, after):
    tokens = chunks[0].shape[0]
    local = weight.shape[0]
    blocks = len(distances)
    count = len(chunks)
    slots = min(3, blocks)

    def kernel(me_ref, *refs):
        chunk_refs, weight_ref = refs[:count], refs[count]
        out, left, held, sems = refs[-4:]

        def fetch(i):
            column = pl.multiple_of(((distances[i] ^ me_ref[0]) * parts + part) * width, LANES)
            return pltpu.make_async_copy(
                weight_ref.at[:, pl.ds(column, width)], held.at[i % slots], sems.at[i % slots]
            )

        for i in range(slots):
            fetch(i).start()
        for ref, begin, end in zip(chunk_refs, edges[:-1], edges[1:]):
            left[:, begin:end] = ref[...]
        for i in range(blocks):
            fetch(i).wait()
            out[i] = jnp.dot(left[...], held[i % slots], preferred_element_type=F32)
            if i + slots < blocks:
                fetch(i + slots).start()

    return pl.pallas_call(
        kernel,
        out_shape=jax.ShapeDtypeStruct((blocks, tokens, width), F32),
        in_specs=[SMEM] + [VMEM] * count + [pl.BlockSpec(memory_space=pltpu.HBM)] + [UNREAD] * len(after),
        out_specs=VMEM,
        scratch_shapes=[
            pltpu.VMEM((tokens, local), BF16),
            pltpu.VMEM((slots, local, width), BF16),
            pltpu.SemaphoreType.DMA((slots,)),
        ],
        cost_estimate=pl.CostEstimate(
            flops=2 * tokens * local * width * blocks,
            bytes_accessed=blocks * width * (2 * local + 4 * tokens),
            transcendentals=0,
        ),
        compiler_params=pltpu.CompilerParams(vmem_limit_bytes=44 * 2**20),
        name="product",
    )(me, *chunks, weight, *after)


def halve(own, got, distances, plans, after):
    width = own.shape[2]
    shapes = []
    for rows, bit in plans:
        shapes += [jax.ShapeDtypeStruct((len(distances) // 2, rows[1] - rows[0], width), F32)] * 2

    def kernel(own_ref, got_ref, *refs):
        outs = refs[-len(shapes):]
        for at, ((begin, end), bit) in enumerate(plans):
            kept = [d for d in distances if not d & bit]
            for place, d in enumerate(kept):
                for out, source in ((outs[2 * at], d), (outs[2 * at + 1], d | bit)):
                    i = distances.index(source)
                    out[place] = own_ref[i, begin:end, :] + got_ref[i, begin:end, :]

    return pl.pallas_call(
        kernel,
        out_shape=shapes,
        in_specs=[VMEM] * 2 + [UNREAD] * len(after),
        out_specs=[VMEM] * len(shapes),
        cost_estimate=pl.CostEstimate(flops=own.size, bytes_accessed=12 * own.size, transcendentals=0),
        compiler_params=PARAMS,
        name="halve",
    )(own, got, *after)


def finish(pieces, tokens, width, parts):
    flat = [x for _, _, own, got in pieces for x in (own, got)]

    def kernel(*refs):
        out = refs[-1]
        for at, (part, (begin, end), _, _) in enumerate(pieces):
            total = refs[2 * at][0] + refs[2 * at + 1][0]
            out[begin:end, part * width:(part + 1) * width] = total.astype(BF16)

    return pl.pallas_call(
        kernel,
        out_shape=jax.ShapeDtypeStruct((tokens, width * parts), BF16),
        in_specs=[VMEM] * len(flat),
        out_specs=VMEM,
        compiler_params=PARAMS,
        name="finish",
    )(*flat)


def body(activations, rotation_small, down_weight):
    shards = lax.axis_size("tensor")
    me = lax.axis_index("tensor").astype(jnp.int32).reshape(1)
    tokens, local = activations.shape
    block = rotation_small.shape[0]
    features = down_weight.shape[1]
    factor = (local // block * shards) ** (-0.5)
    bits = [1 << place for place in range(shards.bit_length() - 1)]
    assert len(bits) >= 2 and shards == 1 << len(bits)

    def swap(x, bit):
        return lax.ppermute(x, "tensor", [(d, d ^ bit) for d in range(shards)])

    tiles = -(-local // LANES)
    count = max(1, min(len(bits), tiles))
    edges = [min(local, (tiles * c // count) * LANES) for c in range(count)] + [local]
    chunks = []
    for begin, end in zip(edges[:-1], edges[1:]):
        chunks.append(mix(activations, rotation_small, begin, end - begin, chunks[-1:]))
    cycle = bits[-1:] + bits[1:-1] + bits[:1]
    events = []
    for phase in range(len(bits)):
        for c in range(count):
            bit = cycle[(phase - c) % len(bits)]
            events.append((phase, bit, c))
    after = []
    for phase, bit, c in sorted(events):
        got = swap(chunks[c], bit)
        chunks[c] = fold(me, chunks[c], got, bit, after, factor if phase == len(bits) - 1 else None)
        after = [chunks[c]]

    share = features // shards
    parts = 2 if share % (2 * LANES) == 0 else 1
    width = share // parts
    order = list(bits)
    twisted = list(bits)
    if len(bits) > 2:
        twisted[1], twisted[2] = twisted[2], twisted[1]
    near = [d for d in range(shards) if not d & bits[0]]
    sends, keeps = [], []
    after = []
    for part in range(parts):
        for found, distances in ((sends, [d | bits[0] for d in near]), (keeps, near)):
            found.append(product(chunks, down_weight, me, edges, distances, width, part, parts, after))
            after = [found[-1]]
    half = tokens // 2
    whole = (0, tokens)
    routes = [[(whole, order)], [((0, half), order), ((half, tokens), twisted)]][-parts:]
    live = []
    for part in range(parts):
        got = swap(sends[part], bits[0])
        plans = [(rows, route[1]) for rows, route in routes[part]]
        outs = halve(keeps[part], got, near, plans, after)
        after = outs[-1:]
        for at, (rows, route) in enumerate(routes[part]):
            live.append((part, rows, route, [d for d in near if not d & route[1]], outs[2 * at], outs[2 * at + 1]))
    live = live[:1] + live[:0:-1]
    for step in range(1, len(bits) - 1):
        later = []
        for part, rows, route, distances, keep, send in live:
            got = swap(send, route[step])
            bit = route[step + 1]
            outs = halve(keep, got, distances, [((0, rows[1] - rows[0]), bit)], after)
            after = outs[-1:]
            later.append((part, rows, route, [d for d in distances if not d & bit], outs[0], outs[1]))
        live = later
    pieces = [(part, rows, keep, swap(send, route[-1])) for part, rows, route, _, keep, send in live]
    return finish(pieces, tokens, width, parts)


def solution(mesh):
    placed = (P("groups", "tensor"), P(), P("tensor", None))
    return jax.shard_map(
        body, mesh=mesh, in_specs=placed, out_specs=P("groups", "tensor"), check_vma=False
    )
```

```python
import functools

import jax
import jax.numpy as jnp
import numpy as np
from jax import lax
from jax.experimental import pallas as pl
from jax.experimental.pallas import tpu as pltpu
from jax.sharding import PartitionSpec as P

LANES = 128
F32 = jnp.float32
BF16 = jnp.bfloat16


def quotient(index, divisor, limit):
    shift = 16
    scale = -(-(1 << shift) // divisor)
    numbers = np.arange(limit, dtype=np.int64)
    assert np.array_equal((numbers * scale) >> shift, numbers // divisor)
    assert limit * scale < 2**31
    return (index * scale) >> shift


def sign_of(common, count):
    parity = common
    for place in range(1, count):
        parity = parity ^ (common >> place)
    return (1 - 2 * (parity & 1)).astype(F32)


def mix_kernel(rows, start, group, activations, small, *refs):
    out = refs[-1]
    local = activations.shape[1]
    block = small.shape[0]
    tokens, cols = out.shape
    tall = group * block
    span = local // block
    low = group.bit_length() - 1
    high = span.bit_length() - 1 - low
    full = small[...]
    head = full.astype(BF16)
    tail = (full - head.astype(F32)).astype(BF16)

    row = lax.broadcasted_iota(jnp.int32, (tall, block), 0)
    unit = lax.broadcasted_iota(jnp.int32, (tall, block), 1)
    spread_rows = (row - quotient(row, block, tall) * block == unit).astype(F32).astype(BF16)
    col = lax.broadcasted_iota(jnp.int32, (block, cols), 1) + start
    unit = lax.broadcasted_iota(jnp.int32, (block, cols), 0)
    spread_cols = (col - quotient(col, block, local) * block == unit).astype(F32).astype(BF16)
    at_row = quotient(lax.broadcasted_iota(jnp.int32, (tall, cols), 0), block, tall)
    at_col = quotient(lax.broadcasted_iota(jnp.int32, (tall, cols), 1) + start, block, local)
    sign = sign_of(at_row & at_col, max(low, 1))

    def tiled(part):
        rolled = jnp.dot(spread_rows, part, preferred_element_type=F32).astype(BF16)
        return (jnp.dot(rolled, spread_cols, preferred_element_type=F32) * sign).astype(BF16)

    head, tail = tiled(head), tiled(tail)
    owner = quotient(lax.broadcasted_iota(jnp.int32, (8, cols), 1) + start, block, local) >> low
    total = jnp.zeros((tokens, cols), F32)
    for piece in range(span // group):
        values = activations[rows[0]:rows[1], piece * tall:(piece + 1) * tall]
        term = jnp.dot(values, head, preferred_element_type=F32)
        term = term + jnp.dot(values, tail, preferred_element_type=F32)
        total = total + term * sign_of(owner & piece, max(high, 1))[0:1]
    out[...] = total


VMEM = pl.BlockSpec(memory_space=pltpu.VMEM)
SMEM = pl.BlockSpec(memory_space=pltpu.SMEM)
UNREAD = pl.BlockSpec(memory_space=pl.ANY)
COST = pl.CostEstimate(flops=10**10, bytes_accessed=10**8, transcendentals=0)


def call(name, kernel, operands, specs, shapes, after, scratch=(), limit=16):
    return pl.pallas_call(
        kernel,
        out_shape=shapes,
        in_specs=list(specs) + [UNREAD] * len(after),
        out_specs=jax.tree.map(lambda _: VMEM, shapes),
        scratch_shapes=list(scratch),
        cost_estimate=COST,
        compiler_params=pltpu.CompilerParams(vmem_limit_bytes=limit * 2**20),
        name=name,
    )(*operands, *after)


def mix(activations, small, rows, cols, after):
    block = small.shape[0]
    group = min(4, activations.shape[1] // block)
    kernel = functools.partial(mix_kernel, rows, cols[0], group)
    shape = jax.ShapeDtypeStruct((rows[1] - rows[0], cols[1] - cols[0]), F32)
    return call("mix", kernel, (activations, small), (VMEM, VMEM), shape, after)


def fold(me, own, got, bit, after, factor=None):
    def kernel(me_ref, own_ref, got_ref, *refs):
        sign = jnp.where((me_ref[0] & bit) != 0, -1.0, 1.0).astype(F32)
        total = got_ref[...] + own_ref[...] * sign
        if factor is not None:
            total = total * factor
        refs[-1][...] = total.astype(refs[-1].dtype)

    shape = jax.ShapeDtypeStruct(own.shape, F32 if factor is None else BF16)
    return call("fold", kernel, (me, own, got), (SMEM, VMEM, VMEM), shape, after)


def gather(me, weight, rows, distances, width, columns, sems):
    parts = 1 + max(part for _, part in distances)
    copies = []
    for i, (distance, part) in enumerate(distances):
        column = pl.multiple_of(((distance ^ me) * parts + part) * width, LANES)
        copies.append(
            pltpu.make_async_copy(
                weight.at[rows[0]:rows[1], pl.ds(column, width)], columns.at[:, pl.ds(i * width, width)], sems.at[i]
            )
        )
    return copies


def step(me, chunk, columns, total, weight, rows, distances, width, after):
    blocks = len(distances)
    values = [] if chunk is None else [chunk, columns] + ([] if total is None else [total])
    wide = max(width, min(1024, blocks * width))

    def kernel(me_ref, weight_ref, *refs):
        refs, sems = refs[:-1], refs[-1]
        loaded = refs[-1]
        copies = gather(me_ref[0], weight_ref, rows, distances, width, loaded, sems)
        for copy in copies:
            copy.start()
        if chunk is not None:
            out = refs[-2]
            for at in range(0, blocks * width, wide):
                sums = jnp.dot(refs[0][...], refs[1][:, at:at + wide], preferred_element_type=F32)
                for i in range(wide // width):
                    term = sums[:, i * width:(i + 1) * width]
                    out[at // width + i] = term if total is None else refs[2][at // width + i] + term
        for copy in copies:
            copy.wait()

    shapes = [jax.ShapeDtypeStruct((rows[1] - rows[0], blocks * width), BF16)]
    if chunk is not None:
        shapes.insert(0, jax.ShapeDtypeStruct((blocks, chunk.shape[0], width), F32))
    outs = call(
        "step",
        kernel,
        (me, weight, *values),
        [SMEM, pl.BlockSpec(memory_space=pltpu.HBM)] + [VMEM] * len(values),
        shapes,
        after,
        [pltpu.SemaphoreType.DMA((blocks,))],
        40 if chunk is None else 28,
    )
    return (None, *outs) if chunk is None else outs


def product(chunk, columns, total, begin, end, after):
    width = total.shape[2]
    wide = max(width, min(1024, (end - begin) * width))

    def kernel(chunk_ref, columns_ref, total_ref, *refs):
        out = refs[-1]
        for at in range(begin * width, end * width, wide):
            sums = jnp.dot(chunk_ref[...], columns_ref[:, at:at + wide], preferred_element_type=F32)
            for i in range(wide // width):
                block = at // width + i
                out[block - begin] = total_ref[block] + sums[:, i * width:(i + 1) * width]

    shape = jax.ShapeDtypeStruct((end - begin, chunk.shape[0], width), F32)
    return call("product", kernel, (chunk, columns, total), [VMEM] * 3, shape, after)


def halve(own, got, distances, plans, after):
    shapes = []
    for rows, _ in plans:
        shapes += [jax.ShapeDtypeStruct((len(distances) // 2, rows[1] - rows[0], own.shape[2]), F32)] * 2

    def kernel(own_ref, got_ref, *refs):
        outs = refs[-len(shapes):]
        for at, ((begin, end), bit) in enumerate(plans):
            for place, d in enumerate(d for d in distances if not d & bit):
                for out, source in ((outs[2 * at], d), (outs[2 * at + 1], d | bit)):
                    i = distances.index(source)
                    out[place] = own_ref[i, begin:end, :] + got_ref[i, begin:end, :]

    return call("halve", kernel, (own, got), (VMEM, VMEM), shapes, after)


def tick(after):
    def kernel(*refs):
        refs[-1][...] = jnp.zeros_like(refs[-1])

    return call("tick", kernel, (), (), jax.ShapeDtypeStruct((8, LANES), F32), after)


def finish(pieces, own, got, tokens, width, parts, after):
    held = [x for _, _, x in pieces[:-1]] if len(pieces) > 1 else []

    def kernel(own_ref, got_ref, *refs):
        out = refs[-1]
        value = (own_ref[0] + got_ref[0]).astype(BF16)
        if not pieces:
            out[...] = value
            return
        for ((begin, end), part, _), ref in zip(pieces, [*refs[:len(held)], None]):
            out[begin:end, part * width:(part + 1) * width] = value if ref is None else ref[...]

    shape = (tokens, width * parts) if pieces else own.shape[1:]
    operands = (own, got, *held)
    return call("finish", kernel, operands, [VMEM] * len(operands), jax.ShapeDtypeStruct(shape, BF16), after)


def body(activations, rotation_small, down_weight):
    shards = lax.axis_size("tensor")
    me = lax.axis_index("tensor").astype(jnp.int32).reshape(1)
    tokens, local = activations.shape
    block = rotation_small.shape[0]
    share = down_weight.shape[1] // shards
    factor = (local // block * shards) ** (-0.5)
    bits = [1 << place for place in range(shards.bit_length() - 1)]
    assert len(bits) >= 3 and shards == 1 << len(bits)
    after = []

    def swap(x, bit):
        return lax.ppermute(x, "tensor", [(d, d ^ bit) for d in range(shards)])

    def ran(outs, link=-1):
        after[:] = [jax.tree.leaves(outs)[link]]
        return outs

    parts = 2 if share % (2 * LANES) == 0 else 1
    width = share // parts
    near = [d for d in range(shards) if not d & bits[0]]
    groups = [(part, kept) for part in range(parts) for kept in (False, True)]
    distances = [(d | (0 if kept else bits[0]), part) for part, kept in groups for d in near]

    tiles = -(-local // LANES)
    count = max(1, min(len(bits), tiles))
    edges = [min(local, (tiles * c // count) * LANES) for c in range(count)] + [local]
    spans = list(zip(edges[:-1], edges[1:]))
    chunks = []
    for span in spans:
        chunks.append(ran(mix(activations, rotation_small, (0, tokens), span, after)))
    cycle = bits[-1:] + bits[1:-1] + bits[:1]
    events = []
    for phase in range(len(bits)):
        for c in range(count):
            events.append((phase, cycle[(phase - c) % len(bits)], c))
    events.sort()
    final = [c for phase, _, c in events if phase == len(bits) - 1]
    total = None
    for number, (phase, bit, c) in enumerate(events):
        got = swap(chunks[c], bit)
        last = phase == len(bits) - 1
        chunks[c] = ran(fold(me, chunks[c], got, bit, after, factor if last else None))
        if number == len(events) - count - 2:
            _, columns = ran(step(me, None, None, None, down_weight, spans[final[0]], distances, width, after))
        if last and c != final[-1]:
            rows = spans[final[final.index(c) + 1]]
            total, columns = ran(step(me, chunks[c], columns, total, down_weight, rows, distances, width, after))

    inner = bits[1:]
    late = inner[-1:] + inner[:-1]
    swapped = [inner[1], inner[0]] + inner[2:]
    half = tokens // 2
    routes = [
        [((0, half), inner), ((half, tokens), late)],
        [((0, half), swapped), ((half, tokens), inner)],
    ][:parts]
    free = dict.fromkeys(bits, 0.0)
    clock = 0.0
    kernels = 0
    pieces = []
    queue = []

    def send(x, bit, use):
        nonlocal clock
        clock += 0.7
        micros = x.size * 4e-6 * (2 if bit == bits[0] else 40 if bit == bits[-1] else 20)
        free[bit] = max(clock + 1.0, free[bit]) + micros
        queue.append((free[bit] + 0.3, kernels, swap(x, bit), use))

    def split(part, stage, pieces_of, left, keep, got):
        base = pieces_of[0][0][0]
        plans = [((begin - base, end - base), route[stage]) for (begin, end), route in pieces_of]
        outs = ran(halve(keep, got, left, plans, after))
        for i, (rows, route) in enumerate(pieces_of):
            rest = [d for d in left if not d & route[stage]]
            if stage + 1 < len(inner):
                use = functools.partial(split, part, stage + 1, [(rows, route)], rest, outs[2 * i])
            else:
                use = functools.partial(close, part, rows, outs[2 * i])
            send(outs[2 * i + 1], route[stage], use)

    def close(part, rows, keep, got):
        last = len(pieces) + 1 == parts * len(routes[0])
        held = pieces + [(rows, part, None)] if last else []
        pieces.append((rows, part, ran(finish(held, keep, got, tokens, width, parts, after))))

    for at, (part, kept) in enumerate(groups):
        begin, end = at * len(near), (at + 1) * len(near)
        x = ran(product(chunks[final[-1]], columns, total, begin, end, after))
        clock += 0.6
        kernels += 1
        if not kept:
            send(x, bits[0], None)
        else:
            when, _, got, _ = queue.pop()
            queue.append((when, kernels - 1, got, functools.partial(split, part, 0, routes[part], near, x)))
    while queue:
        item = min(queue, key=lambda item: item[0])
        queue.remove(item)
        when, at, got, use = item
        if at == kernels:
            ran(tick(after))
            kernels += 1
            clock += 0.1
        clock = max(clock, when) + 0.15
        kernels += 1
        use(got)
    return pieces[-1][2]


def solution(mesh):
    placed = (P("groups", "tensor"), P(), P("tensor", None))
    return jax.shard_map(
        body, mesh=mesh, in_specs=placed, out_specs=P("groups", "tensor"), check_vma=False
    )
```

```python
import functools

import jax
import jax.numpy as jnp
import numpy as np
from jax import lax
from jax.experimental import pallas as pl
from jax.experimental.pallas import tpu as pltpu
from jax.sharding import PartitionSpec as P

LANES = 128
F32 = jnp.float32
BF16 = jnp.bfloat16


def quotient(index, divisor, limit):
    shift = 16
    scale = -(-(1 << shift) // divisor)
    numbers = np.arange(limit, dtype=np.int64)
    assert np.array_equal((numbers * scale) >> shift, numbers // divisor)
    assert limit * scale < 2**31
    return (index * scale) >> shift


def sign_of(common, count):
    parity = common
    for place in range(1, count):
        parity = parity ^ (common >> place)
    return (1 - 2 * (parity & 1)).astype(F32)


def mix_kernel(rows, start, group, activations, small, *refs):
    out = refs[-1]
    local = activations.shape[1]
    block = small.shape[0]
    tokens, cols = out.shape
    tall = group * block
    span = local // block
    low = group.bit_length() - 1
    high = span.bit_length() - 1 - low
    full = small[...]
    head = full.astype(BF16)
    tail = (full - head.astype(F32)).astype(BF16)

    row = lax.broadcasted_iota(jnp.int32, (tall, block), 0)
    unit = lax.broadcasted_iota(jnp.int32, (tall, block), 1)
    spread_rows = (row - quotient(row, block, tall) * block == unit).astype(F32).astype(BF16)
    col = lax.broadcasted_iota(jnp.int32, (block, cols), 1) + start
    unit = lax.broadcasted_iota(jnp.int32, (block, cols), 0)
    spread_cols = (col - quotient(col, block, local) * block == unit).astype(F32).astype(BF16)
    at_row = quotient(lax.broadcasted_iota(jnp.int32, (tall, cols), 0), block, tall)
    at_col = quotient(lax.broadcasted_iota(jnp.int32, (tall, cols), 1) + start, block, local)
    sign = sign_of(at_row & at_col, max(low, 1))

    def tiled(part):
        rolled = jnp.dot(spread_rows, part, preferred_element_type=F32).astype(BF16)
        return (jnp.dot(rolled, spread_cols, preferred_element_type=F32) * sign).astype(BF16)

    head, tail = tiled(head), tiled(tail)
    owner = quotient(lax.broadcasted_iota(jnp.int32, (8, cols), 1) + start, block, local) >> low
    total = jnp.zeros((tokens, cols), F32)
    for piece in range(span // group):
        values = activations[rows[0]:rows[1], piece * tall:(piece + 1) * tall]
        term = jnp.dot(values, head, preferred_element_type=F32)
        term = term + jnp.dot(values, tail, preferred_element_type=F32)
        total = total + term * sign_of(owner & piece, max(high, 1))[0:1]
    out[...] = total


VMEM = pl.BlockSpec(memory_space=pltpu.VMEM)
SMEM = pl.BlockSpec(memory_space=pltpu.SMEM)
UNREAD = pl.BlockSpec(memory_space=pl.ANY)
COST = pl.CostEstimate(flops=10**10, bytes_accessed=10**8, transcendentals=0)


def call(name, kernel, operands, specs, shapes, after, scratch=(), limit=16):
    return pl.pallas_call(
        kernel,
        out_shape=shapes,
        in_specs=list(specs) + [UNREAD] * len(after),
        out_specs=jax.tree.map(lambda _: VMEM, shapes),
        scratch_shapes=list(scratch),
        cost_estimate=COST,
        compiler_params=pltpu.CompilerParams(vmem_limit_bytes=limit * 2**20),
        name=name,
    )(*operands, *after)


def mix(activations, small, rows, cols, after):
    block = small.shape[0]
    group = min(4, activations.shape[1] // block)
    kernel = functools.partial(mix_kernel, rows, cols[0], group)
    shape = jax.ShapeDtypeStruct((rows[1] - rows[0], cols[1] - cols[0]), F32)
    return call("mix", kernel, (activations, small), (VMEM, VMEM), shape, after)


def fold(me, own, got, bit, after, factor=None):
    def kernel(me_ref, own_ref, got_ref, *refs):
        sign = jnp.where((me_ref[0] & bit) != 0, -1.0, 1.0).astype(F32)
        total = got_ref[...] + own_ref[...] * sign
        if factor is not None:
            total = total * factor
        refs[-1][...] = total.astype(refs[-1].dtype)

    shape = jax.ShapeDtypeStruct(own.shape, F32 if factor is None else BF16)
    return call("fold", kernel, (me, own, got), (SMEM, VMEM, VMEM), shape, after)


def load(me, weight, rows, after, limit, distances=(), share=0):
    begin, end = rows

    def kernel(me_ref, weight_ref, *refs):
        out, mark, sems = refs[-3:]
        copies = []
        if not distances:
            copies.append(pltpu.make_async_copy(weight_ref.at[begin:end, :], out, sems.at[0]))
        for i, distance in enumerate(distances):
            column = pl.multiple_of((distance ^ me_ref[0]) * share, LANES)
            copies.append(
                pltpu.make_async_copy(
                    weight_ref.at[begin:end, pl.ds(column, share)], out.at[:, pl.ds(i * share, share)], sems.at[i]
                )
            )
        for copy in copies:
            copy.start()
        mark[...] = jnp.zeros_like(mark)
        for copy in copies:
            copy.wait()

    shapes = [
        jax.ShapeDtypeStruct((end - begin, weight.shape[1]), BF16),
        jax.ShapeDtypeStruct((8, LANES), F32),
    ]
    return call(
        "load",
        kernel,
        (me, weight),
        (SMEM, pl.BlockSpec(memory_space=pltpu.HBM)),
        shapes,
        after,
        [pltpu.SemaphoreType.DMA((max(1, len(distances)),))],
        limit,
    )


def step(chunk, columns, total, shards, after):
    tokens = chunk.shape[0]
    share = columns.shape[1] // shards
    group = max(1, 1024 // share)
    values = [chunk, columns] + ([] if total is None else [total])

    def kernel(*refs):
        out = refs[-1]
        for at in range(0, shards, group):
            sums = jnp.dot(refs[0][...], refs[1][:, at * share:(at + group) * share], preferred_element_type=F32)
            for i in range(group):
                term = sums[:, i * share:(i + 1) * share]
                out[at + i] = term if total is None else refs[2][at + i] + term

    shape = jax.ShapeDtypeStruct((shards, tokens, share), F32)
    return call("step", kernel, values, [VMEM] * len(values), shape, after)


def product(me, chunk, columns, total, begin, distances, parts, after):
    share = total.shape[2]
    width = share // parts
    group = max(1, min(len(distances), 1024 // share))

    def kernel(me_ref, chunk_ref, columns_ref, total_ref, *refs):
        outs = refs[-parts:]
        for at in range(0, len(distances), group):
            start = (begin + at) * share
            sums = jnp.dot(
                chunk_ref[...], columns_ref[:, start:start + group * share], preferred_element_type=F32
            )
            for i in range(group):
                value = total_ref[distances[at + i] ^ me_ref[0]] + sums[:, i * share:(i + 1) * share]
                for part in range(parts):
                    outs[part][at + i] = value[:, part * width:(part + 1) * width]

    shapes = [jax.ShapeDtypeStruct((len(distances), chunk.shape[0], width), F32)] * parts
    return call("product", kernel, (me, chunk, columns, total), [SMEM] + [VMEM] * 3, shapes, after)


def halve(own, got, distances, plans, after):
    shapes = []
    for rows, _ in plans:
        shapes += [jax.ShapeDtypeStruct((len(distances) // 2, rows[1] - rows[0], own.shape[2]), F32)] * 2

    def kernel(own_ref, got_ref, *refs):
        outs = refs[-len(shapes):]
        for at, ((begin, end), bit) in enumerate(plans):
            for place, d in enumerate(d for d in distances if not d & bit):
                for out, source in ((outs[2 * at], d), (outs[2 * at + 1], d | bit)):
                    i = distances.index(source)
                    out[place] = own_ref[i, begin:end, :] + got_ref[i, begin:end, :]

    return call("halve", kernel, (own, got), (VMEM, VMEM), shapes, after)


def tick(after):
    def kernel(*refs):
        refs[-1][...] = jnp.zeros_like(refs[-1])

    return call("tick", kernel, (), (), jax.ShapeDtypeStruct((8, LANES), F32), after)


def finish(pieces, own, got, tokens, width, parts, after):
    held = [x for _, _, x in pieces[:-1]] if len(pieces) > 1 else []

    def kernel(own_ref, got_ref, *refs):
        out = refs[-1]
        value = (own_ref[0] + got_ref[0]).astype(BF16)
        if not pieces:
            out[...] = value
            return
        for ((begin, end), part, _), ref in zip(pieces, [*refs[:len(held)], None]):
            out[begin:end, part * width:(part + 1) * width] = value if ref is None else ref[...]

    shape = (tokens, width * parts) if pieces else own.shape[1:]
    operands = (own, got, *held)
    return call("finish", kernel, operands, [VMEM] * len(operands), jax.ShapeDtypeStruct(shape, BF16), after)


def body(activations, rotation_small, down_weight):
    shards = lax.axis_size("tensor")
    me = lax.axis_index("tensor").astype(jnp.int32).reshape(1)
    tokens, local = activations.shape
    block = rotation_small.shape[0]
    share = down_weight.shape[1] // shards
    factor = (local // block * shards) ** (-0.5)
    bits = [1 << place for place in range(shards.bit_length() - 1)]
    assert len(bits) >= 3 and shards == 1 << len(bits)
    after = []

    def swap(x, bit):
        return lax.ppermute(x, "tensor", [(d, d ^ bit) for d in range(shards)])

    def ran(outs, link=-1):
        after[:] = [jax.tree.leaves(outs)[link]]
        return outs

    parts = 2 if share % (2 * LANES) == 0 else 1
    width = share // parts
    near = [d for d in range(shards) if not d & bits[0]]
    distances = [d | bits[0] for d in near] + near

    tiles = -(-local // LANES)
    count = max(1, min(len(bits), tiles))
    edges = [min(local, (tiles * c // count) * LANES) for c in range(count)] + [local]
    spans = list(zip(edges[:-1], edges[1:]))
    chunks = []
    for span in spans:
        chunks.append(ran(mix(activations, rotation_small, (0, tokens), span, after)))
    cycle = bits[-1:] + bits[1:-1] + bits[:1]
    events = []
    for phase in range(len(bits)):
        for c in range(count):
            events.append((phase, cycle[(phase - c) % len(bits)], c))
    events.sort()
    final = [c for phase, _, c in events if phase == len(bits) - 1]
    total = None
    loaded = []
    room = 40 * 2**20
    places = [0] * (count - count // 2) + [len(events) - count] * (count // 2)
    for number, (phase, bit, c) in enumerate(events):
        got = swap(chunks[c], bit)
        last = phase == len(bits) - 1
        chunks[c] = ran(fold(me, chunks[c], got, bit, after, factor if last else None))
        if last and c != final[-1]:
            total = ran(step(chunks[c], loaded[final.index(c)], total, shards, after))
        while len(loaded) < count and number == places[len(loaded)]:
            rows = spans[final[len(loaded)]]
            wanted = (distances, share) if len(loaded) == count - 1 else ()
            loaded.append(ran(load(me, down_weight, rows, after, room // 2**20, *wanted))[0])
            room -= loaded[-1].size * 2

    inner = bits[1:]
    late = inner[-1:] + inner[:-1]
    swapped = [inner[1], inner[0]] + inner[2:]
    half = tokens // 2
    routes = [
        [((0, half), inner), ((half, tokens), late)],
        [((0, half), swapped), ((half, tokens), inner)],
    ][:parts]
    free = dict.fromkeys(bits, 0.0)
    clock = 0.0
    kernels = 0
    pieces = []
    queue = []

    def send(x, bit, use):
        nonlocal clock
        clock += 0.7
        micros = x.size * 4e-6 * (2 if bit == bits[0] else 40 if bit == bits[-1] else 20)
        free[bit] = max(clock + 1.0, free[bit]) + micros
        queue.append((free[bit] + 0.3, kernels, swap(x, bit), use))

    def split(part, stage, pieces_of, left, keep, got):
        base = pieces_of[0][0][0]
        plans = [((begin - base, end - base), route[stage]) for (begin, end), route in pieces_of]
        outs = ran(halve(keep, got, left, plans, after))
        for i, (rows, route) in enumerate(pieces_of):
            rest = [d for d in left if not d & route[stage]]
            if stage + 1 < len(inner):
                use = functools.partial(split, part, stage + 1, [(rows, route)], rest, outs[2 * i])
            else:
                use = functools.partial(close, part, rows, outs[2 * i])
            send(outs[2 * i + 1], route[stage], use)

    def close(part, rows, keep, got):
        last = len(pieces) + 1 == parts * len(routes[0])
        held = pieces + [(rows, part, None)] if last else []
        pieces.append((rows, part, ran(finish(held, keep, got, tokens, width, parts, after))))

    last_chunk = chunks[final[-1]]
    sends = ran(product(me, last_chunk, loaded[-1], total, 0, distances[:len(near)], parts, after))
    clock += 0.9
    kernels += 1
    for x in sends:
        send(x, bits[0], None)
    keeps = ran(product(me, last_chunk, loaded[-1], total, len(near), near, parts, after))
    clock += 0.9
    kernels += 1
    queue[:] = [
        (when, at, got, functools.partial(split, part, 0, routes[part], near, keeps[part]))
        for part, (when, at, got, _) in enumerate(queue)
    ]
    while queue:
        item = min(queue, key=lambda item: item[0])
        queue.remove(item)
        when, at, got, use = item
        if at == kernels:
            ran(tick(after))
            kernels += 1
            clock += 0.1
        clock = max(clock, when) + 0.15
        kernels += 1
        use(got)
    return pieces[-1][2]


def solution(mesh):
    placed = (P("groups", "tensor"), P(), P("tensor", None))
    return jax.shard_map(
        body, mesh=mesh, in_specs=placed, out_specs=P("groups", "tensor"), check_vma=False
    )
```

```python
import functools

import jax
import jax.numpy as jnp
import numpy as np
from jax import lax
from jax.experimental import pallas as pl
from jax.experimental.pallas import tpu as pltpu
from jax.sharding import PartitionSpec as P

LANES = 128
F32 = jnp.float32
BF16 = jnp.bfloat16


TILES = (3, 3, 3, 4)
ORDERS = ((3, 1, 2, 0), (0, 3, 1, 2), (2, 0, 3, 1), (1, 2, 0, 3))
FIRST = (0, 2, 3, 1)
PATIENCE = 1.8
RULE = 1


def quotient(index, divisor, limit):
    shift = 16
    scale = -(-(1 << shift) // divisor)
    numbers = np.arange(limit, dtype=np.int64)
    assert np.array_equal((numbers * scale) >> shift, numbers // divisor)
    assert limit * scale < 2**31
    return (index * scale) >> shift


def sign_of(common, count):
    parity = common
    for place in range(1, count):
        parity = parity ^ (common >> place)
    return (1 - 2 * (parity & 1)).astype(F32)


def mix_kernel(rows, start, group, activations, small, *refs):
    out = refs[-1]
    local = activations.shape[1]
    block = small.shape[0]
    tokens, cols = out.shape
    tall = group * block
    span = local // block
    low = group.bit_length() - 1
    high = span.bit_length() - 1 - low
    full = small[...]
    head = full.astype(BF16)
    tail = (full - head.astype(F32)).astype(BF16)

    row = lax.broadcasted_iota(jnp.int32, (tall, block), 0)
    unit = lax.broadcasted_iota(jnp.int32, (tall, block), 1)
    spread_rows = (row - quotient(row, block, tall) * block == unit).astype(F32).astype(BF16)
    col = lax.broadcasted_iota(jnp.int32, (block, cols), 1) + start
    unit = lax.broadcasted_iota(jnp.int32, (block, cols), 0)
    spread_cols = (col - quotient(col, block, local) * block == unit).astype(F32).astype(BF16)
    at_row = quotient(lax.broadcasted_iota(jnp.int32, (tall, cols), 0), block, tall)
    at_col = quotient(lax.broadcasted_iota(jnp.int32, (tall, cols), 1) + start, block, local)
    sign = sign_of(at_row & at_col, max(low, 1))

    def tiled(part):
        rolled = jnp.dot(spread_rows, part, preferred_element_type=F32).astype(BF16)
        return (jnp.dot(rolled, spread_cols, preferred_element_type=F32) * sign).astype(BF16)

    head, tail = tiled(head), tiled(tail)
    owner = quotient(lax.broadcasted_iota(jnp.int32, (8, cols), 1) + start, block, local) >> low
    total = jnp.zeros((tokens, cols), F32)
    for piece in range(span // group):
        values = activations[rows[0]:rows[1], piece * tall:(piece + 1) * tall]
        term = jnp.dot(values, head, preferred_element_type=F32)
        term = term + jnp.dot(values, tail, preferred_element_type=F32)
        total = total + term * sign_of(owner & piece, max(high, 1))[0:1]
    out[...] = total


VMEM = pl.BlockSpec(memory_space=pltpu.VMEM)
SMEM = pl.BlockSpec(memory_space=pltpu.SMEM)
UNREAD = pl.BlockSpec(memory_space=pl.ANY)
COST = pl.CostEstimate(flops=10**10, bytes_accessed=10**8, transcendentals=0)


def call(name, kernel, operands, specs, shapes, after, scratch=(), limit=16):
    return pl.pallas_call(
        kernel,
        out_shape=shapes,
        in_specs=list(specs) + [UNREAD] * len(after),
        out_specs=jax.tree.map(lambda _: VMEM, shapes),
        scratch_shapes=list(scratch),
        cost_estimate=COST,
        compiler_params=pltpu.CompilerParams(vmem_limit_bytes=limit * 2**20),
        name=name,
    )(*operands, *after)


def mix(activations, small, rows, cols, after):
    block = small.shape[0]
    group = min(4, activations.shape[1] // block)
    kernel = functools.partial(mix_kernel, rows, cols[0], group)
    shape = jax.ShapeDtypeStruct((rows[1] - rows[0], cols[1] - cols[0]), F32)
    return call("mix", kernel, (activations, small), (VMEM, VMEM), shape, after)


def fold(me, own, got, bit, after, factor=None):
    def kernel(me_ref, own_ref, got_ref, *refs):
        sign = jnp.where((me_ref[0] & bit) != 0, -1.0, 1.0).astype(F32)
        total = got_ref[...] + own_ref[...] * sign
        if factor is not None:
            total = total * factor
        refs[-1][...] = total.astype(refs[-1].dtype)

    shape = jax.ShapeDtypeStruct(own.shape, F32 if factor is None else BF16)
    return call("fold", kernel, (me, own, got), (SMEM, VMEM, VMEM), shape, after)


def load(me, weight, rows, after, limit, distances=(), share=0):
    begin, end = rows

    def kernel(me_ref, weight_ref, *refs):
        out, mark, sems = refs[-3:]
        copies = []
        if not distances:
            copies.append(pltpu.make_async_copy(weight_ref.at[begin:end, :], out, sems.at[0]))
        for i, distance in enumerate(distances):
            column = pl.multiple_of((distance ^ me_ref[0]) * share, LANES)
            copies.append(
                pltpu.make_async_copy(
                    weight_ref.at[begin:end, pl.ds(column, share)], out.at[:, pl.ds(i * share, share)], sems.at[i]
                )
            )
        for copy in copies:
            copy.start()
        mark[...] = jnp.zeros_like(mark)
        for copy in copies:
            copy.wait()

    shapes = [
        jax.ShapeDtypeStruct((end - begin, weight.shape[1]), BF16),
        jax.ShapeDtypeStruct((8, LANES), F32),
    ]
    return call(
        "load",
        kernel,
        (me, weight),
        (SMEM, pl.BlockSpec(memory_space=pltpu.HBM)),
        shapes,
        after,
        [pltpu.SemaphoreType.DMA((max(1, len(distances)),))],
        limit,
    )


def step(chunk, columns, total, shards, after):
    tokens = chunk.shape[0]
    share = columns.shape[1] // shards
    group = max(1, 1024 // share)
    values = [chunk, columns] + ([] if total is None else [total])

    def kernel(*refs):
        out = refs[-1]
        for at in range(0, shards, group):
            sums = jnp.dot(refs[0][...], refs[1][:, at * share:(at + group) * share], preferred_element_type=F32)
            for i in range(group):
                term = sums[:, i * share:(i + 1) * share]
                out[at + i] = term if total is None else refs[2][at + i] + term

    shape = jax.ShapeDtypeStruct((shards, tokens, share), F32)
    return call("step", kernel, values, [VMEM] * len(values), shape, after)


def product(me, chunk, columns, total, begin, distances, parts, after):
    share = total.shape[2]
    width = share // parts
    group = max(1, min(len(distances), 1024 // share))

    def kernel(me_ref, chunk_ref, columns_ref, total_ref, *refs):
        outs = refs[-parts:]
        for at in range(0, len(distances), group):
            start = (begin + at) * share
            sums = jnp.dot(
                chunk_ref[...], columns_ref[:, start:start + group * share], preferred_element_type=F32
            )
            for i in range(group):
                value = total_ref[distances[at + i] ^ me_ref[0]] + sums[:, i * share:(i + 1) * share]
                for part in range(parts):
                    outs[part][at + i] = value[:, part * width:(part + 1) * width]

    shapes = [jax.ShapeDtypeStruct((len(distances), chunk.shape[0], width), F32)] * parts
    return call("product", kernel, (me, chunk, columns, total), [SMEM] + [VMEM] * 3, shapes, after)


def halve(own, got, distances, plans, after):
    shapes = []
    for rows, _ in plans:
        shapes += [jax.ShapeDtypeStruct((len(distances) // 2, rows[1] - rows[0], own.shape[2]), F32)] * 2

    def kernel(own_ref, got_ref, *refs):
        outs = refs[-len(shapes):]
        for at, ((begin, end), bit) in enumerate(plans):
            for place, d in enumerate(d for d in distances if not d & bit):
                for out, source in ((outs[2 * at], d), (outs[2 * at + 1], d | bit)):
                    i = distances.index(source)
                    out[place] = own_ref[i, begin:end, :] + got_ref[i, begin:end, :]

    return call("halve", kernel, (own, got), (VMEM, VMEM), shapes, after)


def tick(after):
    def kernel(*refs):
        refs[-1][...] = jnp.zeros_like(refs[-1])

    return call("tick", kernel, (), (), jax.ShapeDtypeStruct((8, LANES), F32), after)


def finish(pieces, own, got, tokens, width, parts, after):
    held = [x for _, _, x in pieces[:-1]] if len(pieces) > 1 else []

    def kernel(own_ref, got_ref, *refs):
        out = refs[-1]
        value = (own_ref[0] + got_ref[0]).astype(BF16)
        if not pieces:
            out[...] = value
            return
        for ((begin, end), part, _), ref in zip(pieces, [*refs[:len(held)], None]):
            out[begin:end, part * width:(part + 1) * width] = value if ref is None else ref[...]

    shape = (tokens, width * parts) if pieces else own.shape[1:]
    operands = (own, got, *held)
    return call("finish", kernel, operands, [VMEM] * len(operands), jax.ShapeDtypeStruct(shape, BF16), after)


class Links:
    def __init__(self, bits):
        self.bits = bits
        self.taken = {bit: [] for bit in bits}

    def needs(self, bit, size):
        if bit == self.bits[0]:
            return {bit: size * 8e-6}
        if bit != self.bits[-1]:
            return {bit: size * 80e-6}
        return {bit: size * 160e-6, self.bits[-2]: size * 80e-6}

    def free(self, bit, now):
        share, until = 1.0, float("inf")
        for begin, end, used in self.taken[bit]:
            if begin <= now < end:
                share -= used
            if begin <= now < end or begin > now:
                until = min(until, end if begin <= now else begin)
        return max(share, 0.0), until

    def send(self, bit, size, now):
        needs = self.needs(bit, size)
        now += 1.0
        left = 1.0
        spans = []
        while left > 1e-6:
            shares = [(self.free(link, now), need) for link, need in needs.items()]
            rate = min(share / need for (share, _), need in shares)
            until = min(until for (_, until), _ in shares)
            if rate > 1e-6:
                until = min(until, now + left / rate)
                spans.append((now, until, rate))
                left -= rate * (until - now)
            now = until
        for begin, end, rate in spans:
            for link, need in needs.items():
                self.taken[link].append((begin, end, rate * need))
        return now + 0.3


def plan(bits, tokens, sizes, orders, first, loads):
    links = Links(bits)
    clock = 1.8
    flights = []
    done = []
    wait = list(first)
    loads = list(loads)
    missing = list(loads)

    def start(c, stage):
        nonlocal clock
        clock += 0.9
        flights.append((links.send(orders[c][stage], tokens * sizes[c], clock), len(done), c, stage))

    while wait or flights:
        flights.sort(key=lambda flight: (flight[3] if RULE else 0, flight))
        arrival = flights[0][0] if flights else float("inf")
        if wait and arrival > clock:
            done.append(("mix", wait[0]))
            clock += 1.2
            start(wait.pop(0), 0)
        elif loads and arrival - clock > PATIENCE:
            done.append(("load", loads.pop(0)))
            clock += 2.8
        else:
            _, began, c, stage = flights.pop(0)
            if began == len(done):
                done.append(("tick", c))
            clock = max(clock, arrival) + 0.1
            done.append(("fold", c))
            if stage + 1 < len(bits):
                start(c, stage + 1)
            elif flights or wait:
                if c in loads:
                    loads.remove(c)
                    done.append(("load", c))
                    clock += 2.8
                done.append(("step", c))
                clock += 1.3
            else:
                done += [("load", c) for c in loads]
                done.append(("last", c))
    return done


def body(activations, rotation_small, down_weight):
    shards = lax.axis_size("tensor")
    me = lax.axis_index("tensor").astype(jnp.int32).reshape(1)
    tokens, local = activations.shape
    block = rotation_small.shape[0]
    share = down_weight.shape[1] // shards
    factor = (local // block * shards) ** (-0.5)
    bits = [1 << place for place in range(shards.bit_length() - 1)]
    assert len(bits) >= 3 and shards == 1 << len(bits)
    after = []

    def swap(x, bit):
        return lax.ppermute(x, "tensor", [(d, d ^ bit) for d in range(shards)])

    def ran(outs, link=-1):
        after[:] = [jax.tree.leaves(outs)[link]]
        return outs

    parts = 2 if share % (2 * LANES) == 0 else 1
    width = share // parts
    near = [d for d in range(shards) if not d & bits[0]]
    distances = [d | bits[0] for d in near] + near

    tiles = -(-local // LANES)
    ends = [round(tiles * sum(TILES[:c]) / sum(TILES)) for c in range(len(TILES) + 1)]
    edges = [min(local, end * LANES) for end in ends]
    assert all(begin < end for begin, end in zip(edges[:-1], edges[1:]))
    spans = list(zip(edges[:-1], edges[1:]))
    sizes = [end - begin for begin, end in spans]
    roles = [bits[:1], bits[1:-2], bits[-2:-1], bits[-1:]]
    orders = [sum((roles[role] for role in order), []) for order in ORDERS]
    first = FIRST
    loads = [c for what, c in plan(bits, tokens, sizes, orders, first, ()) if what in ("step", "last")]
    total = None
    loaded = {}
    chunks = {}
    stages = [0] * len(spans)
    room = 40 * 2**20
    for what, c in plan(bits, tokens, sizes, orders, first, loads):
        if what == "mix":
            chunks[c] = ran(mix(activations, rotation_small, (0, tokens), spans[c], after))
        elif what == "load":
            wanted = (distances, share) if c == loads[-1] else ()
            loaded[c] = ran(load(me, down_weight, spans[c], after, room // 2**20, *wanted))[0]
            room -= loaded[c].size * 2
        elif what == "fold":
            bit = orders[c][stages[c]]
            stages[c] += 1
            got = swap(chunks[c], bit)
            end = stages[c] == len(bits)
            chunks[c] = ran(fold(me, chunks[c], got, bit, after, factor if end else None))
        elif what == "tick":
            ran(tick(after))
        elif what == "step":
            total = ran(step(chunks[c], loaded[c], total, shards, after))

    inner = bits[1:]
    late = inner[-1:] + inner[:-1]
    swapped = [inner[1], inner[0]] + inner[2:]
    half = tokens // 2
    routes = [
        [((0, half), inner), ((half, tokens), late)],
        [((0, half), swapped), ((half, tokens), inner)],
    ][:parts]
    links = Links(bits)
    clock = 0.0
    kernels = 0
    pieces = []
    queue = []

    def send(x, bit, use):
        nonlocal clock
        clock += 0.9
        queue.append((links.send(bit, x.size, clock), kernels, swap(x, bit), use))

    def split(part, stage, pieces_of, left, keep, got):
        base = pieces_of[0][0][0]
        plans = [((begin - base, end - base), route[stage]) for (begin, end), route in pieces_of]
        outs = ran(halve(keep, got, left, plans, after))
        for i, (rows, route) in enumerate(pieces_of):
            rest = [d for d in left if not d & route[stage]]
            if stage + 1 < len(inner):
                use = functools.partial(split, part, stage + 1, [(rows, route)], rest, outs[2 * i])
            else:
                use = functools.partial(close, part, rows, outs[2 * i])
            send(outs[2 * i + 1], route[stage], use)

    def close(part, rows, keep, got):
        last = len(pieces) + 1 == parts * len(routes[0])
        held = pieces + [(rows, part, None)] if last else []
        pieces.append((rows, part, ran(finish(held, keep, got, tokens, width, parts, after))))

    last_chunk, last_columns = chunks[loads[-1]], loaded[loads[-1]]
    sends = ran(product(me, last_chunk, last_columns, total, 0, distances[:len(near)], parts, after))
    clock += 0.9
    kernels += 1
    for x in sends:
        send(x, bits[0], None)
    keeps = ran(product(me, last_chunk, last_columns, total, len(near), near, parts, after))
    clock += 0.9
    kernels += 1
    queue[:] = [
        (when, at, got, functools.partial(split, part, 0, routes[part], near, keeps[part]))
        for part, (when, at, got, _) in enumerate(queue)
    ]
    while queue:
        item = min(queue, key=lambda item: item[0])
        queue.remove(item)
        when, at, got, use = item
        if at == kernels:
            ran(tick(after))
            kernels += 1
            clock += 0.1
        clock = max(clock, when) + 0.15
        kernels += 1
        use(got)
    return pieces[-1][2]


def solution(mesh):
    placed = (P("groups", "tensor"), P(), P("tensor", None))
    return jax.shard_map(
        body, mesh=mesh, in_specs=placed, out_specs=P("groups", "tensor"), check_vma=False
    )
```

```python
import functools

import jax
import jax.numpy as jnp
import numpy as np
from jax import lax
from jax.experimental import pallas as pl
from jax.experimental.pallas import tpu as pltpu
from jax.sharding import PartitionSpec as P

LANES = 128
F32 = jnp.float32
BF16 = jnp.bfloat16


TILES = (3, 3, 3, 4)
ORDERS = ((3, 0, 2, 1), ("in", "mid", "out", 0, 1), (1, 0, "in", "mid", "out"), (1, 2, 0, 3))
FIRST = (1, 2, 0, 3)
PATIENCE = 1.8


def quotient(index, divisor, limit):
    shift = 16
    scale = -(-(1 << shift) // divisor)
    numbers = np.arange(limit, dtype=np.int64)
    assert np.array_equal((numbers * scale) >> shift, numbers // divisor)
    assert limit * scale < 2**31
    return (index * scale) >> shift


def sign_of(common, count):
    parity = common
    for place in range(1, count):
        parity = parity ^ (common >> place)
    return (1 - 2 * (parity & 1)).astype(F32)


def mix_kernel(rows, start, group, activations, small, *refs):
    out = refs[-1]
    local = activations.shape[1]
    block = small.shape[0]
    tokens, cols = out.shape
    tall = group * block
    span = local // block
    low = group.bit_length() - 1
    high = span.bit_length() - 1 - low
    full = small[...]
    head = full.astype(BF16)
    tail = (full - head.astype(F32)).astype(BF16)

    row = lax.broadcasted_iota(jnp.int32, (tall, block), 0)
    unit = lax.broadcasted_iota(jnp.int32, (tall, block), 1)
    spread_rows = (row - quotient(row, block, tall) * block == unit).astype(F32).astype(BF16)
    col = lax.broadcasted_iota(jnp.int32, (block, cols), 1) + start
    unit = lax.broadcasted_iota(jnp.int32, (block, cols), 0)
    spread_cols = (col - quotient(col, block, local) * block == unit).astype(F32).astype(BF16)
    at_row = quotient(lax.broadcasted_iota(jnp.int32, (tall, cols), 0), block, tall)
    at_col = quotient(lax.broadcasted_iota(jnp.int32, (tall, cols), 1) + start, block, local)
    sign = sign_of(at_row & at_col, max(low, 1))

    def tiled(part):
        rolled = jnp.dot(spread_rows, part, preferred_element_type=F32).astype(BF16)
        return (jnp.dot(rolled, spread_cols, preferred_element_type=F32) * sign).astype(BF16)

    head, tail = tiled(head), tiled(tail)
    owner = quotient(lax.broadcasted_iota(jnp.int32, (8, cols), 1) + start, block, local) >> low
    total = jnp.zeros((tokens, cols), F32)
    for piece in range(span // group):
        values = activations[rows[0]:rows[1], piece * tall:(piece + 1) * tall]
        term = jnp.dot(values, head, preferred_element_type=F32)
        term = term + jnp.dot(values, tail, preferred_element_type=F32)
        total = total + term * sign_of(owner & piece, max(high, 1))[0:1]
    out[...] = total


VMEM = pl.BlockSpec(memory_space=pltpu.VMEM)
SMEM = pl.BlockSpec(memory_space=pltpu.SMEM)
UNREAD = pl.BlockSpec(memory_space=pl.ANY)
COST = pl.CostEstimate(flops=10**10, bytes_accessed=10**8, transcendentals=0)


def call(name, kernel, operands, specs, shapes, after, scratch=(), limit=16):
    return pl.pallas_call(
        kernel,
        out_shape=shapes,
        in_specs=list(specs) + [UNREAD] * len(after),
        out_specs=jax.tree.map(lambda _: VMEM, shapes),
        scratch_shapes=list(scratch),
        cost_estimate=COST,
        compiler_params=pltpu.CompilerParams(vmem_limit_bytes=limit * 2**20),
        name=name,
    )(*operands, *after)


def mix(activations, small, rows, cols, after):
    block = small.shape[0]
    group = min(4, activations.shape[1] // block)
    kernel = functools.partial(mix_kernel, rows, cols[0], group)
    shape = jax.ShapeDtypeStruct((rows[1] - rows[0], cols[1] - cols[0]), F32)
    return call("mix", kernel, (activations, small), (VMEM, VMEM), shape, after)


def fold(me, own, got, bit, after, factor=None):
    def kernel(me_ref, own_ref, got_ref, *refs):
        sign = jnp.where((me_ref[0] & bit) != 0, -1.0, 1.0).astype(F32)
        total = got_ref[...] + own_ref[...] * sign
        if factor is not None:
            total = total * factor
        refs[-1][...] = total.astype(refs[-1].dtype)

    shape = jax.ShapeDtypeStruct(own.shape, F32 if factor is None else BF16)
    return call("fold", kernel, (me, own, got), (SMEM, VMEM, VMEM), shape, after)


def pair(me, own, got, quarter, after):
    def kernel(me_ref, own_ref, got_ref, *refs):
        sign = jnp.where(me_ref[0] // quarter == 2, -1.0, 1.0).astype(F32)
        refs[-1][0] = got_ref[...] + own_ref[...]
        refs[-1][1] = (got_ref[...] - own_ref[...]) * sign

    shape = jax.ShapeDtypeStruct((2, *own.shape), F32)
    return call("pair", kernel, (me, own, got), (SMEM, VMEM, VMEM), shape, after)


def meet(me, own, got, quarter, after):
    def kernel(me_ref, own_ref, got_ref, *refs):
        keep, give = refs[-2:]
        third = me_ref[0] // quarter == 2

        @pl.when(third)
        def _():
            keep[...] = got_ref[0] - own_ref[0]
            give[...] = got_ref[1] - own_ref[1]

        @pl.when(jnp.logical_not(third))
        def _():
            keep[...] = got_ref[1] + own_ref[1]
            give[...] = got_ref[0] + own_ref[0]

    shapes = [jax.ShapeDtypeStruct(own.shape[1:], F32)] * 2
    return call("meet", kernel, (me, own, got), (SMEM, VMEM, VMEM), shapes, after)


def settle(me, own, got, quarter, after, factor=None):
    def kernel(me_ref, own_ref, got_ref, *refs):
        place = me_ref[0] // quarter
        total = jnp.where(jnp.logical_or(place == 0, place == 3), got_ref[...], own_ref[...])
        if factor is not None:
            total = total * factor
        refs[-1][...] = total.astype(refs[-1].dtype)

    shape = jax.ShapeDtypeStruct(own.shape, F32 if factor is None else BF16)
    return call("settle", kernel, (me, own, got), (SMEM, VMEM, VMEM), shape, after)


def load(me, weight, rows, after, limit, distances=(), share=0):
    begin, end = rows

    def kernel(me_ref, weight_ref, *refs):
        out, mark, sems = refs[-3:]
        copies = []
        if not distances:
            copies.append(pltpu.make_async_copy(weight_ref.at[begin:end, :], out, sems.at[0]))
        for i, distance in enumerate(distances):
            column = pl.multiple_of((distance ^ me_ref[0]) * share, LANES)
            copies.append(
                pltpu.make_async_copy(
                    weight_ref.at[begin:end, pl.ds(column, share)], out.at[:, pl.ds(i * share, share)], sems.at[i]
                )
            )
        for copy in copies:
            copy.start()
        mark[...] = jnp.zeros_like(mark)
        for copy in copies:
            copy.wait()

    shapes = [
        jax.ShapeDtypeStruct((end - begin, weight.shape[1]), BF16),
        jax.ShapeDtypeStruct((8, LANES), F32),
    ]
    return call(
        "load",
        kernel,
        (me, weight),
        (SMEM, pl.BlockSpec(memory_space=pltpu.HBM)),
        shapes,
        after,
        [pltpu.SemaphoreType.DMA((max(1, len(distances)),))],
        limit,
    )


def step(chunk, columns, total, shards, after):
    tokens = chunk.shape[0]
    share = columns.shape[1] // shards
    group = max(1, 1024 // share)
    values = [chunk, columns] + ([] if total is None else [total])

    def kernel(*refs):
        out = refs[-1]
        for at in range(0, shards, group):
            sums = jnp.dot(refs[0][...], refs[1][:, at * share:(at + group) * share], preferred_element_type=F32)
            for i in range(group):
                term = sums[:, i * share:(i + 1) * share]
                out[at + i] = term if total is None else refs[2][at + i] + term

    shape = jax.ShapeDtypeStruct((shards, tokens, share), F32)
    return call("step", kernel, values, [VMEM] * len(values), shape, after)


def product(me, chunk, columns, total, begin, distances, parts, after):
    share = total.shape[2]
    width = share // parts
    group = max(1, min(len(distances), 1024 // share))

    def kernel(me_ref, chunk_ref, columns_ref, total_ref, *refs):
        outs = refs[-parts:]
        for at in range(0, len(distances), group):
            start = (begin + at) * share
            sums = jnp.dot(
                chunk_ref[...], columns_ref[:, start:start + group * share], preferred_element_type=F32
            )
            for i in range(group):
                value = total_ref[distances[at + i] ^ me_ref[0]] + sums[:, i * share:(i + 1) * share]
                for part in range(parts):
                    outs[part][at + i] = value[:, part * width:(part + 1) * width]

    shapes = [jax.ShapeDtypeStruct((len(distances), chunk.shape[0], width), F32)] * parts
    return call("product", kernel, (me, chunk, columns, total), [SMEM] + [VMEM] * 3, shapes, after)


def halve(own, got, distances, plans, after):
    shapes = []
    for rows, _ in plans:
        shapes += [jax.ShapeDtypeStruct((len(distances) // 2, rows[1] - rows[0], own.shape[2]), F32)] * 2

    def kernel(own_ref, got_ref, *refs):
        outs = refs[-len(shapes):]
        for at, ((begin, end), bit) in enumerate(plans):
            for place, d in enumerate(d for d in distances if not d & bit):
                for out, source in ((outs[2 * at], d), (outs[2 * at + 1], d | bit)):
                    i = distances.index(source)
                    out[place] = own_ref[i, begin:end, :] + got_ref[i, begin:end, :]

    return call("halve", kernel, (own, got), (VMEM, VMEM), shapes, after)


def tick(after):
    def kernel(*refs):
        refs[-1][...] = jnp.zeros_like(refs[-1])

    return call("tick", kernel, (), (), jax.ShapeDtypeStruct((8, LANES), F32), after)


def finish(pieces, own, got, tokens, width, parts, after):
    held = [x for _, _, x in pieces[:-1]] if len(pieces) > 1 else []

    def kernel(own_ref, got_ref, *refs):
        out = refs[-1]
        value = (own_ref[0] + got_ref[0]).astype(BF16)
        if not pieces:
            out[...] = value
            return
        for ((begin, end), part, _), ref in zip(pieces, [*refs[:len(held)], None]):
            out[begin:end, part * width:(part + 1) * width] = value if ref is None else ref[...]

    shape = (tokens, width * parts) if pieces else own.shape[1:]
    operands = (own, got, *held)
    return call("finish", kernel, operands, [VMEM] * len(operands), jax.ShapeDtypeStruct(shape, BF16), after)


class Links:
    def __init__(self, bits):
        self.bits = bits
        self.taken = {link: [] for link in bits[:-2] + ["in", "mid", "out"]}

    def needs(self, stage, size):
        if stage == self.bits[0]:
            return {stage: size * 8e-6}
        if stage == self.bits[-1]:
            return {"mid": size * 160e-6, "in": size * 112e-6, "out": size * 112e-6}
        if stage == self.bits[-2]:
            return {"in": size * 80e-6, "out": size * 80e-6}
        return {stage: size * 80e-6}

    def free(self, bit, now):
        share, until = 1.0, float("inf")
        for begin, end, used in self.taken[bit]:
            if begin <= now < end:
                share -= used
            if begin <= now < end or begin > now:
                until = min(until, end if begin <= now else begin)
        return max(share, 0.0), until

    def send(self, bit, size, now):
        needs = self.needs(bit, size)
        now += 1.0
        left = 1.0
        spans = []
        while left > 1e-6:
            shares = [(self.free(link, now), need) for link, need in needs.items()]
            rate = min(share / need for (share, _), need in shares)
            until = min(until for (_, until), _ in shares)
            if rate > 1e-6:
                until = min(until, now + left / rate)
                spans.append((now, until, rate))
                left -= rate * (until - now)
            now = until
        for begin, end, rate in spans:
            for link, need in needs.items():
                self.taken[link].append((begin, end, rate * need))
        return now + 0.3


def plan(bits, tokens, sizes, orders, first, loads):
    links = Links(bits)
    clock = 1.8
    flights = []
    done = []
    wait = list(first)
    loads = list(loads)
    missing = list(loads)

    def start(c, stage):
        nonlocal clock
        clock += 0.9
        what = orders[c][stage]
        size = tokens * sizes[c] * (2 if what == "mid" else 1)
        flights.append((links.send(what, size, clock), len(done), c, stage))

    while wait or flights:
        flights.sort()
        arrival = flights[0][0] if flights else float("inf")
        if wait and arrival > clock:
            done.append(("mix", wait[0]))
            clock += 1.2
            start(wait.pop(0), 0)
        elif loads and arrival - clock > PATIENCE:
            done.append(("load", loads.pop(0)))
            clock += 2.8
        else:
            _, began, c, stage = flights.pop(0)
            if began == len(done):
                done.append(("tick", c))
            clock = max(clock, arrival) + 0.1
            done.append(("fold", c))
            if stage + 1 < len(orders[c]):
                start(c, stage + 1)
            elif flights or wait:
                if c in loads:
                    loads.remove(c)
                    done.append(("load", c))
                    clock += 2.8
                done.append(("step", c))
                clock += 1.3
            else:
                done += [("load", c) for c in loads]
                done.append(("last", c))
    return done


def body(activations, rotation_small, down_weight):
    shards = lax.axis_size("tensor")
    me = lax.axis_index("tensor").astype(jnp.int32).reshape(1)
    tokens, local = activations.shape
    block = rotation_small.shape[0]
    share = down_weight.shape[1] // shards
    factor = (local // block * shards) ** (-0.5)
    bits = [1 << place for place in range(shards.bit_length() - 1)]
    assert len(bits) >= 3 and shards == 1 << len(bits)
    after = []

    def swap(x, bit):
        return lax.ppermute(x, "tensor", [(d, d ^ bit) for d in range(shards)])

    def ran(outs, link=-1):
        after[:] = [jax.tree.leaves(outs)[link]]
        return outs

    parts = 2 if share % (2 * LANES) == 0 else 1
    width = share // parts
    near = [d for d in range(shards) if not d & bits[0]]
    distances = [d | bits[0] for d in near] + near

    tiles = -(-local // LANES)
    ends = [round(tiles * sum(TILES[:c]) / sum(TILES)) for c in range(len(TILES) + 1)]
    edges = [min(local, end * LANES) for end in ends]
    assert all(begin < end for begin, end in zip(edges[:-1], edges[1:]))
    spans = list(zip(edges[:-1], edges[1:]))
    sizes = [end - begin for begin, end in spans]
    roles = {0: bits[:1], 1: bits[1:-2], 2: bits[-2:-1], 3: bits[-1:]}
    orders = [sum((roles.get(role, [role]) for role in order), []) for order in ORDERS]
    quarter = shards // 4
    lines = {
        "in": [(d + end, d + to) for d in range(quarter) for end, to in ((0, quarter), (3 * quarter, 2 * quarter))],
        "mid": [(d + end, d + 3 * quarter - end) for d in range(quarter) for end in (quarter, 2 * quarter)],
    }
    lines["out"] = [(to, end) for end, to in lines["in"]]
    first = FIRST
    loads = [c for what, c in plan(bits, tokens, sizes, orders, first, ()) if what in ("step", "last")]
    total = None
    loaded = {}
    chunks = {}
    stages = [0] * len(spans)
    room = 40 * 2**20
    for what, c in plan(bits, tokens, sizes, orders, first, loads):
        if what == "mix":
            chunks[c] = ran(mix(activations, rotation_small, (0, tokens), spans[c], after))
        elif what == "load":
            wanted = (distances, share) if c == loads[-1] else ()
            loaded[c] = ran(load(me, down_weight, spans[c], after, room // 2**20, *wanted))[0]
            room -= loaded[c].size * 2
        elif what == "fold":
            stage = orders[c][stages[c]]
            stages[c] += 1
            scale = factor if stages[c] == len(orders[c]) else None
            if stage == "in":
                got = lax.ppermute(chunks[c], "tensor", lines["in"])
                chunks[c] = ran(pair(me, chunks[c], got, quarter, after))
            elif stage == "mid":
                got = lax.ppermute(chunks[c], "tensor", lines["mid"])
                chunks[c] = ran(meet(me, chunks[c], got, quarter, after))
            elif stage == "out":
                keep, give = chunks[c]
                got = lax.ppermute(give, "tensor", lines["out"])
                chunks[c] = ran(settle(me, keep, got, quarter, after, scale))
            else:
                chunks[c] = ran(fold(me, chunks[c], swap(chunks[c], stage), stage, after, scale))
        elif what == "tick":
            ran(tick(after))
        elif what == "step":
            total = ran(step(chunks[c], loaded[c], total, shards, after))

    inner = bits[1:]
    late = inner[-1:] + inner[:-1]
    swapped = [inner[1], inner[0]] + inner[2:]
    half = tokens // 2
    routes = [
        [((0, half), inner), ((half, tokens), late)],
        [((0, half), swapped), ((half, tokens), inner)],
    ][:parts]
    links = Links(bits)
    clock = 0.0
    kernels = 0
    pieces = []
    queue = []

    def send(x, bit, use):
        nonlocal clock
        clock += 0.9
        queue.append((links.send(bit, x.size, clock), kernels, swap(x, bit), use))

    def split(part, stage, pieces_of, left, keep, got):
        base = pieces_of[0][0][0]
        plans = [((begin - base, end - base), route[stage]) for (begin, end), route in pieces_of]
        outs = ran(halve(keep, got, left, plans, after))
        for i, (rows, route) in enumerate(pieces_of):
            rest = [d for d in left if not d & route[stage]]
            if stage + 1 < len(inner):
                use = functools.partial(split, part, stage + 1, [(rows, route)], rest, outs[2 * i])
            else:
                use = functools.partial(close, part, rows, outs[2 * i])
            send(outs[2 * i + 1], route[stage], use)

    def close(part, rows, keep, got):
        last = len(pieces) + 1 == parts * len(routes[0])
        held = pieces + [(rows, part, None)] if last else []
        pieces.append((rows, part, ran(finish(held, keep, got, tokens, width, parts, after))))

    last_chunk, last_columns = chunks[loads[-1]], loaded[loads[-1]]
    sends = ran(product(me, last_chunk, last_columns, total, 0, distances[:len(near)], parts, after))
    clock += 0.9
    kernels += 1
    for x in sends:
        send(x, bits[0], None)
    keeps = ran(product(me, last_chunk, last_columns, total, len(near), near, parts, after))
    clock += 0.9
    kernels += 1
    queue[:] = [
        (when, at, got, functools.partial(split, part, 0, routes[part], near, keeps[part]))
        for part, (when, at, got, _) in enumerate(queue)
    ]
    while queue:
        item = min(queue, key=lambda item: item[0])
        queue.remove(item)
        when, at, got, use = item
        if at == kernels:
            ran(tick(after))
            kernels += 1
            clock += 0.1
        clock = max(clock, when) + 0.15
        kernels += 1
        use(got)
    return pieces[-1][2]


def solution(mesh):
    placed = (P("groups", "tensor"), P(), P("tensor", None))
    return jax.shard_map(
        body, mesh=mesh, in_specs=placed, out_specs=P("groups", "tensor"), check_vma=False
    )
```

```python
import functools

import jax
import jax.numpy as jnp
import numpy as np
from jax import lax
from jax.experimental import pallas as pl
from jax.experimental.pallas import tpu as pltpu
from jax.sharding import PartitionSpec as P

LANES = 128
F32 = jnp.float32
BF16 = jnp.bfloat16


TILES = (6, 7)


def quotient(index, divisor, limit):
    shift = 16
    scale = -(-(1 << shift) // divisor)
    numbers = np.arange(limit, dtype=np.int64)
    assert np.array_equal((numbers * scale) >> shift, numbers // divisor)
    assert limit * scale < 2**31
    return (index * scale) >> shift


def sign_of(common, count):
    parity = common
    for place in range(1, count):
        parity = parity ^ (common >> place)
    return (1 - 2 * (parity & 1)).astype(F32)


def mix_kernel(rows, start, group, activations, small, *refs):
    out = refs[-1]
    local = activations.shape[1]
    block = small.shape[0]
    tokens, cols = out.shape
    tall = group * block
    span = local // block
    low = group.bit_length() - 1
    high = span.bit_length() - 1 - low
    full = small[...]
    head = full.astype(BF16)
    tail = (full - head.astype(F32)).astype(BF16)

    row = lax.broadcasted_iota(jnp.int32, (tall, block), 0)
    unit = lax.broadcasted_iota(jnp.int32, (tall, block), 1)
    spread_rows = (row - quotient(row, block, tall) * block == unit).astype(F32).astype(BF16)
    col = lax.broadcasted_iota(jnp.int32, (block, cols), 1) + start
    unit = lax.broadcasted_iota(jnp.int32, (block, cols), 0)
    spread_cols = (col - quotient(col, block, local) * block == unit).astype(F32).astype(BF16)
    at_row = quotient(lax.broadcasted_iota(jnp.int32, (tall, cols), 0), block, tall)
    at_col = quotient(lax.broadcasted_iota(jnp.int32, (tall, cols), 1) + start, block, local)
    sign = sign_of(at_row & at_col, max(low, 1))

    def tiled(part):
        rolled = jnp.dot(spread_rows, part, preferred_element_type=F32).astype(BF16)
        return (jnp.dot(rolled, spread_cols, preferred_element_type=F32) * sign).astype(BF16)

    head, tail = tiled(head), tiled(tail)
    owner = quotient(lax.broadcasted_iota(jnp.int32, (8, cols), 1) + start, block, local) >> low
    total = jnp.zeros((tokens, cols), F32)
    for piece in range(span // group):
        values = activations[rows[0]:rows[1], piece * tall:(piece + 1) * tall]
        term = jnp.dot(values, head, preferred_element_type=F32)
        term = term + jnp.dot(values, tail, preferred_element_type=F32)
        total = total + term * sign_of(owner & piece, max(high, 1))[0:1]
    out[...] = total


VMEM = pl.BlockSpec(memory_space=pltpu.VMEM)
SMEM = pl.BlockSpec(memory_space=pltpu.SMEM)
UNREAD = pl.BlockSpec(memory_space=pl.ANY)
COST = pl.CostEstimate(flops=10**10, bytes_accessed=10**8, transcendentals=0)


def call(name, kernel, operands, specs, shapes, after, scratch=(), limit=16):
    return pl.pallas_call(
        kernel,
        out_shape=shapes,
        in_specs=list(specs) + [UNREAD] * len(after),
        out_specs=jax.tree.map(lambda _: VMEM, shapes),
        scratch_shapes=list(scratch),
        cost_estimate=COST,
        compiler_params=pltpu.CompilerParams(vmem_limit_bytes=limit * 2**20),
        name=name,
    )(*operands, *after)


def mix(activations, small, rows, cols, after):
    block = small.shape[0]
    group = min(4, activations.shape[1] // block)
    kernel = functools.partial(mix_kernel, rows, cols[0], group)
    shape = jax.ShapeDtypeStruct((rows[1] - rows[0], cols[1] - cols[0]), F32)
    return call("mix", kernel, (activations, small), (VMEM, VMEM), shape, after)


def spread(blocks, after):
    shards, rows, cols = blocks.shape

    def kernel(blocks_ref, *refs):
        out = refs[-1]
        for at in range(0, cols, LANES):
            end = min(at + LANES, cols)
            values = [blocks_ref[s, :, at:end] for s in range(shards)]
            reach = 1
            while reach < shards:
                values = [
                    values[s ^ reach] - values[s] if s & reach else values[s] + values[s ^ reach]
                    for s in range(shards)
                ]
                reach *= 2
            for s in range(shards):
                out[s, :, at:end] = values[s]

    shape = jax.ShapeDtypeStruct(blocks.shape, F32)
    return call("spread", kernel, (blocks,), (VMEM,), shape, after)


def settle(values, factor, after):
    def kernel(values_ref, *refs):
        refs[-1][...] = (values_ref[...] * factor).astype(BF16)

    shape = jax.ShapeDtypeStruct(values.shape, BF16)
    return call("settle", kernel, (values,), (VMEM,), shape, after)


def load(me, weight, rows, after, limit, distances=(), share=0):
    begin, end = rows

    def kernel(me_ref, weight_ref, *refs):
        out, mark, sems = refs[-3:]
        copies = []
        if not distances:
            copies.append(pltpu.make_async_copy(weight_ref.at[begin:end, :], out, sems.at[0]))
        for i, distance in enumerate(distances):
            column = pl.multiple_of((distance ^ me_ref[0]) * share, LANES)
            copies.append(
                pltpu.make_async_copy(
                    weight_ref.at[begin:end, pl.ds(column, share)], out.at[:, pl.ds(i * share, share)], sems.at[i]
                )
            )
        for copy in copies:
            copy.start()
        mark[...] = jnp.zeros_like(mark)
        for copy in copies:
            copy.wait()

    shapes = [
        jax.ShapeDtypeStruct((end - begin, weight.shape[1]), BF16),
        jax.ShapeDtypeStruct((8, LANES), F32),
    ]
    return call(
        "load",
        kernel,
        (me, weight),
        (SMEM, pl.BlockSpec(memory_space=pltpu.HBM)),
        shapes,
        after,
        [pltpu.SemaphoreType.DMA((max(1, len(distances)),))],
        limit,
    )


def step(chunk, columns, total, shards, after):
    tokens = chunk.shape[0]
    share = columns.shape[1] // shards
    group = max(1, 1024 // share)
    values = [chunk, columns] + ([] if total is None else [total])

    def kernel(*refs):
        out = refs[-1]
        for at in range(0, shards, group):
            sums = jnp.dot(refs[0][...], refs[1][:, at * share:(at + group) * share], preferred_element_type=F32)
            for i in range(group):
                term = sums[:, i * share:(i + 1) * share]
                out[at + i] = term if total is None else refs[2][at + i] + term

    shape = jax.ShapeDtypeStruct((shards, tokens, share), F32)
    return call("step", kernel, values, [VMEM] * len(values), shape, after)


def product(me, chunk, columns, total, begin, distances, parts, after):
    share = total.shape[2]
    width = share // parts
    group = max(1, min(len(distances), 1024 // share))

    def kernel(me_ref, chunk_ref, columns_ref, total_ref, *refs):
        outs = refs[-parts:]
        for at in range(0, len(distances), group):
            start = (begin + at) * share
            sums = jnp.dot(
                chunk_ref[...], columns_ref[:, start:start + group * share], preferred_element_type=F32
            )
            for i in range(group):
                value = total_ref[distances[at + i] ^ me_ref[0]] + sums[:, i * share:(i + 1) * share]
                for part in range(parts):
                    outs[part][at + i] = value[:, part * width:(part + 1) * width]

    shapes = [jax.ShapeDtypeStruct((len(distances), chunk.shape[0], width), F32)] * parts
    return call("product", kernel, (me, chunk, columns, total), [SMEM] + [VMEM] * 3, shapes, after)


def halve(own, got, distances, plans, after):
    shapes = []
    for rows, _ in plans:
        shapes += [jax.ShapeDtypeStruct((len(distances) // 2, rows[1] - rows[0], own.shape[2]), F32)] * 2

    def kernel(own_ref, got_ref, *refs):
        outs = refs[-len(shapes):]
        for at, ((begin, end), bit) in enumerate(plans):
            for place, d in enumerate(d for d in distances if not d & bit):
                for out, source in ((outs[2 * at], d), (outs[2 * at + 1], d | bit)):
                    i = distances.index(source)
                    out[place] = own_ref[i, begin:end, :] + got_ref[i, begin:end, :]

    return call("halve", kernel, (own, got), (VMEM, VMEM), shapes, after)


def tick(after):
    def kernel(*refs):
        refs[-1][...] = jnp.zeros_like(refs[-1])

    return call("tick", kernel, (), (), jax.ShapeDtypeStruct((8, LANES), F32), after)


def finish(pieces, own, got, tokens, width, parts, after):
    held = [x for _, _, x in pieces[:-1]] if len(pieces) > 1 else []

    def kernel(own_ref, got_ref, *refs):
        out = refs[-1]
        value = (own_ref[0] + got_ref[0]).astype(BF16)
        if not pieces:
            out[...] = value
            return
        for ((begin, end), part, _), ref in zip(pieces, [*refs[:len(held)], None]):
            out[begin:end, part * width:(part + 1) * width] = value if ref is None else ref[...]

    shape = (tokens, width * parts) if pieces else own.shape[1:]
    operands = (own, got, *held)
    return call("finish", kernel, operands, [VMEM] * len(operands), jax.ShapeDtypeStruct(shape, BF16), after)


class Links:
    def __init__(self, bits):
        self.bits = bits
        self.taken = {bit: [] for bit in bits}

    def needs(self, bit, size):
        if bit == self.bits[0]:
            return {bit: size * 8e-6}
        if bit != self.bits[-1]:
            return {bit: size * 80e-6}
        return {bit: size * 160e-6, self.bits[-2]: size * 80e-6}

    def free(self, bit, now):
        share, until = 1.0, float("inf")
        for begin, end, used in self.taken[bit]:
            if begin <= now < end:
                share -= used
            if begin <= now < end or begin > now:
                until = min(until, end if begin <= now else begin)
        return max(share, 0.0), until

    def send(self, bit, size, now):
        needs = self.needs(bit, size)
        now += 1.0
        left = 1.0
        spans = []
        while left > 1e-6:
            shares = [(self.free(link, now), need) for link, need in needs.items()]
            rate = min(share / need for (share, _), need in shares)
            until = min(until for (_, until), _ in shares)
            if rate > 1e-6:
                until = min(until, now + left / rate)
                spans.append((now, until, rate))
                left -= rate * (until - now)
            now = until
        for begin, end, rate in spans:
            for link, need in needs.items():
                self.taken[link].append((begin, end, rate * need))
        return now + 0.3


def body(activations, rotation_small, down_weight):
    shards = lax.axis_size("tensor")
    me = lax.axis_index("tensor").astype(jnp.int32).reshape(1)
    tokens, local = activations.shape
    block = rotation_small.shape[0]
    share = down_weight.shape[1] // shards
    factor = (local // block * shards) ** (-0.5)
    bits = [1 << place for place in range(shards.bit_length() - 1)]
    assert len(bits) >= 3 and shards == 1 << len(bits)
    after = []

    def swap(x, bit):
        return lax.ppermute(x, "tensor", [(d, d ^ bit) for d in range(shards)])

    def ran(outs, link=-1):
        after[:] = [jax.tree.leaves(outs)[link]]
        return outs

    parts = 2 if share % (2 * LANES) == 0 else 1
    width = share // parts
    near = [d for d in range(shards) if not d & bits[0]]
    distances = [d | bits[0] for d in near] + near

    tiles = -(-local // LANES)
    ends = [round(tiles * sum(TILES[:c]) / sum(TILES)) for c in range(len(TILES) + 1)]
    edges = [min(local, end * LANES) for end in ends]
    assert all(begin < end for begin, end in zip(edges[:-1], edges[1:]))
    spans = list(zip(edges[:-1], edges[1:]))
    count = len(spans)

    def exchange(x):
        return lax.all_to_all(x, "tensor", split_axis=0, concat_axis=0)

    room = 40 * 2**20
    chunks, loaded = [], []
    for span in spans:
        x = ran(mix(activations, rotation_small, (0, tokens), span, after))
        chunks.append(exchange(x.reshape(shards, tokens // shards, -1)))
    for c, span in enumerate(spans):
        wanted = (distances, share) if c == count - 1 else ()
        loaded.append(ran(load(me, down_weight, span, after, room // 2**20, *wanted))[0])
        room -= loaded[c].size * 2
    for c in range(count):
        chunks[c] = exchange(ran(spread(chunks[c], after))).reshape(tokens, -1)
    total = None
    for c in range(count):
        chunks[c] = ran(settle(chunks[c], factor, after))
        if c < count - 1:
            total = ran(step(chunks[c], loaded[c], total, shards, after))

    inner = bits[1:]
    late = inner[-1:] + inner[:-1]
    swapped = [inner[1], inner[0]] + inner[2:]
    half = tokens // 2
    routes = [
        [((0, half), inner), ((half, tokens), late)],
        [((0, half), swapped), ((half, tokens), inner)],
    ][:parts]
    links = Links(bits)
    clock = 0.0
    kernels = 0
    pieces = []
    queue = []

    def send(x, bit, use):
        nonlocal clock
        clock += 0.9
        queue.append((links.send(bit, x.size, clock), kernels, swap(x, bit), use))

    def split(part, stage, pieces_of, left, keep, got):
        base = pieces_of[0][0][0]
        plans = [((begin - base, end - base), route[stage]) for (begin, end), route in pieces_of]
        outs = ran(halve(keep, got, left, plans, after))
        for i, (rows, route) in enumerate(pieces_of):
            rest = [d for d in left if not d & route[stage]]
            if stage + 1 < len(inner):
                use = functools.partial(split, part, stage + 1, [(rows, route)], rest, outs[2 * i])
            else:
                use = functools.partial(close, part, rows, outs[2 * i])
            send(outs[2 * i + 1], route[stage], use)

    def close(part, rows, keep, got):
        last = len(pieces) + 1 == parts * len(routes[0])
        held = pieces + [(rows, part, None)] if last else []
        pieces.append((rows, part, ran(finish(held, keep, got, tokens, width, parts, after))))

    last_chunk, last_columns = chunks[-1], loaded[-1]
    sends = ran(product(me, last_chunk, last_columns, total, 0, distances[:len(near)], parts, after))
    clock += 0.9
    kernels += 1
    for x in sends:
        send(x, bits[0], None)
    keeps = ran(product(me, last_chunk, last_columns, total, len(near), near, parts, after))
    clock += 0.9
    kernels += 1
    queue[:] = [
        (when, at, got, functools.partial(split, part, 0, routes[part], near, keeps[part]))
        for part, (when, at, got, _) in enumerate(queue)
    ]
    while queue:
        item = min(queue, key=lambda item: item[0])
        queue.remove(item)
        when, at, got, use = item
        if at == kernels:
            ran(tick(after))
            kernels += 1
            clock += 0.1
        clock = max(clock, when) + 0.15
        kernels += 1
        use(got)
    return pieces[-1][2]


def solution(mesh):
    placed = (P("groups", "tensor"), P(), P("tensor", None))
    return jax.shard_map(
        body, mesh=mesh, in_specs=placed, out_specs=P("groups", "tensor"), check_vma=False
    )
```

```python
import functools

import jax
import jax.numpy as jnp
import numpy as np
from jax import lax
from jax.experimental import pallas as pl
from jax.experimental.pallas import tpu as pltpu
from jax.sharding import PartitionSpec as P

LANES = 128
F32 = jnp.float32
BF16 = jnp.bfloat16


TILES = (4, 4, 5)
ORDERS = ((1, 3, 0, 2), (2, 1, 0, 3), (3, 0, 2, 1))
FIRST = (2, 1, 0)
PATIENCE = 1.8
PIECES = 4


def quotient(index, divisor, limit):
    shift = 16
    scale = -(-(1 << shift) // divisor)
    numbers = np.arange(limit, dtype=np.int64)
    assert np.array_equal((numbers * scale) >> shift, numbers // divisor)
    assert limit * scale < 2**31
    return (index * scale) >> shift


def sign_of(common, count):
    parity = common
    for place in range(1, count):
        parity = parity ^ (common >> place)
    return (1 - 2 * (parity & 1)).astype(F32)


def mix_kernel(rows, start, group, activations, small, *refs):
    out = refs[-1]
    local = activations.shape[1]
    block = small.shape[0]
    tokens, cols = out.shape
    tall = group * block
    span = local // block
    low = group.bit_length() - 1
    high = span.bit_length() - 1 - low
    full = small[...]
    head = full.astype(BF16)
    tail = (full - head.astype(F32)).astype(BF16)

    row = lax.broadcasted_iota(jnp.int32, (tall, block), 0)
    unit = lax.broadcasted_iota(jnp.int32, (tall, block), 1)
    spread_rows = (row - quotient(row, block, tall) * block == unit).astype(F32).astype(BF16)
    col = lax.broadcasted_iota(jnp.int32, (block, cols), 1) + start
    unit = lax.broadcasted_iota(jnp.int32, (block, cols), 0)
    spread_cols = (col - quotient(col, block, local) * block == unit).astype(F32).astype(BF16)
    at_row = quotient(lax.broadcasted_iota(jnp.int32, (tall, cols), 0), block, tall)
    at_col = quotient(lax.broadcasted_iota(jnp.int32, (tall, cols), 1) + start, block, local)
    sign = sign_of(at_row & at_col, max(low, 1))

    def tiled(part):
        rolled = jnp.dot(spread_rows, part, preferred_element_type=F32).astype(BF16)
        return (jnp.dot(rolled, spread_cols, preferred_element_type=F32) * sign).astype(BF16)

    head, tail = tiled(head), tiled(tail)
    owner = quotient(lax.broadcasted_iota(jnp.int32, (8, cols), 1) + start, block, local) >> low
    total = jnp.zeros((tokens, cols), F32)
    for piece in range(span // group):
        values = activations[rows[0]:rows[1], piece * tall:(piece + 1) * tall]
        term = jnp.dot(values, head, preferred_element_type=F32)
        term = term + jnp.dot(values, tail, preferred_element_type=F32)
        total = total + term * sign_of(owner & piece, max(high, 1))[0:1]
    out[...] = total


VMEM = pl.BlockSpec(memory_space=pltpu.VMEM)
SMEM = pl.BlockSpec(memory_space=pltpu.SMEM)
UNREAD = pl.BlockSpec(memory_space=pl.ANY)
COST = pl.CostEstimate(flops=10**10, bytes_accessed=10**8, transcendentals=0)


def call(name, kernel, operands, specs, shapes, after, scratch=(), limit=12):
    return pl.pallas_call(
        kernel,
        out_shape=shapes,
        in_specs=list(specs) + [UNREAD] * len(after),
        out_specs=jax.tree.map(lambda _: VMEM, shapes),
        scratch_shapes=list(scratch),
        cost_estimate=COST,
        compiler_params=pltpu.CompilerParams(vmem_limit_bytes=limit * 2**20),
        name=name,
    )(*operands, *after)


def mix(activations, small, rows, cols, after):
    block = small.shape[0]
    group = min(4, activations.shape[1] // block)
    kernel = functools.partial(mix_kernel, rows, cols[0], group)
    shape = jax.ShapeDtypeStruct((rows[1] - rows[0], cols[1] - cols[0]), F32)
    return call("mix", kernel, (activations, small), (VMEM, VMEM), shape, after)


def fold(me, own, got, bit, after, factor=None):
    def kernel(me_ref, own_ref, got_ref, *refs):
        sign = jnp.where((me_ref[0] & bit) != 0, -1.0, 1.0).astype(F32)
        total = got_ref[...] + own_ref[...] * sign
        if factor is not None:
            total = total * factor
        refs[-1][...] = total.astype(refs[-1].dtype)

    shape = jax.ShapeDtypeStruct(own.shape, F32 if factor is None else BF16)
    return call("fold", kernel, (me, own, got), (SMEM, VMEM, VMEM), shape, after)


def pair(me, own, got, quarter, after):
    def kernel(me_ref, own_ref, got_ref, *refs):
        sign = jnp.where(me_ref[0] // quarter == 2, -1.0, 1.0).astype(F32)
        refs[-1][0] = got_ref[...] + own_ref[...]
        refs[-1][1] = (got_ref[...] - own_ref[...]) * sign

    shape = jax.ShapeDtypeStruct((2, *own.shape), F32)
    return call("pair", kernel, (me, own, got), (SMEM, VMEM, VMEM), shape, after)


def meet(me, own, got, quarter, after):
    def kernel(me_ref, own_ref, got_ref, *refs):
        keep, give = refs[-2:]
        third = me_ref[0] // quarter == 2

        @pl.when(third)
        def _():
            keep[...] = got_ref[0] - own_ref[0]
            give[...] = got_ref[1] - own_ref[1]

        @pl.when(jnp.logical_not(third))
        def _():
            keep[...] = got_ref[1] + own_ref[1]
            give[...] = got_ref[0] + own_ref[0]

    shapes = [jax.ShapeDtypeStruct(own.shape[1:], F32)] * 2
    return call("meet", kernel, (me, own, got), (SMEM, VMEM, VMEM), shapes, after)


def settle(me, own, got, quarter, after, factor=None):
    def kernel(me_ref, own_ref, got_ref, *refs):
        place = me_ref[0] // quarter
        total = jnp.where(jnp.logical_or(place == 0, place == 3), got_ref[...], own_ref[...])
        if factor is not None:
            total = total * factor
        refs[-1][...] = total.astype(refs[-1].dtype)

    shape = jax.ShapeDtypeStruct(own.shape, F32 if factor is None else BF16)
    return call("settle", kernel, (me, own, got), (SMEM, VMEM, VMEM), shape, after)


def load(me, weight, rows, after, limit, distances=(), share=0):
    begin, end = rows

    def kernel(me_ref, weight_ref, *refs):
        out, mark, sems = refs[-3:]
        copies = []
        rows_each = (end - begin) // PIECES // 16 * 16
        for i in range(PIECES if not distances else 0):
            low = i * rows_each
            high = low + rows_each if i + 1 < PIECES else end - begin
            copies.append(
                pltpu.make_async_copy(weight_ref.at[begin + low:begin + high, :], out.at[low:high, :], sems.at[i])
            )
        for i, distance in enumerate(distances):
            column = pl.multiple_of((distance ^ me_ref[0]) * share, LANES)
            copies.append(
                pltpu.make_async_copy(
                    weight_ref.at[begin:end, pl.ds(column, share)], out.at[:, pl.ds(i * share, share)], sems.at[i]
                )
            )
        for copy in copies:
            copy.start()
        mark[...] = jnp.zeros_like(mark)
        for copy in copies:
            copy.wait()

    shapes = [
        jax.ShapeDtypeStruct((end - begin, weight.shape[1]), BF16),
        jax.ShapeDtypeStruct((8, LANES), F32),
    ]
    return call(
        "load",
        kernel,
        (me, weight),
        (SMEM, pl.BlockSpec(memory_space=pltpu.HBM)),
        shapes,
        after,
        [pltpu.SemaphoreType.DMA((max(PIECES, len(distances)),))],
        limit,
    )


def step(chunk, columns, total, shards, after):
    tokens = chunk.shape[0]
    share = columns.shape[1] // shards
    group = max(1, 1024 // share)
    values = [chunk, columns] + ([] if total is None else [total])

    def kernel(*refs):
        out = refs[-1]
        for at in range(0, shards, group):
            sums = jnp.dot(refs[0][...], refs[1][:, at * share:(at + group) * share], preferred_element_type=F32)
            for i in range(group):
                term = sums[:, i * share:(i + 1) * share]
                out[at + i] = term if total is None else refs[2][at + i] + term

    shape = jax.ShapeDtypeStruct((shards, tokens, share), F32)
    return call("step", kernel, values, [VMEM] * len(values), shape, after)


def product(me, chunk, columns, total, begin, distances, parts, after):
    share = total.shape[2]
    width = share // parts
    group = max(1, min(len(distances), 1024 // share))

    def kernel(me_ref, chunk_ref, columns_ref, total_ref, *refs):
        outs = refs[-parts:]
        for at in range(0, len(distances), group):
            start = (begin + at) * share
            sums = jnp.dot(
                chunk_ref[...], columns_ref[:, start:start + group * share], preferred_element_type=F32
            )
            for i in range(group):
                value = total_ref[distances[at + i] ^ me_ref[0]] + sums[:, i * share:(i + 1) * share]
                for part in range(parts):
                    outs[part][at + i] = value[:, part * width:(part + 1) * width]

    shapes = [jax.ShapeDtypeStruct((len(distances), chunk.shape[0], width), F32)] * parts
    return call("product", kernel, (me, chunk, columns, total), [SMEM] + [VMEM] * 3, shapes, after)


def halve(own, got, distances, plans, after):
    shapes = []
    for rows, _ in plans:
        shapes += [jax.ShapeDtypeStruct((len(distances) // 2, rows[1] - rows[0], own.shape[2]), F32)] * 2

    def kernel(own_ref, got_ref, *refs):
        outs = refs[-len(shapes):]
        for at, ((begin, end), bit) in enumerate(plans):
            for place, d in enumerate(d for d in distances if not d & bit):
                for out, source in ((outs[2 * at], d), (outs[2 * at + 1], d | bit)):
                    i = distances.index(source)
                    out[place] = own_ref[i, begin:end, :] + got_ref[i, begin:end, :]

    return call("halve", kernel, (own, got), (VMEM, VMEM), shapes, after)


def tick(after):
    def kernel(*refs):
        refs[-1][...] = jnp.zeros_like(refs[-1])

    return call("tick", kernel, (), (), jax.ShapeDtypeStruct((8, LANES), F32), after)


def finish(pieces, own, got, tokens, width, parts, after):
    held = [x for _, _, x in pieces[:-1]] if len(pieces) > 1 else []

    def kernel(own_ref, got_ref, *refs):
        out = refs[-1]
        value = (own_ref[0] + got_ref[0]).astype(BF16)
        if not pieces:
            out[...] = value
            return
        for ((begin, end), part, _), ref in zip(pieces, [*refs[:len(held)], None]):
            out[begin:end, part * width:(part + 1) * width] = value if ref is None else ref[...]

    shape = (tokens, width * parts) if pieces else own.shape[1:]
    operands = (own, got, *held)
    return call("finish", kernel, operands, [VMEM] * len(operands), jax.ShapeDtypeStruct(shape, BF16), after)


class Links:
    def __init__(self, bits):
        self.bits = bits
        self.taken = {link: [] for link in bits[:-2] + ["in", "mid", "out"]}

    def needs(self, stage, size):
        if stage == self.bits[0]:
            return {stage: size * 8e-6}
        if stage == self.bits[-1]:
            return {"mid": size * 160e-6, "in": size * 100e-6, "out": size * 100e-6}
        if stage == self.bits[-2]:
            return {"in": size * 80e-6, "out": size * 80e-6}
        return {stage: size * 80e-6}

    def free(self, bit, now):
        share, until = 1.0, float("inf")
        for begin, end, used in self.taken[bit]:
            if begin <= now < end:
                share -= used
            if begin <= now < end or begin > now:
                until = min(until, end if begin <= now else begin)
        return max(share, 0.0), until

    def send(self, bit, size, now):
        needs = self.needs(bit, size)
        now += 1.0
        left = 1.0
        spans = []
        while left > 1e-6:
            shares = [(self.free(link, now), need) for link, need in needs.items()]
            rate = min(share / need for (share, _), need in shares)
            until = min(until for (_, until), _ in shares)
            if rate > 1e-6:
                until = min(until, now + left / rate)
                spans.append((now, until, rate))
                left -= rate * (until - now)
            now = until
        for begin, end, rate in spans:
            for link, need in needs.items():
                self.taken[link].append((begin, end, rate * need))
        return now + 0.3


def plan(bits, tokens, sizes, orders, first, loads):
    links = Links(bits)
    clock = 1.8
    flights = []
    done = []
    wait = list(first)
    loads = list(loads)
    missing = list(loads)

    def start(c, stage):
        nonlocal clock
        clock += 1.2
        what = orders[c][stage]
        size = tokens * sizes[c] * (2 if what == "mid" else 1)
        flights.append((links.send(what, size, clock), len(done), c, stage))

    while wait or flights:
        flights.sort()
        arrival = flights[0][0] if flights else float("inf")
        if wait and arrival > clock:
            done.append(("mix", wait[0]))
            clock += 1.2
            start(wait.pop(0), 0)
        elif loads and arrival - clock > PATIENCE:
            done.append(("load", loads.pop(0)))
            clock += 2.8
        else:
            _, began, c, stage = flights.pop(0)
            if began == len(done):
                done.append(("tick", c))
            clock = max(clock, arrival) + 0.1
            done.append(("fold", c))
            if stage + 1 < len(orders[c]):
                start(c, stage + 1)
            elif flights or wait:
                if c in loads:
                    loads.remove(c)
                    done.append(("load", c))
                    clock += 2.8
                done.append(("step", c))
                clock += 1.3
            else:
                done += [("load", c) for c in loads]
                done.append(("last", c))
    return done


def body(activations, rotation_small, down_weight):
    shards = lax.axis_size("tensor")
    me = lax.axis_index("tensor").astype(jnp.int32).reshape(1)
    tokens, local = activations.shape
    block = rotation_small.shape[0]
    share = down_weight.shape[1] // shards
    factor = (local // block * shards) ** (-0.5)
    bits = [1 << place for place in range(shards.bit_length() - 1)]
    assert len(bits) >= 3 and shards == 1 << len(bits)
    after = []

    def swap(x, bit):
        return lax.ppermute(x, "tensor", [(d, d ^ bit) for d in range(shards)])

    def ran(outs, link=-1):
        after[:] = [jax.tree.leaves(outs)[link]]
        return outs

    parts = 2 if share % (2 * LANES) == 0 else 1
    width = share // parts
    near = [d for d in range(shards) if not d & bits[0]]
    distances = [d | bits[0] for d in near] + near

    tiles = -(-local // LANES)
    ends = [round(tiles * sum(TILES[:c]) / sum(TILES)) for c in range(len(TILES) + 1)]
    edges = [min(local, end * LANES) for end in ends]
    assert all(begin < end for begin, end in zip(edges[:-1], edges[1:]))
    spans = list(zip(edges[:-1], edges[1:]))
    sizes = [end - begin for begin, end in spans]
    roles = {0: bits[:1], 1: bits[1:-2], 2: bits[-2:-1], 3: bits[-1:]}
    orders = [sum((roles.get(role, [role]) for role in order), []) for order in ORDERS]
    quarter = shards // 4
    lines = {
        "in": [(d + end, d + to) for d in range(quarter) for end, to in ((0, quarter), (3 * quarter, 2 * quarter))],
        "mid": [(d + end, d + 3 * quarter - end) for d in range(quarter) for end in (quarter, 2 * quarter)],
    }
    lines["out"] = [(to, end) for end, to in lines["in"]]
    first = FIRST
    loads = [c for what, c in plan(bits, tokens, sizes, orders, first, ()) if what in ("step", "last")]
    total = None
    loaded = {}
    chunks = {}
    stages = [0] * len(spans)
    room = 40 * 2**20
    for what, c in plan(bits, tokens, sizes, orders, first, loads):
        if what == "mix":
            chunks[c] = ran(mix(activations, rotation_small, (0, tokens), spans[c], after))
        elif what == "load":
            wanted = (distances, share) if c == loads[-1] else ()
            loaded[c] = ran(load(me, down_weight, spans[c], after, room // 2**20, *wanted))[0]
            room -= loaded[c].size * 2
        elif what == "fold":
            stage = orders[c][stages[c]]
            stages[c] += 1
            scale = factor if stages[c] == len(orders[c]) else None
            if stage == "in":
                got = lax.ppermute(chunks[c], "tensor", lines["in"])
                chunks[c] = ran(pair(me, chunks[c], got, quarter, after))
            elif stage == "mid":
                got = lax.ppermute(chunks[c], "tensor", lines["mid"])
                chunks[c] = ran(meet(me, chunks[c], got, quarter, after))
            elif stage == "out":
                keep, give = chunks[c]
                got = lax.ppermute(give, "tensor", lines["out"])
                chunks[c] = ran(settle(me, keep, got, quarter, after, scale))
            else:
                chunks[c] = ran(fold(me, chunks[c], swap(chunks[c], stage), stage, after, scale))
        elif what == "tick":
            ran(tick(after))
        elif what == "step":
            total = ran(step(chunks[c], loaded[c], total, shards, after))

    inner = bits[1:]
    late = inner[-1:] + inner[:-1]
    swapped = [inner[1], inner[0]] + inner[2:]
    half = tokens // 2
    routes = [
        [((0, half), inner), ((half, tokens), late)],
        [((0, half), swapped), ((half, tokens), inner)],
    ][:parts]
    links = Links(bits)
    clock = 0.0
    kernels = 0
    pieces = []
    queue = []

    def send(x, bit, use):
        nonlocal clock
        clock += 0.9
        queue.append((links.send(bit, x.size, clock), kernels, swap(x, bit), use))

    def split(part, stage, pieces_of, left, keep, got):
        base = pieces_of[0][0][0]
        plans = [((begin - base, end - base), route[stage]) for (begin, end), route in pieces_of]
        outs = ran(halve(keep, got, left, plans, after))
        for i, (rows, route) in enumerate(pieces_of):
            rest = [d for d in left if not d & route[stage]]
            if stage + 1 < len(inner):
                use = functools.partial(split, part, stage + 1, [(rows, route)], rest, outs[2 * i])
            else:
                use = functools.partial(close, part, rows, outs[2 * i])
            send(outs[2 * i + 1], route[stage], use)

    def close(part, rows, keep, got):
        last = len(pieces) + 1 == parts * len(routes[0])
        held = pieces + [(rows, part, None)] if last else []
        pieces.append((rows, part, ran(finish(held, keep, got, tokens, width, parts, after))))

    last_chunk, last_columns = chunks[loads[-1]], loaded[loads[-1]]
    sends = ran(product(me, last_chunk, last_columns, total, 0, distances[:len(near)], parts, after))
    clock += 0.9
    kernels += 1
    for x in sends:
        send(x, bits[0], None)
    keeps = ran(product(me, last_chunk, last_columns, total, len(near), near, parts, after))
    clock += 0.9
    kernels += 1
    queue[:] = [
        (when, at, got, functools.partial(split, part, 0, routes[part], near, keeps[part]))
        for part, (when, at, got, _) in enumerate(queue)
    ]
    while queue:
        item = min(queue, key=lambda item: item[0])
        queue.remove(item)
        when, at, got, use = item
        if at == kernels:
            ran(tick(after))
            kernels += 1
            clock += 0.1
        clock = max(clock, when) + 0.15
        kernels += 1
        use(got)
    return pieces[-1][2]


def solution(mesh):
    placed = (P("groups", "tensor"), P(), P("tensor", None))
    return jax.shard_map(
        body, mesh=mesh, in_specs=placed, out_specs=P("groups", "tensor"), check_vma=False
    )
```

```python
import functools

import jax
import jax.numpy as jnp
import numpy as np
from jax import lax
from jax.experimental import pallas as pl
from jax.experimental.pallas import tpu as pltpu
from jax.sharding import PartitionSpec as P

LANES = 128
F32 = jnp.float32
BF16 = jnp.bfloat16


PIECES = 4
PERM = (0, 1, 3, 2)


def quotient(index, divisor, limit):
    shift = 16
    scale = -(-(1 << shift) // divisor)
    numbers = np.arange(limit, dtype=np.int64)
    assert np.array_equal((numbers * scale) >> shift, numbers // divisor)
    assert limit * scale < 2**31
    return (index * scale) >> shift


def sign_of(common, count):
    parity = common
    for place in range(1, count):
        parity = parity ^ (common >> place)
    return (1 - 2 * (parity & 1)).astype(F32)


def mix_kernel(rows, start, group, activations, small, *refs):
    out = refs[-1]
    local = activations.shape[1]
    block = small.shape[0]
    tokens, cols = out.shape
    tall = group * block
    span = local // block
    low = group.bit_length() - 1
    high = span.bit_length() - 1 - low
    full = small[...]
    head = full.astype(BF16)
    tail = (full - head.astype(F32)).astype(BF16)

    row = lax.broadcasted_iota(jnp.int32, (tall, block), 0)
    unit = lax.broadcasted_iota(jnp.int32, (tall, block), 1)
    spread_rows = (row - quotient(row, block, tall) * block == unit).astype(F32).astype(BF16)
    col = lax.broadcasted_iota(jnp.int32, (block, cols), 1) + start
    unit = lax.broadcasted_iota(jnp.int32, (block, cols), 0)
    spread_cols = (col - quotient(col, block, local) * block == unit).astype(F32).astype(BF16)
    at_row = quotient(lax.broadcasted_iota(jnp.int32, (tall, cols), 0), block, tall)
    at_col = quotient(lax.broadcasted_iota(jnp.int32, (tall, cols), 1) + start, block, local)
    sign = sign_of(at_row & at_col, max(low, 1))

    def tiled(part):
        rolled = jnp.dot(spread_rows, part, preferred_element_type=F32).astype(BF16)
        return (jnp.dot(rolled, spread_cols, preferred_element_type=F32) * sign).astype(BF16)

    head, tail = tiled(head), tiled(tail)
    owner = quotient(lax.broadcasted_iota(jnp.int32, (8, cols), 1) + start, block, local) >> low
    total = jnp.zeros((tokens, cols), F32)
    for piece in range(span // group):
        values = activations[rows[0]:rows[1], piece * tall:(piece + 1) * tall]
        term = jnp.dot(values, head, preferred_element_type=F32)
        term = term + jnp.dot(values, tail, preferred_element_type=F32)
        total = total + term * sign_of(owner & piece, max(high, 1))[0:1]
    out[...] = total


VMEM = pl.BlockSpec(memory_space=pltpu.VMEM)
SMEM = pl.BlockSpec(memory_space=pltpu.SMEM)
UNREAD = pl.BlockSpec(memory_space=pl.ANY)
COST = pl.CostEstimate(flops=10**10, bytes_accessed=10**8, transcendentals=0)


def call(name, kernel, operands, specs, shapes, after, scratch=(), limit=12):
    return pl.pallas_call(
        kernel,
        out_shape=shapes,
        in_specs=list(specs) + [UNREAD] * len(after),
        out_specs=jax.tree.map(lambda _: VMEM, shapes),
        scratch_shapes=list(scratch),
        cost_estimate=COST,
        compiler_params=pltpu.CompilerParams(vmem_limit_bytes=limit * 2**20),
        name=name,
    )(*operands, *after)


def mix(activations, small, rows, cols, after):
    block = small.shape[0]
    group = min(4, activations.shape[1] // block)
    kernel = functools.partial(mix_kernel, rows, cols[0], group)
    shape = jax.ShapeDtypeStruct((rows[1] - rows[0], cols[1] - cols[0]), F32)
    return call("mix", kernel, (activations, small), (VMEM, VMEM), shape, after)


def fetch(me, weight, out, sems, rows, distances):
    begin, end = rows
    copies = []
    if not distances:
        each = (end - begin) // PIECES // 16 * 16
        for i in range(PIECES):
            low, high = i * each, (i + 1) * each if i + 1 < PIECES else end - begin
            copies.append(
                pltpu.make_async_copy(weight.at[begin + low:begin + high, :], out.at[low:high, :], sems.at[i])
            )
    for i, distance in enumerate(distances):
        share = weight.shape[1] // len(distances)
        column = pl.multiple_of((distance ^ me) * share, LANES)
        copies.append(
            pltpu.make_async_copy(
                weight.at[begin:end, pl.ds(column, share)], out.at[:, pl.ds(i * share, share)], sems.at[i]
            )
        )
    for copy in copies:
        copy.start()
    return copies


def loading(name, work, operands, specs, shape, after, me, weight, rows, distances, limit):
    count = len(operands)

    def kernel(me_ref, weight_ref, *refs):
        columns, out, sems = refs[-3:]
        copies = fetch(me_ref[0], weight_ref, columns, sems, rows, distances)
        work(me_ref, refs[:count], out)
        for copy in copies:
            copy.wait()

    columns = jax.ShapeDtypeStruct((rows[1] - rows[0], weight.shape[1]), BF16)
    outs = call(
        name,
        kernel,
        (me, weight, *operands),
        [SMEM, pl.BlockSpec(memory_space=pltpu.HBM), *specs],
        [columns, shape],
        after,
        [pltpu.SemaphoreType.DMA((max(PIECES, len(distances)),))],
        limit,
    )
    return outs[1], outs[0]


def load(me, weight, rows, distances, limit, after):
    def work(me_ref, refs, out):
        out[...] = jnp.zeros_like(out)

    shape = jax.ShapeDtypeStruct((8, LANES), F32)
    return loading("load", work, (), (), shape, after, me, weight, rows, distances, limit)


def fold(me, own, got, bit, after, factor=None, *more):
    def work(me_ref, refs, out):
        own_ref, got_ref = refs
        sign = jnp.where((me_ref[0] & bit) != 0, -1.0, 1.0).astype(F32)
        total = got_ref[...] + own_ref[...] * sign
        if factor is not None:
            total = total * factor
        out[...] = total.astype(out.dtype)

    def kernel(me_ref, *refs):
        work(me_ref, refs[:2], refs[-1])

    shape = jax.ShapeDtypeStruct(own.shape, F32 if factor is None else BF16)
    if more:
        return loading("fold", work, (own, got), (VMEM, VMEM), shape, after, me, *more)
    return call("fold", kernel, (me, own, got), (SMEM, VMEM, VMEM), shape, after)


def step(me, chunk, columns, total, shards, after, *more):
    tokens = chunk.shape[0]
    share = columns.shape[1] // shards
    group = max(1, 1024 // share)
    values = [chunk, columns] + ([] if total is None else [total])

    def work(me_ref, refs, out):
        for at in range(0, shards, group):
            sums = jnp.dot(refs[0][...], refs[1][:, at * share:(at + group) * share], preferred_element_type=F32)
            for i in range(group):
                term = sums[:, i * share:(i + 1) * share]
                out[at + i] = term if total is None else refs[2][at + i] + term

    def kernel(*refs):
        work(None, refs, refs[-1])

    shape = jax.ShapeDtypeStruct((shards, tokens, share), F32)
    specs = [VMEM] * len(values)
    if more:
        return loading("step", work, values, specs, shape, after, me, *more)
    return call("step", kernel, values, specs, shape, after)


def product(me, chunk, columns, total, begin, distances, parts, after):
    share = total.shape[2]
    width = share // parts
    group = max(1, min(len(distances), 1024 // share))

    def kernel(me_ref, chunk_ref, columns_ref, total_ref, *refs):
        outs = refs[-parts:]
        for at in range(0, len(distances), group):
            start = (begin + at) * share
            sums = jnp.dot(
                chunk_ref[...], columns_ref[:, start:start + group * share], preferred_element_type=F32
            )
            for i in range(group):
                value = total_ref[distances[at + i] ^ me_ref[0]] + sums[:, i * share:(i + 1) * share]
                for part in range(parts):
                    outs[part][at + i] = value[:, part * width:(part + 1) * width]

    shapes = [jax.ShapeDtypeStruct((len(distances), chunk.shape[0], width), F32)] * parts
    return call("product", kernel, (me, chunk, columns, total), [SMEM] + [VMEM] * 3, shapes, after)


def halve(own, got, distances, plans, after):
    shapes = []
    for rows, _ in plans:
        shapes += [jax.ShapeDtypeStruct((len(distances) // 2, rows[1] - rows[0], own.shape[2]), F32)] * 2

    def kernel(own_ref, got_ref, *refs):
        outs = refs[-len(shapes):]
        for at, ((begin, end), bit) in enumerate(plans):
            for place, d in enumerate(d for d in distances if not d & bit):
                for out, source in ((outs[2 * at], d), (outs[2 * at + 1], d | bit)):
                    i = distances.index(source)
                    out[place] = own_ref[i, begin:end, :] + got_ref[i, begin:end, :]

    return call("halve", kernel, (own, got), (VMEM, VMEM), shapes, after)


def tick(after):
    def kernel(*refs):
        refs[-1][...] = jnp.zeros_like(refs[-1])

    return call("tick", kernel, (), (), jax.ShapeDtypeStruct((8, LANES), F32), after)


def finish(pieces, own, got, tokens, width, parts, after):
    held = [x for _, _, x in pieces[:-1]] if len(pieces) > 1 else []

    def kernel(own_ref, got_ref, *refs):
        out = refs[-1]
        value = (own_ref[0] + got_ref[0]).astype(BF16)
        if not pieces:
            out[...] = value
            return
        for ((begin, end), part, _), ref in zip(pieces, [*refs[:len(held)], None]):
            out[begin:end, part * width:(part + 1) * width] = value if ref is None else ref[...]

    shape = (tokens, width * parts) if pieces else own.shape[1:]
    operands = (own, got, *held)
    return call("finish", kernel, operands, [VMEM] * len(operands), jax.ShapeDtypeStruct(shape, BF16), after)


class Links:
    def __init__(self, bits):
        self.bits = bits
        self.taken = {bit: [] for bit in bits}

    def needs(self, bit, size):
        if bit == self.bits[0]:
            return {bit: size * 8e-6}
        if bit != self.bits[-1]:
            return {bit: size * 80e-6}
        return {bit: size * 160e-6, self.bits[-2]: size * 80e-6}

    def free(self, bit, now):
        share, until = 1.0, float("inf")
        for begin, end, used in self.taken[bit]:
            if begin <= now < end:
                share -= used
            if begin <= now < end or begin > now:
                until = min(until, end if begin <= now else begin)
        return max(share, 0.0), until

    def send(self, bit, size, now):
        needs = self.needs(bit, size)
        now += 1.0
        left = 1.0
        spans = []
        while left > 1e-6:
            shares = [(self.free(link, now), need) for link, need in needs.items()]
            rate = min(share / need for (share, _), need in shares)
            until = min(until for (_, until), _ in shares)
            if rate > 1e-6:
                until = min(until, now + left / rate)
                spans.append((now, until, rate))
                left -= rate * (until - now)
            now = until
        for begin, end, rate in spans:
            for link, need in needs.items():
                self.taken[link].append((begin, end, rate * need))
        return now + 0.3


def body(activations, rotation_small, down_weight):
    shards = lax.axis_size("tensor")
    me = lax.axis_index("tensor").astype(jnp.int32).reshape(1)
    tokens, local = activations.shape
    block = rotation_small.shape[0]
    share = down_weight.shape[1] // shards
    factor = (local // block * shards) ** (-0.5)
    bits = [1 << place for place in range(shards.bit_length() - 1)]
    assert len(bits) >= 3 and shards == 1 << len(bits)
    after = []

    def swap(x, bit):
        return lax.ppermute(x, "tensor", [(d, d ^ bit) for d in range(shards)])

    def ran(outs, link=-1):
        after[:] = [jax.tree.leaves(outs)[link]]
        return outs

    parts = 2 if share % (2 * LANES) == 0 else 1
    width = share // parts
    near = [d for d in range(shards) if not d & bits[0]]
    distances = [d | bits[0] for d in near] + near

    tiles = -(-local // LANES)
    count = min(4, len(bits), tiles)
    edges = [min(local, (tiles * c // count) * LANES) for c in range(count)] + [local]
    spans = list(zip(edges[:-1], edges[1:]))
    chunks = []
    for span in spans:
        chunks.append(ran(mix(activations, rotation_small, (0, tokens), span, after)))
    cycle = bits[-1:] + bits[1:-1] + bits[:1]
    events = sorted((phase, cycle[(phase - c) % len(bits)], c) for phase in range(len(bits)) for c in range(count))
    final = [c for phase, _, c in events if phase == len(bits) - 1]
    loads = [final[i] for i in (PERM if count == len(PERM) else range(count))]
    total = None
    loaded = []
    room = 40 * 2**20

    def wanted():
        nonlocal room
        c = loads[len(loaded)]
        limit = room // 2**20
        room -= (spans[c][1] - spans[c][0]) * down_weight.shape[1] * 2
        return me, down_weight, spans[c], distances if c == final[-1] else (), limit

    for number, (phase, bit, c) in enumerate(events):
        got = swap(chunks[c], bit)
        last = phase == len(bits) - 1
        scale = factor if last else None
        if number == count + 1 and len(loaded) < count - 1:
            chunks[c], columns = ran(fold(me, chunks[c], got, bit, after, scale, *wanted()[1:]), 0)
            loaded.append(columns)
        else:
            chunks[c] = ran(fold(me, chunks[c], got, bit, after, scale))
        while number == 0 and len(loaded) < count - 2:
            loaded.append(ran(load(*wanted(), after), 0)[1])
        if last and c != final[-1]:
            columns = loaded[loads.index(c)]
            if len(loaded) < count:
                total, columns = ran(step(me, chunks[c], columns, total, shards, after, *wanted()[1:]), 0)
                loaded.append(columns)
            else:
                total = ran(step(me, chunks[c], columns, total, shards, after))

    inner = bits[1:]
    late = inner[-1:] + inner[:-1]
    swapped = [inner[1], inner[0]] + inner[2:]
    half = tokens // 2
    routes = [
        [((0, half), inner), ((half, tokens), late)],
        [((0, half), swapped), ((half, tokens), inner)],
    ][:parts]
    links = Links(bits)
    clock = 0.0
    kernels = 0
    pieces = []
    queue = []

    def send(x, bit, use):
        nonlocal clock
        clock += 0.9
        queue.append((links.send(bit, x.size, clock), kernels, swap(x, bit), use))

    def split(part, stage, pieces_of, left, keep, got):
        base = pieces_of[0][0][0]
        plans = [((begin - base, end - base), route[stage]) for (begin, end), route in pieces_of]
        outs = ran(halve(keep, got, left, plans, after))
        for i, (rows, route) in enumerate(pieces_of):
            rest = [d for d in left if not d & route[stage]]
            if stage + 1 < len(inner):
                use = functools.partial(split, part, stage + 1, [(rows, route)], rest, outs[2 * i])
            else:
                use = functools.partial(close, part, rows, outs[2 * i])
            send(outs[2 * i + 1], route[stage], use)

    def close(part, rows, keep, got):
        last = len(pieces) + 1 == parts * len(routes[0])
        held = pieces + [(rows, part, None)] if last else []
        pieces.append((rows, part, ran(finish(held, keep, got, tokens, width, parts, after))))

    last_chunk, last_columns = chunks[final[-1]], loaded[loads.index(final[-1])]
    sends = ran(product(me, last_chunk, last_columns, total, 0, distances[:len(near)], parts, after))
    clock += 0.9
    kernels += 1
    for x in sends:
        send(x, bits[0], None)
    keeps = ran(product(me, last_chunk, last_columns, total, len(near), near, parts, after))
    clock += 0.9
    kernels += 1
    queue[:] = [
        (when, at, got, functools.partial(split, part, 0, routes[part], near, keeps[part]))
        for part, (when, at, got, _) in enumerate(queue)
    ]
    while queue:
        item = min(queue, key=lambda item: item[0])
        queue.remove(item)
        when, at, got, use = item
        if at == kernels:
            ran(tick(after))
            kernels += 1
            clock += 0.1
        clock = max(clock, when) + 0.15
        kernels += 1
        use(got)
    return pieces[-1][2]


def solution(mesh):
    placed = (P("groups", "tensor"), P(), P("tensor", None))
    return jax.shard_map(
        body, mesh=mesh, in_specs=placed, out_specs=P("groups", "tensor"), check_vma=False
    )
```

```python
import functools

import jax
import jax.numpy as jnp
import numpy as np
from jax import lax
from jax.experimental import pallas as pl
from jax.experimental.pallas import tpu as pltpu
from jax.sharding import PartitionSpec as P

LANES = 128
F32 = jnp.float32
BF16 = jnp.bfloat16


PIECES = 4
PERM = (0, 1, 3, 2)


def quotient(index, divisor, limit):
    shift = 16
    scale = -(-(1 << shift) // divisor)
    numbers = np.arange(limit, dtype=np.int64)
    assert np.array_equal((numbers * scale) >> shift, numbers // divisor)
    assert limit * scale < 2**31
    return (index * scale) >> shift


def sign_of(common, count):
    parity = common
    for place in range(1, count):
        parity = parity ^ (common >> place)
    return (1 - 2 * (parity & 1)).astype(F32)


def mix_kernel(rows, start, group, activations, small, *refs):
    out = refs[-1]
    local = activations.shape[1]
    block = small.shape[0]
    tokens, cols = out.shape
    tall = group * block
    span = local // block
    low = group.bit_length() - 1
    high = span.bit_length() - 1 - low
    full = small[...]
    head = full.astype(BF16)
    tail = (full - head.astype(F32)).astype(BF16)

    row = lax.broadcasted_iota(jnp.int32, (tall, block), 0)
    unit = lax.broadcasted_iota(jnp.int32, (tall, block), 1)
    spread_rows = (row - quotient(row, block, tall) * block == unit).astype(F32).astype(BF16)
    col = lax.broadcasted_iota(jnp.int32, (block, cols), 1) + start
    unit = lax.broadcasted_iota(jnp.int32, (block, cols), 0)
    spread_cols = (col - quotient(col, block, local) * block == unit).astype(F32).astype(BF16)
    at_row = quotient(lax.broadcasted_iota(jnp.int32, (tall, cols), 0), block, tall)
    at_col = quotient(lax.broadcasted_iota(jnp.int32, (tall, cols), 1) + start, block, local)
    sign = sign_of(at_row & at_col, max(low, 1))

    def tiled(part):
        rolled = jnp.dot(spread_rows, part, preferred_element_type=F32).astype(BF16)
        return (jnp.dot(rolled, spread_cols, preferred_element_type=F32) * sign).astype(BF16)

    head, tail = tiled(head), tiled(tail)
    owner = quotient(lax.broadcasted_iota(jnp.int32, (8, cols), 1) + start, block, local) >> low
    total = jnp.zeros((tokens, cols), F32)
    for piece in range(span // group):
        values = activations[rows[0]:rows[1], piece * tall:(piece + 1) * tall]
        term = jnp.dot(values, head, preferred_element_type=F32)
        term = term + jnp.dot(values, tail, preferred_element_type=F32)
        total = total + term * sign_of(owner & piece, max(high, 1))[0:1]
    out[...] = total


VMEM = pl.BlockSpec(memory_space=pltpu.VMEM)
SMEM = pl.BlockSpec(memory_space=pltpu.SMEM)
UNREAD = pl.BlockSpec(memory_space=pl.ANY)
COST = pl.CostEstimate(flops=10**10, bytes_accessed=10**8, transcendentals=0)


def call(name, kernel, operands, specs, shapes, after, scratch=(), limit=8):
    return pl.pallas_call(
        kernel,
        out_shape=shapes,
        in_specs=list(specs) + [UNREAD] * len(after),
        out_specs=jax.tree.map(lambda _: VMEM, shapes),
        scratch_shapes=list(scratch),
        cost_estimate=COST,
        compiler_params=pltpu.CompilerParams(vmem_limit_bytes=limit * 2**20),
        name=name,
    )(*operands, *after)


def mix(activations, small, rows, cols, after):
    block = small.shape[0]
    group = min(4, activations.shape[1] // block)
    kernel = functools.partial(mix_kernel, rows, cols[0], group)
    shape = jax.ShapeDtypeStruct((rows[1] - rows[0], cols[1] - cols[0]), F32)
    return call("mix", kernel, (activations, small), (VMEM, VMEM), shape, after)


def fetch(me, weight, out, sems, rows, distances):
    begin, end = rows
    copies = []
    if not distances:
        each = (end - begin) // PIECES // 16 * 16
        for i in range(PIECES):
            low, high = i * each, (i + 1) * each if i + 1 < PIECES else end - begin
            copies.append(
                pltpu.make_async_copy(weight.at[begin + low:begin + high, :], out.at[low:high, :], sems.at[i])
            )
    for i, distance in enumerate(distances):
        share = weight.shape[1] // len(distances)
        column = pl.multiple_of((distance ^ me) * share, LANES)
        copies.append(
            pltpu.make_async_copy(
                weight.at[begin:end, pl.ds(column, share)], out.at[:, pl.ds(i * share, share)], sems.at[i]
            )
        )
    for copy in copies:
        copy.start()
    return copies


def loading(name, work, operands, specs, shape, after, me, weight, rows, distances, limit):
    count = len(operands)

    def kernel(me_ref, weight_ref, *refs):
        columns, out, sems = refs[-3:]
        copies = fetch(me_ref[0], weight_ref, columns, sems, rows, distances)
        work(me_ref, refs[:count], out)
        for copy in copies:
            copy.wait()

    columns = jax.ShapeDtypeStruct((rows[1] - rows[0], weight.shape[1]), BF16)
    outs = call(
        name,
        kernel,
        (me, weight, *operands),
        [SMEM, pl.BlockSpec(memory_space=pltpu.HBM), *specs],
        [columns, shape],
        after,
        [pltpu.SemaphoreType.DMA((max(PIECES, len(distances)),))],
        limit,
    )
    return outs[1], outs[0]


def load(me, weight, rows, distances, limit, after):
    def work(me_ref, refs, out):
        out[...] = jnp.zeros_like(out)

    shape = jax.ShapeDtypeStruct((8, LANES), F32)
    return loading("load", work, (), (), shape, after, me, weight, rows, distances, limit)


def fold(me, own, got, bit, after, factor=None, *more):
    def work(me_ref, refs, out):
        own_ref, got_ref = refs
        sign = jnp.where((me_ref[0] & bit) != 0, -1.0, 1.0).astype(F32)
        total = got_ref[...] + own_ref[...] * sign
        if factor is not None:
            total = total * factor
        out[...] = total.astype(out.dtype)

    def kernel(me_ref, *refs):
        work(me_ref, refs[:2], refs[-1])

    shape = jax.ShapeDtypeStruct(own.shape, F32 if factor is None else BF16)
    if more:
        return loading("fold", work, (own, got), (VMEM, VMEM), shape, after, me, *more)
    return call("fold", kernel, (me, own, got), (SMEM, VMEM, VMEM), shape, after)


def step(me, chunk, columns, total, shards, after, *more):
    tokens = chunk.shape[0]
    share = columns.shape[1] // shards
    group = max(1, 1024 // share)
    values = [chunk, columns] + ([] if total is None else [total])

    def work(me_ref, refs, out):
        for at in range(0, shards, group):
            sums = jnp.dot(refs[0][...], refs[1][:, at * share:(at + group) * share], preferred_element_type=F32)
            for i in range(group):
                term = sums[:, i * share:(i + 1) * share]
                out[at + i] = term if total is None else refs[2][at + i] + term

    def kernel(*refs):
        work(None, refs, refs[-1])

    shape = jax.ShapeDtypeStruct((shards, tokens, share), F32)
    specs = [VMEM] * len(values)
    if more:
        return loading("step", work, values, specs, shape, after, me, *more)
    return call("step", kernel, values, specs, shape, after)


def product(me, chunk, columns, total, begin, distances, parts, after):
    share = total.shape[2]
    width = share // parts
    group = max(1, min(len(distances), 1024 // share))

    def kernel(me_ref, chunk_ref, columns_ref, total_ref, *refs):
        outs = refs[-parts:]
        for at in range(0, len(distances), group):
            start = (begin + at) * share
            sums = jnp.dot(
                chunk_ref[...], columns_ref[:, start:start + group * share], preferred_element_type=F32
            )
            for i in range(group):
                value = total_ref[distances[at + i] ^ me_ref[0]] + sums[:, i * share:(i + 1) * share]
                for part in range(parts):
                    outs[part][at + i] = value[:, part * width:(part + 1) * width]

    shapes = [jax.ShapeDtypeStruct((len(distances), chunk.shape[0], width), F32)] * parts
    return call("product", kernel, (me, chunk, columns, total), [SMEM] + [VMEM] * 3, shapes, after)


def halve(own, got, distances, plans, after):
    shapes = []
    for rows, _ in plans:
        shapes += [jax.ShapeDtypeStruct((len(distances) // 2, rows[1] - rows[0], own.shape[2]), F32)] * 2

    def kernel(own_ref, got_ref, *refs):
        outs = refs[-len(shapes):]
        for at, ((begin, end), bit) in enumerate(plans):
            for place, d in enumerate(d for d in distances if not d & bit):
                for out, source in ((outs[2 * at], d), (outs[2 * at + 1], d | bit)):
                    i = distances.index(source)
                    out[place] = own_ref[i, begin:end, :] + got_ref[i, begin:end, :]

    return call("halve", kernel, (own, got), (VMEM, VMEM), shapes, after)


def tick(after):
    def kernel(*refs):
        refs[-1][...] = jnp.zeros_like(refs[-1])

    return call("tick", kernel, (), (), jax.ShapeDtypeStruct((8, LANES), F32), after)


def finish(pieces, own, got, tokens, width, parts, after):
    held = [x for _, _, x in pieces[:-1]] if len(pieces) > 1 else []

    def kernel(own_ref, got_ref, *refs):
        out = refs[-1]
        value = (own_ref[0] + got_ref[0]).astype(BF16)
        if not pieces:
            out[...] = value
            return
        for ((begin, end), part, _), ref in zip(pieces, [*refs[:len(held)], None]):
            out[begin:end, part * width:(part + 1) * width] = value if ref is None else ref[...]

    shape = (tokens, width * parts) if pieces else own.shape[1:]
    operands = (own, got, *held)
    return call("finish", kernel, operands, [VMEM] * len(operands), jax.ShapeDtypeStruct(shape, BF16), after)


class Links:
    def __init__(self, bits):
        self.bits = bits
        self.taken = {bit: [] for bit in bits}

    def needs(self, bit, size):
        if bit == self.bits[0]:
            return {bit: size * 8e-6}
        if bit != self.bits[-1]:
            return {bit: size * 80e-6}
        return {bit: size * 160e-6, self.bits[-2]: size * 80e-6}

    def free(self, bit, now):
        share, until = 1.0, float("inf")
        for begin, end, used in self.taken[bit]:
            if begin <= now < end:
                share -= used
            if begin <= now < end or begin > now:
                until = min(until, end if begin <= now else begin)
        return max(share, 0.0), until

    def send(self, bit, size, now):
        needs = self.needs(bit, size)
        now += 1.0
        left = 1.0
        spans = []
        while left > 1e-6:
            shares = [(self.free(link, now), need) for link, need in needs.items()]
            rate = min(share / need for (share, _), need in shares)
            until = min(until for (_, until), _ in shares)
            if rate > 1e-6:
                until = min(until, now + left / rate)
                spans.append((now, until, rate))
                left -= rate * (until - now)
            now = until
        for begin, end, rate in spans:
            for link, need in needs.items():
                self.taken[link].append((begin, end, rate * need))
        return now + 0.3


def body(activations, rotation_small, down_weight):
    shards = lax.axis_size("tensor")
    me = lax.axis_index("tensor").astype(jnp.int32).reshape(1)
    tokens, local = activations.shape
    block = rotation_small.shape[0]
    share = down_weight.shape[1] // shards
    factor = (local // block * shards) ** (-0.5)
    bits = [1 << place for place in range(shards.bit_length() - 1)]
    assert len(bits) >= 3 and shards == 1 << len(bits)
    after = []

    def swap(x, bit):
        return lax.ppermute(x, "tensor", [(d, d ^ bit) for d in range(shards)])

    def ran(outs, link=-1):
        after[:] = [jax.tree.leaves(outs)[link]]
        return outs

    parts = 2 if share % (2 * LANES) == 0 else 1
    width = share // parts
    near = [d for d in range(shards) if not d & bits[0]]
    distances = [d | bits[0] for d in near] + near

    tiles = -(-local // LANES)
    count = min(4, len(bits), tiles)
    edges = [min(local, (tiles * c // count) * LANES) for c in range(count)] + [local]
    spans = list(zip(edges[:-1], edges[1:]))
    chunks = []
    for span in spans:
        chunks.append(ran(mix(activations, rotation_small, (0, tokens), span, after)))
    cycle = bits[-1:] + bits[1:-1] + bits[:1]
    events = sorted((phase, cycle[(phase - c) % len(bits)], c) for phase in range(len(bits)) for c in range(count))
    final = [c for phase, _, c in events if phase == len(bits) - 1]
    loads = [final[i] for i in (PERM if count == len(PERM) else range(count))]
    total = None
    loaded = []
    room = 37 * 2**20

    def wanted():
        nonlocal room
        c = loads[len(loaded)]
        limit = room // 2**20 + (0 if loaded else 3)
        room -= (spans[c][1] - spans[c][0]) * down_weight.shape[1] * 2
        return me, down_weight, spans[c], distances if c == final[-1] else (), limit

    for number, (phase, bit, c) in enumerate(events):
        got = swap(chunks[c], bit)
        last = phase == len(bits) - 1
        scale = factor if last else None
        if number == count + 1 and len(loaded) < count - 1:
            chunks[c], columns = ran(fold(me, chunks[c], got, bit, after, scale, *wanted()[1:]), 0)
            loaded.append(columns)
        else:
            chunks[c] = ran(fold(me, chunks[c], got, bit, after, scale))
        while number == 0 and len(loaded) < count - 2:
            loaded.append(ran(load(*wanted(), after), 0)[1])
        if last and c != final[-1]:
            columns = loaded[loads.index(c)]
            if len(loaded) < count:
                total, columns = ran(step(me, chunks[c], columns, total, shards, after, *wanted()[1:]), 0)
                loaded.append(columns)
            else:
                total = ran(step(me, chunks[c], columns, total, shards, after))

    inner = bits[1:]
    late = inner[-1:] + inner[:-1]
    swapped = [inner[1], inner[0]] + inner[2:]
    half = tokens // 2
    routes = [
        [((0, half), inner), ((half, tokens), late)],
        [((0, half), swapped), ((half, tokens), inner)],
    ][:parts]
    links = Links(bits)
    clock = 0.0
    kernels = 0
    pieces = []
    queue = []

    def send(x, bit, use):
        nonlocal clock
        clock += 0.9
        queue.append((links.send(bit, x.size, clock), kernels, swap(x, bit), use))

    def split(part, stage, pieces_of, left, keep, got):
        base = pieces_of[0][0][0]
        plans = [((begin - base, end - base), route[stage]) for (begin, end), route in pieces_of]
        outs = ran(halve(keep, got, left, plans, after))
        for i, (rows, route) in enumerate(pieces_of):
            rest = [d for d in left if not d & route[stage]]
            if stage + 1 < len(inner):
                use = functools.partial(split, part, stage + 1, [(rows, route)], rest, outs[2 * i])
            else:
                use = functools.partial(close, part, rows, outs[2 * i])
            send(outs[2 * i + 1], route[stage], use)

    def close(part, rows, keep, got):
        last = len(pieces) + 1 == parts * len(routes[0])
        held = pieces + [(rows, part, None)] if last else []
        pieces.append((rows, part, ran(finish(held, keep, got, tokens, width, parts, after))))

    last_chunk, last_columns = chunks[final[-1]], loaded[loads.index(final[-1])]
    sends = ran(product(me, last_chunk, last_columns, total, 0, distances[:len(near)], parts, after))
    clock += 0.9
    kernels += 1
    for x in sends:
        send(x, bits[0], None)
    keeps = ran(product(me, last_chunk, last_columns, total, len(near), near, parts, after))
    clock += 0.9
    kernels += 1
    queue[:] = [
        (when, at, got, functools.partial(split, part, 0, routes[part], near, keeps[part]))
        for part, (when, at, got, _) in enumerate(queue)
    ]
    while queue:
        item = min(queue, key=lambda item: item[0])
        queue.remove(item)
        when, at, got, use = item
        if at == kernels:
            ran(tick(after))
            kernels += 1
            clock += 0.1
        clock = max(clock, when) + 0.15
        kernels += 1
        use(got)
    return pieces[-1][2]


def solution(mesh):
    placed = (P("groups", "tensor"), P(), P("tensor", None))
    return jax.shard_map(
        body, mesh=mesh, in_specs=placed, out_specs=P("groups", "tensor"), check_vma=False
    )
```

```python
import functools

import jax
import jax.numpy as jnp
import numpy as np
from jax import lax
from jax.experimental import pallas as pl
from jax.experimental.pallas import tpu as pltpu
from jax.sharding import PartitionSpec as P

LANES = 128
F32 = jnp.float32
BF16 = jnp.bfloat16


TILES = (4, 3, 3, 3)
PIECES = 4
PERM = (0, 1, 3, 2)


def quotient(index, divisor, limit):
    shift = 16
    scale = -(-(1 << shift) // divisor)
    numbers = np.arange(limit, dtype=np.int64)
    assert np.array_equal((numbers * scale) >> shift, numbers // divisor)
    assert limit * scale < 2**31
    return (index * scale) >> shift


def sign_of(common, count):
    parity = common
    for place in range(1, count):
        parity = parity ^ (common >> place)
    return (1 - 2 * (parity & 1)).astype(F32)


def mix_kernel(rows, start, group, activations, small, *refs):
    out = refs[-1]
    local = activations.shape[1]
    block = small.shape[0]
    tokens, cols = out.shape
    tall = group * block
    span = local // block
    low = group.bit_length() - 1
    high = span.bit_length() - 1 - low
    full = small[...]
    head = full.astype(BF16)
    tail = (full - head.astype(F32)).astype(BF16)

    row = lax.broadcasted_iota(jnp.int32, (tall, block), 0)
    unit = lax.broadcasted_iota(jnp.int32, (tall, block), 1)
    spread_rows = (row - quotient(row, block, tall) * block == unit).astype(F32).astype(BF16)
    col = lax.broadcasted_iota(jnp.int32, (block, cols), 1) + start
    unit = lax.broadcasted_iota(jnp.int32, (block, cols), 0)
    spread_cols = (col - quotient(col, block, local) * block == unit).astype(F32).astype(BF16)
    at_row = quotient(lax.broadcasted_iota(jnp.int32, (tall, cols), 0), block, tall)
    at_col = quotient(lax.broadcasted_iota(jnp.int32, (tall, cols), 1) + start, block, local)
    sign = sign_of(at_row & at_col, max(low, 1))

    def tiled(part):
        rolled = jnp.dot(spread_rows, part, preferred_element_type=F32).astype(BF16)
        return (jnp.dot(rolled, spread_cols, preferred_element_type=F32) * sign).astype(BF16)

    head, tail = tiled(head), tiled(tail)
    owner = quotient(lax.broadcasted_iota(jnp.int32, (8, cols), 1) + start, block, local) >> low
    total = jnp.zeros((tokens, cols), F32)
    for piece in range(span // group):
        values = activations[rows[0]:rows[1], piece * tall:(piece + 1) * tall]
        term = jnp.dot(values, head, preferred_element_type=F32)
        term = term + jnp.dot(values, tail, preferred_element_type=F32)
        total = total + term * sign_of(owner & piece, max(high, 1))[0:1]
    out[...] = total


VMEM = pl.BlockSpec(memory_space=pltpu.VMEM)
SMEM = pl.BlockSpec(memory_space=pltpu.SMEM)
UNREAD = pl.BlockSpec(memory_space=pl.ANY)
COST = pl.CostEstimate(flops=10**10, bytes_accessed=10**8, transcendentals=0)


def call(name, kernel, operands, specs, shapes, after, scratch=(), limit=8):
    return pl.pallas_call(
        kernel,
        out_shape=shapes,
        in_specs=list(specs) + [UNREAD] * len(after),
        out_specs=jax.tree.map(lambda _: VMEM, shapes),
        scratch_shapes=list(scratch),
        cost_estimate=COST,
        compiler_params=pltpu.CompilerParams(vmem_limit_bytes=limit * 2**20),
        name=name,
    )(*operands, *after)


def mix(activations, small, rows, cols, after):
    block = small.shape[0]
    group = min(4, activations.shape[1] // block)
    kernel = functools.partial(mix_kernel, rows, cols[0], group)
    shape = jax.ShapeDtypeStruct((rows[1] - rows[0], cols[1] - cols[0]), F32)
    return call("mix", kernel, (activations, small), (VMEM, VMEM), shape, after)


def fetch(me, weight, out, sems, rows, distances):
    begin, end = rows
    copies = []
    if not distances:
        each = (end - begin) // PIECES // 16 * 16
        for i in range(PIECES):
            low, high = i * each, (i + 1) * each if i + 1 < PIECES else end - begin
            copies.append(
                pltpu.make_async_copy(weight.at[begin + low:begin + high, :], out.at[low:high, :], sems.at[i])
            )
    for i, distance in enumerate(distances):
        share = weight.shape[1] // len(distances)
        column = pl.multiple_of((distance ^ me) * share, LANES)
        copies.append(
            pltpu.make_async_copy(
                weight.at[begin:end, pl.ds(column, share)], out.at[:, pl.ds(i * share, share)], sems.at[i]
            )
        )
    for copy in copies:
        copy.start()
    return copies


def loading(name, work, operands, specs, shape, after, me, weight, rows, distances, limit):
    count = len(operands)

    def kernel(me_ref, weight_ref, *refs):
        columns, out, sems = refs[-3:]
        copies = fetch(me_ref[0], weight_ref, columns, sems, rows, distances)
        work(me_ref, refs[:count], out)
        for copy in copies:
            copy.wait()

    columns = jax.ShapeDtypeStruct((rows[1] - rows[0], weight.shape[1]), BF16)
    outs = call(
        name,
        kernel,
        (me, weight, *operands),
        [SMEM, pl.BlockSpec(memory_space=pltpu.HBM), *specs],
        [columns, shape],
        after,
        [pltpu.SemaphoreType.DMA((max(PIECES, len(distances)),))],
        limit,
    )
    return outs[1], outs[0]


def load(me, weight, rows, distances, limit, after):
    def work(me_ref, refs, out):
        out[...] = jnp.zeros_like(out)

    shape = jax.ShapeDtypeStruct((8, LANES), F32)
    return loading("load", work, (), (), shape, after, me, weight, rows, distances, limit)


def fold(me, own, got, bit, after, factor=None, *more):
    def work(me_ref, refs, out):
        own_ref, got_ref = refs
        sign = jnp.where((me_ref[0] & bit) != 0, -1.0, 1.0).astype(F32)
        total = got_ref[...] + own_ref[...] * sign
        if factor is not None:
            total = total * factor
        out[...] = total.astype(out.dtype)

    def kernel(me_ref, *refs):
        work(me_ref, refs[:2], refs[-1])

    shape = jax.ShapeDtypeStruct(own.shape, F32 if factor is None else BF16)
    if more:
        return loading("fold", work, (own, got), (VMEM, VMEM), shape, after, me, *more)
    return call("fold", kernel, (me, own, got), (SMEM, VMEM, VMEM), shape, after)


def step(me, chunk, columns, total, shards, after, *more):
    tokens = chunk.shape[0]
    share = columns.shape[1] // shards
    group = max(1, 1024 // share)
    values = [chunk, columns] + ([] if total is None else [total])

    def work(me_ref, refs, out):
        for at in range(0, shards, group):
            sums = jnp.dot(refs[0][...], refs[1][:, at * share:(at + group) * share], preferred_element_type=F32)
            for i in range(group):
                term = sums[:, i * share:(i + 1) * share]
                out[at + i] = term if total is None else refs[2][at + i] + term

    def kernel(*refs):
        work(None, refs, refs[-1])

    shape = jax.ShapeDtypeStruct((shards, tokens, share), F32)
    specs = [VMEM] * len(values)
    if more:
        return loading("step", work, values, specs, shape, after, me, *more)
    return call("step", kernel, values, specs, shape, after)


def product(me, chunk, columns, total, begin, distances, parts, after):
    share = total.shape[2]
    width = share // parts
    group = max(1, min(len(distances), 1024 // share))

    def kernel(me_ref, chunk_ref, columns_ref, total_ref, *refs):
        outs = refs[-parts:]
        for at in range(0, len(distances), group):
            start = (begin + at) * share
            sums = jnp.dot(
                chunk_ref[...], columns_ref[:, start:start + group * share], preferred_element_type=F32
            )
            for i in range(group):
                value = total_ref[distances[at + i] ^ me_ref[0]] + sums[:, i * share:(i + 1) * share]
                for part in range(parts):
                    outs[part][at + i] = value[:, part * width:(part + 1) * width]

    shapes = [jax.ShapeDtypeStruct((len(distances), chunk.shape[0], width), F32)] * parts
    return call("product", kernel, (me, chunk, columns, total), [SMEM] + [VMEM] * 3, shapes, after)


def halve(own, got, distances, plans, after):
    shapes = []
    for rows, _ in plans:
        shapes += [jax.ShapeDtypeStruct((len(distances) // 2, rows[1] - rows[0], own.shape[2]), F32)] * 2

    def kernel(own_ref, got_ref, *refs):
        outs = refs[-len(shapes):]
        for at, ((begin, end), bit) in enumerate(plans):
            for place, d in enumerate(d for d in distances if not d & bit):
                for out, source in ((outs[2 * at], d), (outs[2 * at + 1], d | bit)):
                    i = distances.index(source)
                    out[place] = own_ref[i, begin:end, :] + got_ref[i, begin:end, :]

    return call("halve", kernel, (own, got), (VMEM, VMEM), shapes, after)


def tick(after):
    def kernel(*refs):
        refs[-1][...] = jnp.zeros_like(refs[-1])

    return call("tick", kernel, (), (), jax.ShapeDtypeStruct((8, LANES), F32), after)


def finish(pieces, own, got, tokens, width, parts, after):
    held = [x for _, _, x in pieces[:-1]] if len(pieces) > 1 else []

    def kernel(own_ref, got_ref, *refs):
        out = refs[-1]
        value = (own_ref[0] + got_ref[0]).astype(BF16)
        if not pieces:
            out[...] = value
            return
        for ((begin, end), part, _), ref in zip(pieces, [*refs[:len(held)], None]):
            out[begin:end, part * width:(part + 1) * width] = value if ref is None else ref[...]

    shape = (tokens, width * parts) if pieces else own.shape[1:]
    operands = (own, got, *held)
    return call("finish", kernel, operands, [VMEM] * len(operands), jax.ShapeDtypeStruct(shape, BF16), after)


class Links:
    def __init__(self, bits):
        self.bits = bits
        self.taken = {bit: [] for bit in bits}

    def needs(self, bit, size):
        if bit == self.bits[0]:
            return {bit: size * 8e-6}
        if bit != self.bits[-1]:
            return {bit: size * 80e-6}
        return {bit: size * 160e-6, self.bits[-2]: size * 80e-6}

    def free(self, bit, now):
        share, until = 1.0, float("inf")
        for begin, end, used in self.taken[bit]:
            if begin <= now < end:
                share -= used
            if begin <= now < end or begin > now:
                until = min(until, end if begin <= now else begin)
        return max(share, 0.0), until

    def send(self, bit, size, now):
        needs = self.needs(bit, size)
        now += 1.0
        left = 1.0
        spans = []
        while left > 1e-6:
            shares = [(self.free(link, now), need) for link, need in needs.items()]
            rate = min(share / need for (share, _), need in shares)
            until = min(until for (_, until), _ in shares)
            if rate > 1e-6:
                until = min(until, now + left / rate)
                spans.append((now, until, rate))
                left -= rate * (until - now)
            now = until
        for begin, end, rate in spans:
            for link, need in needs.items():
                self.taken[link].append((begin, end, rate * need))
        return now + 0.3


def body(activations, rotation_small, down_weight):
    shards = lax.axis_size("tensor")
    me = lax.axis_index("tensor").astype(jnp.int32).reshape(1)
    tokens, local = activations.shape
    block = rotation_small.shape[0]
    share = down_weight.shape[1] // shards
    factor = (local // block * shards) ** (-0.5)
    bits = [1 << place for place in range(shards.bit_length() - 1)]
    assert len(bits) >= 3 and shards == 1 << len(bits)
    after = []

    def swap(x, bit):
        return lax.ppermute(x, "tensor", [(d, d ^ bit) for d in range(shards)])

    def ran(outs, link=-1):
        after[:] = [jax.tree.leaves(outs)[link]]
        return outs

    parts = 2 if share % (2 * LANES) == 0 else 1
    width = share // parts
    near = [d for d in range(shards) if not d & bits[0]]
    distances = [d | bits[0] for d in near] + near

    tiles = -(-local // LANES)
    count = len(TILES)
    edges = [min(local, round(tiles * sum(TILES[:c]) / sum(TILES)) * LANES) for c in range(count + 1)]
    assert all(begin < end for begin, end in zip(edges[:-1], edges[1:]))
    spans = list(zip(edges[:-1], edges[1:]))
    chunks = []
    for span in spans:
        chunks.append(ran(mix(activations, rotation_small, (0, tokens), span, after)))
    cycle = bits[:0:-1] + bits[:1]
    rank = {bit: place for place, bit in enumerate(bits[:-2] + bits[:-3:-1])}
    events = [(phase, cycle[(phase - c) % len(bits)], c) for phase in range(len(bits)) for c in range(count)]
    events.sort(key=lambda event: (event[0], rank[event[1]]))
    final = [c for phase, _, c in events if phase == len(bits) - 1]
    loads = [final[i] for i in (PERM if count == len(PERM) else range(count))]
    total = None
    loaded = []
    room = 37 * 2**20

    def wanted():
        nonlocal room
        c = loads[len(loaded)]
        limit = room // 2**20 + (0 if loaded else 3)
        room -= (spans[c][1] - spans[c][0]) * down_weight.shape[1] * 2
        return me, down_weight, spans[c], distances if c == final[-1] else (), limit

    for number, (phase, bit, c) in enumerate(events):
        got = swap(chunks[c], bit)
        last = phase == len(bits) - 1
        scale = factor if last else None
        if number == count + 1 and len(loaded) < count - 1:
            chunks[c], columns = ran(fold(me, chunks[c], got, bit, after, scale, *wanted()[1:]), 0)
            loaded.append(columns)
        else:
            chunks[c] = ran(fold(me, chunks[c], got, bit, after, scale))
        while number == 0 and len(loaded) < count - 2:
            loaded.append(ran(load(*wanted(), after), 0)[1])
        if last and c != final[-1]:
            columns = loaded[loads.index(c)]
            if len(loaded) < count:
                total, columns = ran(step(me, chunks[c], columns, total, shards, after, *wanted()[1:]), 0)
                loaded.append(columns)
            else:
                total = ran(step(me, chunks[c], columns, total, shards, after))

    inner = bits[1:]
    late = inner[-1:] + inner[:-1]
    swapped = [inner[1], inner[0]] + inner[2:]
    half = tokens // 2
    routes = [
        [((0, half), inner), ((half, tokens), late)],
        [((0, half), swapped), ((half, tokens), inner)],
    ][:parts]
    links = Links(bits)
    clock = 0.0
    kernels = 0
    pieces = []
    queue = []

    def send(x, bit, use):
        nonlocal clock
        clock += 0.9
        queue.append((links.send(bit, x.size, clock), kernels, swap(x, bit), use))

    def split(part, stage, pieces_of, left, keep, got):
        base = pieces_of[0][0][0]
        plans = [((begin - base, end - base), route[stage]) for (begin, end), route in pieces_of]
        outs = ran(halve(keep, got, left, plans, after))
        for i, (rows, route) in enumerate(pieces_of):
            rest = [d for d in left if not d & route[stage]]
            if stage + 1 < len(inner):
                use = functools.partial(split, part, stage + 1, [(rows, route)], rest, outs[2 * i])
            else:
                use = functools.partial(close, part, rows, outs[2 * i])
            send(outs[2 * i + 1], route[stage], use)

    def close(part, rows, keep, got):
        last = len(pieces) + 1 == parts * len(routes[0])
        held = pieces + [(rows, part, None)] if last else []
        pieces.append((rows, part, ran(finish(held, keep, got, tokens, width, parts, after))))

    last_chunk, last_columns = chunks[final[-1]], loaded[loads.index(final[-1])]
    sends = ran(product(me, last_chunk, last_columns, total, 0, distances[:len(near)], parts, after))
    clock += 0.9
    kernels += 1
    for x in sends:
        send(x, bits[0], None)
    keeps = ran(product(me, last_chunk, last_columns, total, len(near), near, parts, after))
    clock += 0.9
    kernels += 1
    queue[:] = [
        (when, at, got, functools.partial(split, part, 0, routes[part], near, keeps[part]))
        for part, (when, at, got, _) in enumerate(queue)
    ]
    while queue:
        item = min(queue, key=lambda item: item[0])
        queue.remove(item)
        when, at, got, use = item
        if at == kernels:
            ran(tick(after))
            kernels += 1
            clock += 0.1
        clock = max(clock, when) + 0.15
        kernels += 1
        use(got)
    return pieces[-1][2]


def solution(mesh):
    placed = (P("groups", "tensor"), P(), P("tensor", None))
    return jax.shard_map(
        body, mesh=mesh, in_specs=placed, out_specs=P("groups", "tensor"), check_vma=False
    )
```

```python
import functools

import jax
import jax.numpy as jnp
import numpy as np
from jax import lax
from jax.experimental import pallas as pl
from jax.experimental.pallas import tpu as pltpu
from jax.sharding import PartitionSpec as P

LANES = 128
F32 = jnp.float32
BF16 = jnp.bfloat16


TILES = (4, 3, 3, 3)
PIECES = 4
PERM = (0, 1, 3, 2)


def quotient(index, divisor, limit):
    shift = 16
    scale = -(-(1 << shift) // divisor)
    numbers = np.arange(limit, dtype=np.int64)
    assert np.array_equal((numbers * scale) >> shift, numbers // divisor)
    assert limit * scale < 2**31
    return (index * scale) >> shift


def sign_of(common, count):
    parity = common
    for place in range(1, count):
        parity = parity ^ (common >> place)
    return (1 - 2 * (parity & 1)).astype(F32)


def mix_kernel(rows, start, group, activations, small, *refs):
    out = refs[-1]
    local = activations.shape[1]
    block = small.shape[0]
    tokens, cols = out.shape
    tall = group * block
    span = local // block
    low = group.bit_length() - 1
    high = span.bit_length() - 1 - low
    full = small[...]
    head = full.astype(BF16)
    tail = (full - head.astype(F32)).astype(BF16)

    row = lax.broadcasted_iota(jnp.int32, (tall, block), 0)
    unit = lax.broadcasted_iota(jnp.int32, (tall, block), 1)
    spread_rows = (row - quotient(row, block, tall) * block == unit).astype(F32).astype(BF16)
    col = lax.broadcasted_iota(jnp.int32, (block, cols), 1) + start
    unit = lax.broadcasted_iota(jnp.int32, (block, cols), 0)
    spread_cols = (col - quotient(col, block, local) * block == unit).astype(F32).astype(BF16)
    at_row = quotient(lax.broadcasted_iota(jnp.int32, (tall, cols), 0), block, tall)
    at_col = quotient(lax.broadcasted_iota(jnp.int32, (tall, cols), 1) + start, block, local)
    sign = sign_of(at_row & at_col, max(low, 1))

    def tiled(part):
        rolled = jnp.dot(spread_rows, part, preferred_element_type=F32).astype(BF16)
        return (jnp.dot(rolled, spread_cols, preferred_element_type=F32) * sign).astype(BF16)

    head, tail = tiled(head), tiled(tail)
    owner = quotient(lax.broadcasted_iota(jnp.int32, (8, cols), 1) + start, block, local) >> low
    total = jnp.zeros((tokens, cols), F32)
    for piece in range(span // group):
        values = activations[rows[0]:rows[1], piece * tall:(piece + 1) * tall]
        term = jnp.dot(values, head, preferred_element_type=F32)
        term = term + jnp.dot(values, tail, preferred_element_type=F32)
        total = total + term * sign_of(owner & piece, max(high, 1))[0:1]
    out[...] = total


VMEM = pl.BlockSpec(memory_space=pltpu.VMEM)
SMEM = pl.BlockSpec(memory_space=pltpu.SMEM)
UNREAD = pl.BlockSpec(memory_space=pl.ANY)
COST = pl.CostEstimate(flops=10**10, bytes_accessed=10**8, transcendentals=0)


def call(name, kernel, operands, specs, shapes, after, scratch=(), limit=8):
    return pl.pallas_call(
        kernel,
        out_shape=shapes,
        in_specs=list(specs) + [UNREAD] * len(after),
        out_specs=jax.tree.map(lambda _: VMEM, shapes),
        scratch_shapes=list(scratch),
        cost_estimate=COST,
        compiler_params=pltpu.CompilerParams(vmem_limit_bytes=limit * 2**20),
        name=name,
    )(*operands, *after)


def mix(activations, small, rows, cols, after):
    block = small.shape[0]
    group = min(4, activations.shape[1] // block)
    kernel = functools.partial(mix_kernel, rows, cols[0], group)
    shape = jax.ShapeDtypeStruct((rows[1] - rows[0], cols[1] - cols[0]), F32)
    return call("mix", kernel, (activations, small), (VMEM, VMEM), shape, after)


def fetch(me, weight, out, sems, rows, distances):
    begin, end = rows
    copies = []
    if not distances:
        each = (end - begin) // PIECES // 16 * 16
        for i in range(PIECES):
            low, high = i * each, (i + 1) * each if i + 1 < PIECES else end - begin
            copies.append(
                pltpu.make_async_copy(weight.at[begin + low:begin + high, :], out.at[low:high, :], sems.at[i])
            )
    for i, distance in enumerate(distances):
        share = weight.shape[1] // len(distances)
        column = pl.multiple_of((distance ^ me) * share, LANES)
        copies.append(
            pltpu.make_async_copy(
                weight.at[begin:end, pl.ds(column, share)], out.at[:, pl.ds(i * share, share)], sems.at[i]
            )
        )
    for copy in copies:
        copy.start()
    return copies


def loading(name, work, operands, specs, shape, after, me, weight, rows, distances, limit):
    count = len(operands)

    def kernel(me_ref, weight_ref, *refs):
        columns, out, sems = refs[-3:]
        copies = fetch(me_ref[0], weight_ref, columns, sems, rows, distances)
        work(me_ref, refs[:count], out)
        for copy in copies:
            copy.wait()

    columns = jax.ShapeDtypeStruct((rows[1] - rows[0], weight.shape[1]), BF16)
    outs = call(
        name,
        kernel,
        (me, weight, *operands),
        [SMEM, pl.BlockSpec(memory_space=pltpu.HBM), *specs],
        [columns, shape],
        after,
        [pltpu.SemaphoreType.DMA((max(PIECES, len(distances)),))],
        limit,
    )
    return outs[1], outs[0]


def load(me, weight, rows, distances, limit, after):
    def work(me_ref, refs, out):
        out[...] = jnp.zeros_like(out)

    shape = jax.ShapeDtypeStruct((8, LANES), F32)
    return loading("load", work, (), (), shape, after, me, weight, rows, distances, limit)


def fold(me, own, got, bit, after, factor=None, *more):
    def work(me_ref, refs, out):
        own_ref, got_ref = refs
        sign = jnp.where((me_ref[0] & bit) != 0, -1.0, 1.0).astype(F32)
        total = got_ref[...] + own_ref[...] * sign
        if factor is not None:
            total = total * factor
        out[...] = total.astype(out.dtype)

    def kernel(me_ref, *refs):
        work(me_ref, refs[:2], refs[-1])

    shape = jax.ShapeDtypeStruct(own.shape, F32 if factor is None else BF16)
    if more:
        return loading("fold", work, (own, got), (VMEM, VMEM), shape, after, me, *more)
    return call("fold", kernel, (me, own, got), (SMEM, VMEM, VMEM), shape, after)


def step(me, chunk, columns, total, shards, after, *more):
    tokens = chunk.shape[0]
    share = columns.shape[1] // shards
    group = max(1, 1024 // share)
    values = [chunk, columns] + ([] if total is None else [total])

    def work(me_ref, refs, out):
        for at in range(0, shards, group):
            sums = jnp.dot(refs[0][...], refs[1][:, at * share:(at + group) * share], preferred_element_type=F32)
            for i in range(group):
                term = sums[:, i * share:(i + 1) * share]
                out[at + i] = term if total is None else refs[2][at + i] + term

    def kernel(*refs):
        work(None, refs, refs[-1])

    shape = jax.ShapeDtypeStruct((shards, tokens, share), F32)
    specs = [VMEM] * len(values)
    if more:
        return loading("step", work, values, specs, shape, after, me, *more)
    return call("step", kernel, values, specs, shape, after)


def product(me, chunk, columns, total, begin, distances, parts, after):
    share = total.shape[2]
    width = share // parts
    group = max(1, min(len(distances), 1024 // share))

    def kernel(me_ref, chunk_ref, columns_ref, total_ref, *refs):
        outs = refs[-parts:]
        for at in range(0, len(distances), group):
            start = (begin + at) * share
            sums = jnp.dot(
                chunk_ref[...], columns_ref[:, start:start + group * share], preferred_element_type=F32
            )
            for i in range(group):
                value = total_ref[distances[at + i] ^ me_ref[0]] + sums[:, i * share:(i + 1) * share]
                for part in range(parts):
                    outs[part][at + i] = value[:, part * width:(part + 1) * width]

    shapes = [jax.ShapeDtypeStruct((len(distances), chunk.shape[0], width), F32)] * parts
    return call("product", kernel, (me, chunk, columns, total), [SMEM] + [VMEM] * 3, shapes, after)


def halve(own, got, distances, plans, after):
    shapes = []
    for rows, _ in plans:
        shapes += [jax.ShapeDtypeStruct((len(distances) // 2, rows[1] - rows[0], own.shape[2]), F32)] * 2

    def kernel(own_ref, got_ref, *refs):
        outs = refs[-len(shapes):]
        for at, ((begin, end), bit) in enumerate(plans):
            for place, d in enumerate(d for d in distances if not d & bit):
                for out, source in ((outs[2 * at], d), (outs[2 * at + 1], d | bit)):
                    i = distances.index(source)
                    out[place] = own_ref[i, begin:end, :] + got_ref[i, begin:end, :]

    return call("halve", kernel, (own, got), (VMEM, VMEM), shapes, after)


def tick(after):
    def kernel(*refs):
        refs[-1][...] = jnp.zeros_like(refs[-1])

    return call("tick", kernel, (), (), jax.ShapeDtypeStruct((8, LANES), F32), after)


def finish(pieces, own, got, tokens, width, parts, after):
    held = [x for _, _, x in pieces[:-1]] if len(pieces) > 1 else []

    def kernel(own_ref, got_ref, *refs):
        out = refs[-1]
        value = (own_ref[0] + got_ref[0]).astype(BF16)
        if not pieces:
            out[...] = value
            return
        for ((begin, end), part, _), ref in zip(pieces, [*refs[:len(held)], None]):
            out[begin:end, part * width:(part + 1) * width] = value if ref is None else ref[...]

    shape = (tokens, width * parts) if pieces else own.shape[1:]
    operands = (own, got, *held)
    return call("finish", kernel, operands, [VMEM] * len(operands), jax.ShapeDtypeStruct(shape, BF16), after)


class Links:
    def __init__(self, bits):
        self.bits = bits
        self.taken = {bit: [] for bit in bits}

    def needs(self, bit, size):
        if bit == self.bits[0]:
            return {bit: size * 8e-6}
        if bit != self.bits[-1]:
            return {bit: size * 80e-6}
        return {bit: size * 160e-6, self.bits[-2]: size * 80e-6}

    def free(self, bit, now):
        share, until = 1.0, float("inf")
        for begin, end, used in self.taken[bit]:
            if begin <= now < end:
                share -= used
            if begin <= now < end or begin > now:
                until = min(until, end if begin <= now else begin)
        return max(share, 0.0), until

    def send(self, bit, size, now):
        needs = self.needs(bit, size)
        now += 1.0
        left = 1.0
        spans = []
        while left > 1e-6:
            shares = [(self.free(link, now), need) for link, need in needs.items()]
            rate = min(share / need for (share, _), need in shares)
            until = min(until for (_, until), _ in shares)
            if rate > 1e-6:
                until = min(until, now + left / rate)
                spans.append((now, until, rate))
                left -= rate * (until - now)
            now = until
        for begin, end, rate in spans:
            for link, need in needs.items():
                self.taken[link].append((begin, end, rate * need))
        return now + 0.3


def body(activations, rotation_small, down_weight):
    shards = lax.axis_size("tensor")
    me = lax.axis_index("tensor").astype(jnp.int32).reshape(1)
    tokens, local = activations.shape
    block = rotation_small.shape[0]
    share = down_weight.shape[1] // shards
    factor = (local // block * shards) ** (-0.5)
    bits = [1 << place for place in range(shards.bit_length() - 1)]
    assert len(bits) >= 3 and shards == 1 << len(bits)
    after = []

    def swap(x, bit):
        return lax.ppermute(x, "tensor", [(d, d ^ bit) for d in range(shards)])

    def ran(outs, link=-1):
        after[:] = [jax.tree.leaves(outs)[link]]
        return outs

    parts = 2 if share % (2 * LANES) == 0 else 1
    width = share // parts
    near = [d for d in range(shards) if not d & bits[0]]
    distances = [d | bits[0] for d in near] + near

    tiles = -(-local // LANES)
    count = len(TILES)
    edges = [min(local, round(tiles * sum(TILES[:c]) / sum(TILES)) * LANES) for c in range(count + 1)]
    assert all(begin < end for begin, end in zip(edges[:-1], edges[1:]))
    spans = list(zip(edges[:-1], edges[1:]))
    chunks = []
    for span in spans:
        chunks.append(ran(mix(activations, rotation_small, (0, tokens), span, after)))
    cycle = bits[:0:-1] + bits[:1]
    rank = {bit: place for place, bit in enumerate(bits[:-2] + bits[:-3:-1])}
    events = [(phase, cycle[(phase - c) % len(bits)], c) for phase in range(len(bits)) for c in range(count)]
    events.sort(key=lambda event: (event[0], rank[event[1]]))
    final = [c for phase, _, c in events if phase == len(bits) - 1]
    loads = [final[i] for i in (PERM if count == len(PERM) else range(count))]
    total = None
    loaded = []
    room = 37 * 2**20

    def wanted():
        nonlocal room
        c = loads[len(loaded)]
        limit = room // 2**20 + (0 if loaded else 3)
        room -= (spans[c][1] - spans[c][0]) * down_weight.shape[1] * 2
        return me, down_weight, spans[c], distances if c == final[-1] else (), limit

    for number, (phase, bit, c) in enumerate(events):
        got = swap(chunks[c], bit)
        last = phase == len(bits) - 1
        scale = factor if last else None
        if number == 6 and len(loaded) < count - 1:
            chunks[c], columns = ran(fold(me, chunks[c], got, bit, after, scale, *wanted()[1:]), 0)
            loaded.append(columns)
        else:
            chunks[c] = ran(fold(me, chunks[c], got, bit, after, scale))
        while number == 0 and len(loaded) < count - 2:
            loaded.append(ran(load(*wanted(), after), 0)[1])
        if last and c != final[-1]:
            columns = loaded[loads.index(c)]
            if len(loaded) < count:
                total, columns = ran(step(me, chunks[c], columns, total, shards, after, *wanted()[1:]), 0)
                loaded.append(columns)
            else:
                total = ran(step(me, chunks[c], columns, total, shards, after))

    inner = bits[1:]
    late = inner[:1] + inner[:0:-1]
    swapped = [inner[1], inner[0]] + inner[2:]
    half = tokens // 2
    routes = [
        [((0, half), swapped), ((half, tokens), late)],
        [((0, half), inner), ((half, tokens), swapped)],
    ][:parts]
    links = Links(bits)
    clock = 0.0
    kernels = 0
    pieces = []
    queue = []

    def send(x, bit, use):
        nonlocal clock
        clock += 0.9
        queue.append((links.send(bit, x.size, clock), kernels, swap(x, bit), use))

    def split(part, stage, pieces_of, left, keep, got):
        base = pieces_of[0][0][0]
        plans = [((begin - base, end - base), route[stage]) for (begin, end), route in pieces_of]
        outs = ran(halve(keep, got, left, plans, after))
        for i, (rows, route) in enumerate(pieces_of):
            rest = [d for d in left if not d & route[stage]]
            if stage + 1 < len(inner):
                use = functools.partial(split, part, stage + 1, [(rows, route)], rest, outs[2 * i])
            else:
                use = functools.partial(close, part, rows, outs[2 * i])
            send(outs[2 * i + 1], route[stage], use)

    def close(part, rows, keep, got):
        last = len(pieces) + 1 == parts * len(routes[0])
        held = pieces + [(rows, part, None)] if last else []
        pieces.append((rows, part, ran(finish(held, keep, got, tokens, width, parts, after))))

    last_chunk, last_columns = chunks[final[-1]], loaded[loads.index(final[-1])]
    sends = ran(product(me, last_chunk, last_columns, total, 0, distances[:len(near)], parts, after))
    clock += 0.9
    kernels += 1
    for x in sends:
        send(x, bits[0], None)
    keeps = ran(product(me, last_chunk, last_columns, total, len(near), near, parts, after))
    clock += 0.9
    kernels += 1
    queue[:] = [
        (when, at, got, functools.partial(split, part, 0, routes[part], near, keeps[part]))
        for part, (when, at, got, _) in enumerate(queue)
    ]
    while queue:
        item = min(queue, key=lambda item: item[0])
        queue.remove(item)
        when, at, got, use = item
        if at == kernels:
            ran(tick(after))
            kernels += 1
            clock += 0.1
        clock = max(clock, when) + 0.15
        kernels += 1
        use(got)
    return pieces[-1][2]


def solution(mesh):
    placed = (P("groups", "tensor"), P(), P("tensor", None))
    return jax.shard_map(
        body, mesh=mesh, in_specs=placed, out_specs=P("groups", "tensor"), check_vma=False
    )
```

```python
import functools

import jax
import jax.numpy as jnp
import numpy as np
from jax import lax
from jax.experimental import pallas as pl
from jax.experimental.pallas import tpu as pltpu
from jax.sharding import PartitionSpec as P

LANES = 128
F32 = jnp.float32
BF16 = jnp.bfloat16


TILES = (4, 3, 3, 3)
DIRECT = 2
PIECES = 4
PERM = (0, 3, 2, 1)


def quotient(index, divisor, limit):
    shift = 16
    scale = -(-(1 << shift) // divisor)
    numbers = np.arange(limit, dtype=np.int64)
    assert np.array_equal((numbers * scale) >> shift, numbers // divisor)
    assert limit * scale < 2**31
    return (index * scale) >> shift


def sign_of(common, count):
    parity = common
    for place in range(1, count):
        parity = parity ^ (common >> place)
    return (1 - 2 * (parity & 1)).astype(F32)


def mix_kernel(rows, start, group, activations, small, *refs):
    out = refs[-1]
    local = activations.shape[1]
    block = small.shape[0]
    tokens, cols = out.shape
    tall = group * block
    span = local // block
    low = group.bit_length() - 1
    high = span.bit_length() - 1 - low
    full = small[...]
    head = full.astype(BF16)
    tail = (full - head.astype(F32)).astype(BF16)

    row = lax.broadcasted_iota(jnp.int32, (tall, block), 0)
    unit = lax.broadcasted_iota(jnp.int32, (tall, block), 1)
    spread_rows = (row - quotient(row, block, tall) * block == unit).astype(F32).astype(BF16)
    col = lax.broadcasted_iota(jnp.int32, (block, cols), 1) + start
    unit = lax.broadcasted_iota(jnp.int32, (block, cols), 0)
    spread_cols = (col - quotient(col, block, local) * block == unit).astype(F32).astype(BF16)
    at_row = quotient(lax.broadcasted_iota(jnp.int32, (tall, cols), 0), block, tall)
    at_col = quotient(lax.broadcasted_iota(jnp.int32, (tall, cols), 1) + start, block, local)
    sign = sign_of(at_row & at_col, max(low, 1))

    def tiled(part):
        rolled = jnp.dot(spread_rows, part, preferred_element_type=F32).astype(BF16)
        return (jnp.dot(rolled, spread_cols, preferred_element_type=F32) * sign).astype(BF16)

    head, tail = tiled(head), tiled(tail)
    owner = quotient(lax.broadcasted_iota(jnp.int32, (8, cols), 1) + start, block, local) >> low
    total = jnp.zeros((tokens, cols), F32)
    for piece in range(span // group):
        values = activations[rows[0]:rows[1], piece * tall:(piece + 1) * tall]
        term = jnp.dot(values, head, preferred_element_type=F32)
        term = term + jnp.dot(values, tail, preferred_element_type=F32)
        total = total + term * sign_of(owner & piece, max(high, 1))[0:1]
    out[...] = total


VMEM = pl.BlockSpec(memory_space=pltpu.VMEM)
SMEM = pl.BlockSpec(memory_space=pltpu.SMEM)
UNREAD = pl.BlockSpec(memory_space=pl.ANY)
COST = pl.CostEstimate(flops=10**10, bytes_accessed=10**8, transcendentals=0)


def call(name, kernel, operands, specs, shapes, after, scratch=(), limit=8):
    return pl.pallas_call(
        kernel,
        out_shape=shapes,
        in_specs=list(specs) + [UNREAD] * len(after),
        out_specs=jax.tree.map(lambda _: VMEM, shapes),
        scratch_shapes=list(scratch),
        cost_estimate=COST,
        compiler_params=pltpu.CompilerParams(vmem_limit_bytes=limit * 2**20),
        name=name,
    )(*operands, *after)


def mix(activations, small, rows, cols, after):
    block = small.shape[0]
    group = min(4, activations.shape[1] // block)
    kernel = functools.partial(mix_kernel, rows, cols[0], group)
    shape = jax.ShapeDtypeStruct((rows[1] - rows[0], cols[1] - cols[0]), F32)
    return call("mix", kernel, (activations, small), (VMEM, VMEM), shape, after)


def fetch(me, weight, out, sems, rows, distances):
    begin, end = rows
    copies = []
    if not distances:
        each = (end - begin) // PIECES // 16 * 16
        for i in range(PIECES):
            low, high = i * each, (i + 1) * each if i + 1 < PIECES else end - begin
            copies.append(
                pltpu.make_async_copy(weight.at[begin + low:begin + high, :], out.at[low:high, :], sems.at[i])
            )
    for i, distance in enumerate(distances):
        share = weight.shape[1] // len(distances)
        column = pl.multiple_of((distance ^ me) * share, LANES)
        copies.append(
            pltpu.make_async_copy(
                weight.at[begin:end, pl.ds(column, share)], out.at[:, pl.ds(i * share, share)], sems.at[i]
            )
        )
    for copy in copies:
        copy.start()
    return copies


def loading(name, work, operands, specs, shape, after, me, weight, rows, distances, limit):
    count = len(operands)

    def kernel(me_ref, weight_ref, *refs):
        columns, out, sems = refs[-3:]
        copies = fetch(me_ref[0], weight_ref, columns, sems, rows, distances)
        work(me_ref, refs[:count], out)
        for copy in copies:
            copy.wait()

    columns = jax.ShapeDtypeStruct((rows[1] - rows[0], weight.shape[1]), BF16)
    outs = call(
        name,
        kernel,
        (me, weight, *operands),
        [SMEM, pl.BlockSpec(memory_space=pltpu.HBM), *specs],
        [columns, shape],
        after,
        [pltpu.SemaphoreType.DMA((max(PIECES, len(distances)),))],
        limit,
    )
    return outs[1], outs[0]


def load(me, weight, rows, distances, limit, after):
    def work(me_ref, refs, out):
        out[...] = jnp.zeros_like(out)

    shape = jax.ShapeDtypeStruct((8, LANES), F32)
    return loading("load", work, (), (), shape, after, me, weight, rows, distances, limit)


def fold(me, own, got, bit, after, factor=None, *more):
    def work(me_ref, refs, out):
        own_ref, got_ref = refs
        sign = jnp.where((me_ref[0] & bit) != 0, -1.0, 1.0).astype(F32)
        total = got_ref[...] + own_ref[...] * sign
        if factor is not None:
            total = total * factor
        out[...] = total.astype(out.dtype)

    def kernel(me_ref, *refs):
        work(me_ref, refs[:2], refs[-1])

    shape = jax.ShapeDtypeStruct(own.shape, F32 if factor is None else BF16)
    if more:
        return loading("fold", work, (own, got), (VMEM, VMEM), shape, after, me, *more)
    return call("fold", kernel, (me, own, got), (SMEM, VMEM, VMEM), shape, after)


def step(me, chunk, columns, total, shards, after, *more):
    tokens = chunk.shape[0]
    share = columns.shape[1] // shards
    group = max(1, 1024 // share)
    values = [chunk, columns] + ([] if total is None else [total])

    def work(me_ref, refs, out):
        for at in range(0, shards, group):
            sums = jnp.dot(refs[0][...], refs[1][:, at * share:(at + group) * share], preferred_element_type=F32)
            for i in range(group):
                term = sums[:, i * share:(i + 1) * share]
                out[at + i] = term if total is None else refs[2][at + i] + term

    def kernel(*refs):
        work(None, refs, refs[-1])

    shape = jax.ShapeDtypeStruct((shards, tokens, share), F32)
    specs = [VMEM] * len(values)
    if more:
        return loading("step", work, values, specs, shape, after, me, *more)
    return call("step", kernel, values, specs, shape, after)


def product(me, factors, total, begin, distances, parts, after):
    share = total.shape[2]
    width = share // parts
    count = len(factors)

    def kernel(me_ref, total_ref, *refs):
        chunks, weights, outs = refs[:count], refs[count:2 * count], refs[-parts:]
        for at, distance in enumerate(distances):
            owner = distance ^ me_ref[0]
            value = total_ref[owner]
            for (_, _, in_order), chunk, columns in zip(factors, chunks, weights):
                start = (begin + at) * share if in_order else pl.multiple_of(owner * share, LANES)
                value = value + jnp.dot(
                    chunk[...], columns[:, pl.ds(start, share)], preferred_element_type=F32
                )
            for part in range(parts):
                outs[part][at] = value[:, part * width:(part + 1) * width]

    tokens = factors[0][0].shape[0]
    shapes = [jax.ShapeDtypeStruct((len(distances), tokens, width), F32)] * parts
    operands = (me, total, *[f[0] for f in factors], *[f[1] for f in factors])
    return call("product", kernel, operands, [SMEM] + [VMEM] * (1 + 2 * count), shapes, after)


def halve(own, got, distances, plans, after):
    shapes = []
    for rows, _ in plans:
        shapes += [jax.ShapeDtypeStruct((len(distances) // 2, rows[1] - rows[0], own.shape[2]), F32)] * 2

    def kernel(own_ref, got_ref, *refs):
        outs = refs[-len(shapes):]
        for at, ((begin, end), bit) in enumerate(plans):
            for place, d in enumerate(d for d in distances if not d & bit):
                for out, source in ((outs[2 * at], d), (outs[2 * at + 1], d | bit)):
                    i = distances.index(source)
                    out[place] = own_ref[i, begin:end, :] + got_ref[i, begin:end, :]

    return call("halve", kernel, (own, got), (VMEM, VMEM), shapes, after)


def tick(after):
    def kernel(*refs):
        refs[-1][...] = jnp.zeros_like(refs[-1])

    return call("tick", kernel, (), (), jax.ShapeDtypeStruct((8, LANES), F32), after)


def finish(pieces, own, got, tokens, width, parts, after):
    held = [x for _, _, x in pieces[:-1]] if len(pieces) > 1 else []

    def kernel(own_ref, got_ref, *refs):
        out = refs[-1]
        value = (own_ref[0] + got_ref[0]).astype(BF16)
        if not pieces:
            out[...] = value
            return
        for ((begin, end), part, _), ref in zip(pieces, [*refs[:len(held)], None]):
            out[begin:end, part * width:(part + 1) * width] = value if ref is None else ref[...]

    shape = (tokens, width * parts) if pieces else own.shape[1:]
    operands = (own, got, *held)
    return call("finish", kernel, operands, [VMEM] * len(operands), jax.ShapeDtypeStruct(shape, BF16), after)


class Links:
    def __init__(self, bits):
        self.bits = bits
        self.taken = {bit: [] for bit in bits}

    def needs(self, bit, size):
        if bit == self.bits[0]:
            return {bit: size * 8e-6}
        if bit != self.bits[-1]:
            return {bit: size * 80e-6}
        return {bit: size * 160e-6, self.bits[-2]: size * 80e-6}

    def free(self, bit, now):
        share, until = 1.0, float("inf")
        for begin, end, used in self.taken[bit]:
            if begin <= now < end:
                share -= used
            if begin <= now < end or begin > now:
                until = min(until, end if begin <= now else begin)
        return max(share, 0.0), until

    def send(self, bit, size, now):
        needs = self.needs(bit, size)
        now += 1.0
        left = 1.0
        spans = []
        while left > 1e-6:
            shares = [(self.free(link, now), need) for link, need in needs.items()]
            rate = min(share / need for (share, _), need in shares)
            until = min(until for (_, until), _ in shares)
            if rate > 1e-6:
                until = min(until, now + left / rate)
                spans.append((now, until, rate))
                left -= rate * (until - now)
            now = until
        for begin, end, rate in spans:
            for link, need in needs.items():
                self.taken[link].append((begin, end, rate * need))
        return now + 0.3


def body(activations, rotation_small, down_weight):
    shards = lax.axis_size("tensor")
    me = lax.axis_index("tensor").astype(jnp.int32).reshape(1)
    tokens, local = activations.shape
    block = rotation_small.shape[0]
    share = down_weight.shape[1] // shards
    factor = (local // block * shards) ** (-0.5)
    bits = [1 << place for place in range(shards.bit_length() - 1)]
    assert len(bits) >= 3 and shards == 1 << len(bits)
    after = []

    def swap(x, bit):
        return lax.ppermute(x, "tensor", [(d, d ^ bit) for d in range(shards)])

    def ran(outs, link=-1):
        after[:] = [jax.tree.leaves(outs)[link]]
        return outs

    parts = 2 if share % (2 * LANES) == 0 else 1
    width = share // parts
    near = [d for d in range(shards) if not d & bits[0]]
    distances = [d | bits[0] for d in near] + near

    tiles = -(-local // LANES)
    count = len(TILES)
    edges = [min(local, round(tiles * sum(TILES[:c]) / sum(TILES)) * LANES) for c in range(count + 1)]
    assert all(begin < end for begin, end in zip(edges[:-1], edges[1:]))
    spans = list(zip(edges[:-1], edges[1:]))
    chunks = []
    for span in spans:
        chunks.append(ran(mix(activations, rotation_small, (0, tokens), span, after)))
    cycle = bits[:0:-1] + bits[:1]
    rank = {bit: place for place, bit in enumerate(bits[:-2] + bits[:-3:-1])}
    events = [(phase, cycle[(phase - c) % len(bits)], c) for phase in range(len(bits)) for c in range(count)]
    events.sort(key=lambda event: (event[0], rank[event[1]]))
    final = [c for phase, _, c in events if phase == len(bits) - 1]
    loads = [final[i] for i in (PERM if count == len(PERM) else range(count))]
    total = None
    loaded = []
    room = 37 * 2**20

    def wanted():
        nonlocal room
        c = loads[len(loaded)]
        limit = room // 2**20 + (0 if loaded else 3)
        room -= (spans[c][1] - spans[c][0]) * down_weight.shape[1] * 2
        return me, down_weight, spans[c], distances if c == final[-1] else (), limit

    for number, (phase, bit, c) in enumerate(events):
        got = swap(chunks[c], bit)
        last = phase == len(bits) - 1
        scale = factor if last else None
        if number == 1 and len(loaded) < count - 1:
            chunks[c], columns = ran(fold(me, chunks[c], got, bit, after, scale, *wanted()[1:]), 0)
            loaded.append(columns)
        else:
            chunks[c] = ran(fold(me, chunks[c], got, bit, after, scale))
        while number == 0 and len(loaded) < count - 2:
            loaded.append(ran(load(*wanted(), after), 0)[1])
        if last and c in final[:count - DIRECT]:
            columns = loaded[loads.index(c)]
            if len(loaded) < count:
                total, columns = ran(step(me, chunks[c], columns, total, shards, after, *wanted()[1:]), 0)
                loaded.append(columns)
            else:
                total = ran(step(me, chunks[c], columns, total, shards, after))

    inner = bits[1:]
    late = inner[:1] + inner[:0:-1]
    swapped = [inner[1], inner[0]] + inner[2:]
    half = tokens // 2
    routes = [
        [((0, half), swapped), ((half, tokens), late)],
        [((0, half), inner), ((half, tokens), swapped)],
    ][:parts]
    links = Links(bits)
    clock = 0.0
    kernels = 0
    pieces = []
    queue = []

    def send(x, bit, use):
        nonlocal clock
        clock += 0.9
        queue.append((links.send(bit, x.size, clock), kernels, swap(x, bit), use))

    def split(part, stage, pieces_of, left, keep, got):
        base = pieces_of[0][0][0]
        plans = [((begin - base, end - base), route[stage]) for (begin, end), route in pieces_of]
        outs = ran(halve(keep, got, left, plans, after))
        for i, (rows, route) in enumerate(pieces_of):
            rest = [d for d in left if not d & route[stage]]
            if stage + 1 < len(inner):
                use = functools.partial(split, part, stage + 1, [(rows, route)], rest, outs[2 * i])
            else:
                use = functools.partial(close, part, rows, outs[2 * i])
            send(outs[2 * i + 1], route[stage], use)

    def close(part, rows, keep, got):
        last = len(pieces) + 1 == parts * len(routes[0])
        held = pieces + [(rows, part, None)] if last else []
        pieces.append((rows, part, ran(finish(held, keep, got, tokens, width, parts, after))))

    factors = [(chunks[c], loaded[loads.index(c)], c == final[-1]) for c in final[count - DIRECT:]]
    sends = ran(product(me, factors, total, 0, distances[:len(near)], parts, after))
    clock += 0.9
    kernels += 1
    for x in sends:
        send(x, bits[0], None)
    keeps = ran(product(me, factors, total, len(near), near, parts, after))
    clock += 0.9
    kernels += 1
    queue[:] = [
        (when, at, got, functools.partial(split, part, 0, routes[part], near, keeps[part]))
        for part, (when, at, got, _) in enumerate(queue)
    ]
    while queue:
        item = min(queue, key=lambda item: item[0])
        queue.remove(item)
        when, at, got, use = item
        if at == kernels:
            ran(tick(after))
            kernels += 1
            clock += 0.1
        clock = max(clock, when) + 0.15
        kernels += 1
        use(got)
    return pieces[-1][2]


def solution(mesh):
    placed = (P("groups", "tensor"), P(), P("tensor", None))
    return jax.shard_map(
        body, mesh=mesh, in_specs=placed, out_specs=P("groups", "tensor"), check_vma=False
    )
```

```python
import functools

import jax
import jax.numpy as jnp
import numpy as np
from jax import lax
from jax.experimental import pallas as pl
from jax.experimental.pallas import tpu as pltpu
from jax.sharding import PartitionSpec as P

LANES = 128
F32 = jnp.float32
BF16 = jnp.bfloat16


TILES = (3, 3, 3, 4)
DIRECT = 2
PIECES = 4
PERM = (0, 1, 3, 2)


def quotient(index, divisor, limit):
    shift = 16
    scale = -(-(1 << shift) // divisor)
    numbers = np.arange(limit, dtype=np.int64)
    assert np.array_equal((numbers * scale) >> shift, numbers // divisor)
    assert limit * scale < 2**31
    return (index * scale) >> shift


def sign_of(common, count):
    parity = common
    for place in range(1, count):
        parity = parity ^ (common >> place)
    return (1 - 2 * (parity & 1)).astype(F32)


def mix_kernel(rows, start, group, activations, small, *refs):
    out = refs[-1]
    local = activations.shape[1]
    block = small.shape[0]
    tokens, cols = out.shape
    tall = group * block
    span = local // block
    low = group.bit_length() - 1
    high = span.bit_length() - 1 - low
    full = small[...]
    head = full.astype(BF16)
    tail = (full - head.astype(F32)).astype(BF16)

    row = lax.broadcasted_iota(jnp.int32, (tall, block), 0)
    unit = lax.broadcasted_iota(jnp.int32, (tall, block), 1)
    spread_rows = (row - quotient(row, block, tall) * block == unit).astype(F32).astype(BF16)
    col = lax.broadcasted_iota(jnp.int32, (block, cols), 1) + start
    unit = lax.broadcasted_iota(jnp.int32, (block, cols), 0)
    spread_cols = (col - quotient(col, block, local) * block == unit).astype(F32).astype(BF16)
    at_row = quotient(lax.broadcasted_iota(jnp.int32, (tall, cols), 0), block, tall)
    at_col = quotient(lax.broadcasted_iota(jnp.int32, (tall, cols), 1) + start, block, local)
    sign = sign_of(at_row & at_col, max(low, 1))

    def tiled(part):
        rolled = jnp.dot(spread_rows, part, preferred_element_type=F32).astype(BF16)
        return (jnp.dot(rolled, spread_cols, preferred_element_type=F32) * sign).astype(BF16)

    head, tail = tiled(head), tiled(tail)
    owner = quotient(lax.broadcasted_iota(jnp.int32, (8, cols), 1) + start, block, local) >> low
    total = jnp.zeros((tokens, cols), F32)
    for piece in range(span // group):
        values = activations[rows[0]:rows[1], piece * tall:(piece + 1) * tall]
        term = jnp.dot(values, head, preferred_element_type=F32)
        term = term + jnp.dot(values, tail, preferred_element_type=F32)
        total = total + term * sign_of(owner & piece, max(high, 1))[0:1]
    out[...] = total


VMEM = pl.BlockSpec(memory_space=pltpu.VMEM)
SMEM = pl.BlockSpec(memory_space=pltpu.SMEM)
UNREAD = pl.BlockSpec(memory_space=pl.ANY)
COST = pl.CostEstimate(flops=10**10, bytes_accessed=10**8, transcendentals=0)


def call(name, kernel, operands, specs, shapes, after, scratch=(), limit=8):
    return pl.pallas_call(
        kernel,
        out_shape=shapes,
        in_specs=list(specs) + [UNREAD] * len(after),
        out_specs=jax.tree.map(lambda _: VMEM, shapes),
        scratch_shapes=list(scratch),
        cost_estimate=COST,
        compiler_params=pltpu.CompilerParams(vmem_limit_bytes=limit * 2**20),
        name=name,
    )(*operands, *after)


def mix(activations, small, rows, cols, after):
    block = small.shape[0]
    group = min(4, activations.shape[1] // block)
    kernel = functools.partial(mix_kernel, rows, cols[0], group)
    shape = jax.ShapeDtypeStruct((rows[1] - rows[0], cols[1] - cols[0]), F32)
    return call("mix", kernel, (activations, small), (VMEM, VMEM), shape, after)


def fetch(me, weight, out, sems, rows, distances):
    begin, end = rows
    copies = []
    if not distances:
        each = (end - begin) // PIECES // 16 * 16
        for i in range(PIECES):
            low, high = i * each, (i + 1) * each if i + 1 < PIECES else end - begin
            copies.append(
                pltpu.make_async_copy(weight.at[begin + low:begin + high, :], out.at[low:high, :], sems.at[i])
            )
    for i, distance in enumerate(distances):
        share = weight.shape[1] // len(distances)
        column = pl.multiple_of((distance ^ me) * share, LANES)
        copies.append(
            pltpu.make_async_copy(
                weight.at[begin:end, pl.ds(column, share)], out.at[:, pl.ds(i * share, share)], sems.at[i]
            )
        )
    for copy in copies:
        copy.start()
    return copies


def loading(name, work, operands, specs, shape, after, me, weight, rows, distances, limit):
    count = len(operands)

    def kernel(me_ref, weight_ref, *refs):
        columns, out, sems = refs[-3:]
        copies = fetch(me_ref[0], weight_ref, columns, sems, rows, distances)
        work(me_ref, refs[:count], out)
        for copy in copies:
            copy.wait()

    columns = jax.ShapeDtypeStruct((rows[1] - rows[0], weight.shape[1]), BF16)
    outs = call(
        name,
        kernel,
        (me, weight, *operands),
        [SMEM, pl.BlockSpec(memory_space=pltpu.HBM), *specs],
        [columns, shape],
        after,
        [pltpu.SemaphoreType.DMA((max(PIECES, len(distances)),))],
        limit,
    )
    return outs[1], outs[0]


def load(me, weight, rows, distances, limit, after):
    def work(me_ref, refs, out):
        out[...] = jnp.zeros_like(out)

    shape = jax.ShapeDtypeStruct((8, LANES), F32)
    return loading("load", work, (), (), shape, after, me, weight, rows, distances, limit)


def fold(me, own, got, bit, after, factor=None, *more):
    def work(me_ref, refs, out):
        own_ref, got_ref = refs
        sign = jnp.where((me_ref[0] & bit) != 0, -1.0, 1.0).astype(F32)
        total = got_ref[...] + own_ref[...] * sign
        if factor is not None:
            total = total * factor
        out[...] = total.astype(out.dtype)

    def kernel(me_ref, *refs):
        work(me_ref, refs[:2], refs[-1])

    shape = jax.ShapeDtypeStruct(own.shape, F32 if factor is None else BF16)
    if more:
        return loading("fold", work, (own, got), (VMEM, VMEM), shape, after, me, *more)
    return call("fold", kernel, (me, own, got), (SMEM, VMEM, VMEM), shape, after)


def step(me, chunk, columns, total, shards, after, *more):
    tokens = chunk.shape[0]
    share = columns.shape[1] // shards
    group = max(1, 1024 // share)
    values = [chunk, columns] + ([] if total is None else [total])

    def work(me_ref, refs, out):
        for at in range(0, shards, group):
            sums = jnp.dot(refs[0][...], refs[1][:, at * share:(at + group) * share], preferred_element_type=F32)
            for i in range(group):
                term = sums[:, i * share:(i + 1) * share]
                out[at + i] = term if total is None else refs[2][at + i] + term

    def kernel(*refs):
        work(None, refs, refs[-1])

    shape = jax.ShapeDtypeStruct((shards, tokens, share), F32)
    specs = [VMEM] * len(values)
    if more:
        return loading("step", work, values, specs, shape, after, me, *more)
    return call("step", kernel, values, specs, shape, after)


def product(me, factors, total, begin, distances, parts, after):
    share = total.shape[2]
    width = share // parts
    count = len(factors)

    def kernel(me_ref, total_ref, *refs):
        chunks, weights, outs = refs[:count], refs[count:2 * count], refs[-parts:]
        for at, distance in enumerate(distances):
            owner = distance ^ me_ref[0]
            value = total_ref[owner]
            for (_, _, in_order), chunk, columns in zip(factors, chunks, weights):
                start = (begin + at) * share if in_order else pl.multiple_of(owner * share, LANES)
                value = value + jnp.dot(
                    chunk[...], columns[:, pl.ds(start, share)], preferred_element_type=F32
                )
            for part in range(parts):
                outs[part][at] = value[:, part * width:(part + 1) * width]

    tokens = factors[0][0].shape[0]
    shapes = [jax.ShapeDtypeStruct((len(distances), tokens, width), F32)] * parts
    operands = (me, total, *[f[0] for f in factors], *[f[1] for f in factors])
    return call("product", kernel, operands, [SMEM] + [VMEM] * (1 + 2 * count), shapes, after)


def halve(own, got, distances, plans, after):
    shapes = []
    for rows, _ in plans:
        shapes += [jax.ShapeDtypeStruct((len(distances) // 2, rows[1] - rows[0], own.shape[2]), F32)] * 2

    def kernel(own_ref, got_ref, *refs):
        outs = refs[-len(shapes):]
        for at, ((begin, end), bit) in enumerate(plans):
            for place, d in enumerate(d for d in distances if not d & bit):
                for out, source in ((outs[2 * at], d), (outs[2 * at + 1], d | bit)):
                    i = distances.index(source)
                    out[place] = own_ref[i, begin:end, :] + got_ref[i, begin:end, :]

    return call("halve", kernel, (own, got), (VMEM, VMEM), shapes, after)


def tick(after):
    def kernel(*refs):
        refs[-1][...] = jnp.zeros_like(refs[-1])

    return call("tick", kernel, (), (), jax.ShapeDtypeStruct((8, LANES), F32), after)


def finish(pieces, own, got, tokens, width, parts, after):
    held = [x for _, _, x in pieces[:-1]] if len(pieces) > 1 else []

    def kernel(own_ref, got_ref, *refs):
        out = refs[-1]
        value = (own_ref[0] + got_ref[0]).astype(BF16)
        if not pieces:
            out[...] = value
            return
        for ((begin, end), part, _), ref in zip(pieces, [*refs[:len(held)], None]):
            out[begin:end, part * width:(part + 1) * width] = value if ref is None else ref[...]

    shape = (tokens, width * parts) if pieces else own.shape[1:]
    operands = (own, got, *held)
    return call("finish", kernel, operands, [VMEM] * len(operands), jax.ShapeDtypeStruct(shape, BF16), after)


class Links:
    def __init__(self, bits):
        self.bits = bits
        self.taken = {bit: [] for bit in bits}

    def needs(self, bit, size):
        if bit == self.bits[0]:
            return {bit: size * 8e-6}
        if bit != self.bits[-1]:
            return {bit: size * 80e-6}
        return {bit: size * 160e-6, self.bits[-2]: size * 80e-6}

    def free(self, bit, now):
        share, until = 1.0, float("inf")
        for begin, end, used in self.taken[bit]:
            if begin <= now < end:
                share -= used
            if begin <= now < end or begin > now:
                until = min(until, end if begin <= now else begin)
        return max(share, 0.0), until

    def send(self, bit, size, now):
        needs = self.needs(bit, size)
        now += 1.0
        left = 1.0
        spans = []
        while left > 1e-6:
            shares = [(self.free(link, now), need) for link, need in needs.items()]
            rate = min(share / need for (share, _), need in shares)
            until = min(until for (_, until), _ in shares)
            if rate > 1e-6:
                until = min(until, now + left / rate)
                spans.append((now, until, rate))
                left -= rate * (until - now)
            now = until
        for begin, end, rate in spans:
            for link, need in needs.items():
                self.taken[link].append((begin, end, rate * need))
        return now + 0.3


def body(activations, rotation_small, down_weight):
    shards = lax.axis_size("tensor")
    me = lax.axis_index("tensor").astype(jnp.int32).reshape(1)
    tokens, local = activations.shape
    block = rotation_small.shape[0]
    share = down_weight.shape[1] // shards
    factor = (local // block * shards) ** (-0.5)
    bits = [1 << place for place in range(shards.bit_length() - 1)]
    assert len(bits) >= 3 and shards == 1 << len(bits)
    after = []

    def swap(x, bit):
        return lax.ppermute(x, "tensor", [(d, d ^ bit) for d in range(shards)])

    def ran(outs, link=-1):
        after[:] = [jax.tree.leaves(outs)[link]]
        return outs

    parts = 2 if share % (2 * LANES) == 0 else 1
    width = share // parts
    near = [d for d in range(shards) if not d & bits[0]]
    distances = [d | bits[0] for d in near] + near

    tiles = -(-local // LANES)
    count = len(TILES)
    edges = [min(local, round(tiles * sum(TILES[:c]) / sum(TILES)) * LANES) for c in range(count + 1)]
    assert all(begin < end for begin, end in zip(edges[:-1], edges[1:]))
    spans = list(zip(edges[:-1], edges[1:]))
    chunks = []
    for span in spans:
        chunks.append(ran(mix(activations, rotation_small, (0, tokens), span, after)))
    cycle = bits[:0:-1] + bits[:1]
    rank = {bit: place for place, bit in enumerate(bits[:-2] + bits[:-3:-1])}
    events = [(phase, cycle[(phase - c) % len(bits)], c) for phase in range(len(bits)) for c in range(count)]
    events.sort(key=lambda event: (event[0], rank[event[1]]))
    final = [c for phase, _, c in events if phase == len(bits) - 1]
    loads = [final[i] for i in (PERM if count == len(PERM) else range(count))]
    total = None
    loaded = []
    room = 37 * 2**20

    def wanted():
        nonlocal room
        c = loads[len(loaded)]
        limit = room // 2**20 + (0 if loaded else 3)
        room -= (spans[c][1] - spans[c][0]) * down_weight.shape[1] * 2
        return me, down_weight, spans[c], distances if c == final[-1] else (), limit

    for number, (phase, bit, c) in enumerate(events):
        got = swap(chunks[c], bit)
        last = phase == len(bits) - 1
        scale = factor if last else None
        if number == 1 and len(loaded) < count - 1:
            chunks[c], columns = ran(fold(me, chunks[c], got, bit, after, scale, *wanted()[1:]), 0)
            loaded.append(columns)
        else:
            chunks[c] = ran(fold(me, chunks[c], got, bit, after, scale))
        while number == 0 and len(loaded) < count - 2:
            loaded.append(ran(load(*wanted(), after), 0)[1])
        if last and c in final[:count - DIRECT]:
            columns = loaded[loads.index(c)]
            if len(loaded) < count:
                total, columns = ran(step(me, chunks[c], columns, total, shards, after, *wanted()[1:]), 0)
                loaded.append(columns)
            else:
                total = ran(step(me, chunks[c], columns, total, shards, after))

    inner = bits[1:]
    late = inner[:1] + inner[:0:-1]
    swapped = [inner[1], inner[0]] + inner[2:]
    half = tokens // 2
    routes = [
        [((0, half), swapped), ((half, tokens), late)],
        [((0, half), inner), ((half, tokens), swapped)],
    ][:parts]
    links = Links(bits)
    clock = 0.0
    kernels = 0
    pieces = []
    queue = []

    def send(x, bit, use):
        nonlocal clock
        clock += 0.9
        queue.append((links.send(bit, x.size, clock), kernels, swap(x, bit), use))

    def split(part, stage, pieces_of, left, keep, got):
        base = pieces_of[0][0][0]
        plans = [((begin - base, end - base), route[stage]) for (begin, end), route in pieces_of]
        outs = ran(halve(keep, got, left, plans, after))
        for i, (rows, route) in enumerate(pieces_of):
            rest = [d for d in left if not d & route[stage]]
            if stage + 1 < len(inner):
                use = functools.partial(split, part, stage + 1, [(rows, route)], rest, outs[2 * i])
            else:
                use = functools.partial(close, part, rows, outs[2 * i])
            send(outs[2 * i + 1], route[stage], use)

    def close(part, rows, keep, got):
        last = len(pieces) + 1 == parts * len(routes[0])
        held = pieces + [(rows, part, None)] if last else []
        pieces.append((rows, part, ran(finish(held, keep, got, tokens, width, parts, after))))

    factors = [(chunks[c], loaded[loads.index(c)], c == final[-1]) for c in final[count - DIRECT:]]
    sends = ran(product(me, factors, total, 0, distances[:len(near)], parts, after))
    clock += 0.9
    kernels += 1
    for x in sends:
        send(x, bits[0], None)
    keeps = ran(product(me, factors, total, len(near), near, parts, after))
    clock += 0.9
    kernels += 1
    queue[:] = [
        (when, at, got, functools.partial(split, part, 0, routes[part], near, keeps[part]))
        for part, (when, at, got, _) in enumerate(queue)
    ]
    while queue:
        item = min(queue, key=lambda item: item[0])
        queue.remove(item)
        when, at, got, use = item
        if at == kernels:
            ran(tick(after))
            kernels += 1
            clock += 0.1
        clock = max(clock, when) + 0.15
        kernels += 1
        use(got)
    return pieces[-1][2]


def solution(mesh):
    placed = (P("groups", "tensor"), P(), P("tensor", None))
    return jax.shard_map(
        body, mesh=mesh, in_specs=placed, out_specs=P("groups", "tensor"), check_vma=False
    )
```

```python
import functools

import jax
import jax.numpy as jnp
import numpy as np
from jax import lax
from jax.experimental import pallas as pl
from jax.experimental.pallas import tpu as pltpu
from jax.sharding import PartitionSpec as P

LANES = 128
F32 = jnp.float32
BF16 = jnp.bfloat16


TILES = (3, 4, 3, 3)
DIRECT = 2
PIECES = 4
PERM = (0, 1, 3, 2)


def quotient(index, divisor, limit):
    shift = 16
    scale = -(-(1 << shift) // divisor)
    numbers = np.arange(limit, dtype=np.int64)
    assert np.array_equal((numbers * scale) >> shift, numbers // divisor)
    assert limit * scale < 2**31
    return (index * scale) >> shift


def sign_of(common, count):
    parity = common
    for place in range(1, count):
        parity = parity ^ (common >> place)
    return (1 - 2 * (parity & 1)).astype(F32)


def mix_kernel(rows, start, group, activations, small, *refs):
    out = refs[-1]
    local = activations.shape[1]
    block = small.shape[0]
    tokens, cols = out.shape
    tall = group * block
    span = local // block
    low = group.bit_length() - 1
    high = span.bit_length() - 1 - low
    full = small[...]
    head = full.astype(BF16)
    tail = (full - head.astype(F32)).astype(BF16)

    row = lax.broadcasted_iota(jnp.int32, (tall, block), 0)
    unit = lax.broadcasted_iota(jnp.int32, (tall, block), 1)
    spread_rows = (row - quotient(row, block, tall) * block == unit).astype(F32).astype(BF16)
    col = lax.broadcasted_iota(jnp.int32, (block, cols), 1) + start
    unit = lax.broadcasted_iota(jnp.int32, (block, cols), 0)
    spread_cols = (col - quotient(col, block, local) * block == unit).astype(F32).astype(BF16)
    at_row = quotient(lax.broadcasted_iota(jnp.int32, (tall, cols), 0), block, tall)
    at_col = quotient(lax.broadcasted_iota(jnp.int32, (tall, cols), 1) + start, block, local)
    sign = sign_of(at_row & at_col, max(low, 1))

    def tiled(part):
        rolled = jnp.dot(spread_rows, part, preferred_element_type=F32).astype(BF16)
        return (jnp.dot(rolled, spread_cols, preferred_element_type=F32) * sign).astype(BF16)

    head, tail = tiled(head), tiled(tail)
    owner = quotient(lax.broadcasted_iota(jnp.int32, (8, cols), 1) + start, block, local) >> low
    total = jnp.zeros((tokens, cols), F32)
    for piece in range(span // group):
        values = activations[rows[0]:rows[1], piece * tall:(piece + 1) * tall]
        term = jnp.dot(values, head, preferred_element_type=F32)
        term = term + jnp.dot(values, tail, preferred_element_type=F32)
        total = total + term * sign_of(owner & piece, max(high, 1))[0:1]
    out[...] = total


VMEM = pl.BlockSpec(memory_space=pltpu.VMEM)
SMEM = pl.BlockSpec(memory_space=pltpu.SMEM)
UNREAD = pl.BlockSpec(memory_space=pl.ANY)
COST = pl.CostEstimate(flops=10**10, bytes_accessed=10**8, transcendentals=0)


def call(name, kernel, operands, specs, shapes, after, scratch=(), limit=4):
    return pl.pallas_call(
        kernel,
        out_shape=shapes,
        in_specs=list(specs) + [UNREAD] * len(after),
        out_specs=jax.tree.map(lambda _: VMEM, shapes),
        scratch_shapes=list(scratch),
        cost_estimate=COST,
        compiler_params=pltpu.CompilerParams(vmem_limit_bytes=limit * 2**20),
        name=name,
    )(*operands, *after)


def mix(activations, small, rows, cols, after):
    block = small.shape[0]
    group = min(4, activations.shape[1] // block)
    kernel = functools.partial(mix_kernel, rows, cols[0], group)
    shape = jax.ShapeDtypeStruct((rows[1] - rows[0], cols[1] - cols[0]), F32)
    return call("mix", kernel, (activations, small), (VMEM, VMEM), shape, after)


def fetch(me, weight, out, sems, rows, distances):
    begin, end = rows
    copies = []
    if not distances:
        each = (end - begin) // PIECES // 16 * 16
        for i in range(PIECES):
            low, high = i * each, (i + 1) * each if i + 1 < PIECES else end - begin
            copies.append(
                pltpu.make_async_copy(weight.at[begin + low:begin + high, :], out.at[low:high, :], sems.at[i])
            )
    for i, distance in enumerate(distances):
        share = weight.shape[1] // len(distances)
        column = pl.multiple_of((distance ^ me) * share, LANES)
        copies.append(
            pltpu.make_async_copy(
                weight.at[begin:end, pl.ds(column, share)], out.at[:, pl.ds(i * share, share)], sems.at[i]
            )
        )
    for copy in copies:
        copy.start()
    return copies


def loading(name, work, operands, specs, shape, after, me, weight, rows, distances, limit):
    count = len(operands)

    def kernel(me_ref, weight_ref, *refs):
        columns, out, sems = refs[-3:]
        copies = fetch(me_ref[0], weight_ref, columns, sems, rows, distances)
        work(me_ref, refs[:count], out)
        for copy in copies:
            copy.wait()

    columns = jax.ShapeDtypeStruct((rows[1] - rows[0], weight.shape[1]), BF16)
    outs = call(
        name,
        kernel,
        (me, weight, *operands),
        [SMEM, pl.BlockSpec(memory_space=pltpu.HBM), *specs],
        [columns, shape],
        after,
        [pltpu.SemaphoreType.DMA((max(PIECES, len(distances)),))],
        limit,
    )
    return outs[1], outs[0]


def load(me, weight, rows, distances, limit, after):
    def work(me_ref, refs, out):
        out[...] = jnp.zeros_like(out)

    shape = jax.ShapeDtypeStruct((8, LANES), F32)
    return loading("load", work, (), (), shape, after, me, weight, rows, distances, limit)


def fold(me, own, got, bit, after, factor=None, *more):
    def work(me_ref, refs, out):
        own_ref, got_ref = refs
        sign = jnp.where((me_ref[0] & bit) != 0, -1.0, 1.0).astype(F32)
        total = got_ref[...] + own_ref[...] * sign
        if factor is not None:
            total = total * factor
        out[...] = total.astype(out.dtype)

    def kernel(me_ref, *refs):
        work(me_ref, refs[:2], refs[-1])

    shape = jax.ShapeDtypeStruct(own.shape, F32 if factor is None else BF16)
    if more:
        return loading("fold", work, (own, got), (VMEM, VMEM), shape, after, me, *more)
    return call("fold", kernel, (me, own, got), (SMEM, VMEM, VMEM), shape, after)


def step(me, chunk, columns, total, shards, after, *more):
    tokens = chunk.shape[0]
    share = columns.shape[1] // shards
    group = max(1, 1024 // share)
    values = [chunk, columns] + ([] if total is None else [total])

    def work(me_ref, refs, out):
        for at in range(0, shards, group):
            sums = jnp.dot(refs[0][...], refs[1][:, at * share:(at + group) * share], preferred_element_type=F32)
            for i in range(group):
                term = sums[:, i * share:(i + 1) * share]
                out[at + i] = term if total is None else refs[2][at + i] + term

    def kernel(*refs):
        work(None, refs, refs[-1])

    shape = jax.ShapeDtypeStruct((shards, tokens, share), F32)
    specs = [VMEM] * len(values)
    if more:
        return loading("step", work, values, specs, shape, after, me, *more)
    return call("step", kernel, values, specs, shape, after)


def product(me, factors, total, begin, distances, parts, after):
    share = total.shape[2]
    width = share // parts
    count = len(factors)

    def kernel(me_ref, total_ref, *refs):
        chunks, weights, outs = refs[:count], refs[count:2 * count], refs[-parts:]
        for at, distance in enumerate(distances):
            owner = distance ^ me_ref[0]
            value = total_ref[owner]
            for (_, _, in_order), chunk, columns in zip(factors, chunks, weights):
                start = (begin + at) * share if in_order else pl.multiple_of(owner * share, LANES)
                value = value + jnp.dot(
                    chunk[...], columns[:, pl.ds(start, share)], preferred_element_type=F32
                )
            for part in range(parts):
                outs[part][at] = value[:, part * width:(part + 1) * width]

    tokens = factors[0][0].shape[0]
    shapes = [jax.ShapeDtypeStruct((len(distances), tokens, width), F32)] * parts
    operands = (me, total, *[f[0] for f in factors], *[f[1] for f in factors])
    return call("product", kernel, operands, [SMEM] + [VMEM] * (1 + 2 * count), shapes, after)


def halve(own, got, distances, plans, after):
    shapes = []
    for rows, _ in plans:
        shapes += [jax.ShapeDtypeStruct((len(distances) // 2, rows[1] - rows[0], own.shape[2]), F32)] * 2

    def kernel(own_ref, got_ref, *refs):
        outs = refs[-len(shapes):]
        for at, ((begin, end), bit) in enumerate(plans):
            for place, d in enumerate(d for d in distances if not d & bit):
                for out, source in ((outs[2 * at], d), (outs[2 * at + 1], d | bit)):
                    i = distances.index(source)
                    out[place] = own_ref[i, begin:end, :] + got_ref[i, begin:end, :]

    return call("halve", kernel, (own, got), (VMEM, VMEM), shapes, after)


def tick(after):
    def kernel(*refs):
        refs[-1][...] = jnp.zeros_like(refs[-1])

    return call("tick", kernel, (), (), jax.ShapeDtypeStruct((8, LANES), F32), after)


def finish(pieces, own, got, tokens, width, parts, after):
    held = [x for _, _, x in pieces[:-1]] if len(pieces) > 1 else []

    def kernel(own_ref, got_ref, *refs):
        out = refs[-1]
        value = (own_ref[0] + got_ref[0]).astype(BF16)
        if not pieces:
            out[...] = value
            return
        for ((begin, end), part, _), ref in zip(pieces, [*refs[:len(held)], None]):
            out[begin:end, part * width:(part + 1) * width] = value if ref is None else ref[...]

    shape = (tokens, width * parts) if pieces else own.shape[1:]
    operands = (own, got, *held)
    return call("finish", kernel, operands, [VMEM] * len(operands), jax.ShapeDtypeStruct(shape, BF16), after)


class Links:
    def __init__(self, bits):
        self.bits = bits
        self.taken = {bit: [] for bit in bits}

    def needs(self, bit, size):
        if bit == self.bits[0]:
            return {bit: size * 8e-6}
        if bit != self.bits[-1]:
            return {bit: size * 80e-6}
        return {bit: size * 160e-6, self.bits[-2]: size * 80e-6}

    def free(self, bit, now):
        share, until = 1.0, float("inf")
        for begin, end, used in self.taken[bit]:
            if begin <= now < end:
                share -= used
            if begin <= now < end or begin > now:
                until = min(until, end if begin <= now else begin)
        return max(share, 0.0), until

    def send(self, bit, size, now):
        needs = self.needs(bit, size)
        now += 1.0
        left = 1.0
        spans = []
        while left > 1e-6:
            shares = [(self.free(link, now), need) for link, need in needs.items()]
            rate = min(share / need for (share, _), need in shares)
            until = min(until for (_, until), _ in shares)
            if rate > 1e-6:
                until = min(until, now + left / rate)
                spans.append((now, until, rate))
                left -= rate * (until - now)
            now = until
        for begin, end, rate in spans:
            for link, need in needs.items():
                self.taken[link].append((begin, end, rate * need))
        return now + 0.3


def body(activations, rotation_small, down_weight):
    shards = lax.axis_size("tensor")
    me = lax.axis_index("tensor").astype(jnp.int32).reshape(1)
    tokens, local = activations.shape
    block = rotation_small.shape[0]
    share = down_weight.shape[1] // shards
    factor = (local // block * shards) ** (-0.5)
    bits = [1 << place for place in range(shards.bit_length() - 1)]
    assert len(bits) >= 3 and shards == 1 << len(bits)
    after = []

    def swap(x, bit):
        return lax.ppermute(x, "tensor", [(d, d ^ bit) for d in range(shards)])

    def ran(outs, link=-1):
        after[:] = [jax.tree.leaves(outs)[link]]
        return outs

    parts = 2 if share % (2 * LANES) == 0 else 1
    width = share // parts
    near = [d for d in range(shards) if not d & bits[0]]
    distances = [d | bits[0] for d in near] + near

    tiles = -(-local // LANES)
    count = len(TILES)
    edges = [min(local, round(tiles * sum(TILES[:c]) / sum(TILES)) * LANES) for c in range(count + 1)]
    assert all(begin < end for begin, end in zip(edges[:-1], edges[1:]))
    spans = list(zip(edges[:-1], edges[1:]))
    chunks = []
    for span in spans:
        chunks.append(ran(mix(activations, rotation_small, (0, tokens), span, after)))
    cycle = bits[:0:-1] + bits[:1]
    rank = {bit: place for place, bit in enumerate(bits[:-2] + bits[:-3:-1])}
    events = [(phase, cycle[(phase - c) % len(bits)], c) for phase in range(len(bits)) for c in range(count)]
    events.sort(key=lambda event: (event[0], rank[event[1]]))
    final = [c for phase, _, c in events if phase == len(bits) - 1]
    loads = [final[i] for i in (PERM if count == len(PERM) else range(count))]
    total = None
    loaded = []
    room = 37 * 2**20

    def wanted():
        nonlocal room
        c = loads[len(loaded)]
        limit = room // 2**20 + (0 if loaded else 3)
        room -= (spans[c][1] - spans[c][0]) * down_weight.shape[1] * 2
        return me, down_weight, spans[c], distances if c == final[-1] else (), limit

    for number, (phase, bit, c) in enumerate(events):
        got = swap(chunks[c], bit)
        last = phase == len(bits) - 1
        scale = factor if last else None
        if number == 1 and len(loaded) < count - 1:
            chunks[c], columns = ran(fold(me, chunks[c], got, bit, after, scale, *wanted()[1:]), 0)
            loaded.append(columns)
        else:
            chunks[c] = ran(fold(me, chunks[c], got, bit, after, scale))
        while number == 0 and len(loaded) < count - 2:
            loaded.append(ran(load(*wanted(), after), 0)[1])
        if last and c in final[:count - DIRECT]:
            columns = loaded[loads.index(c)]
            if len(loaded) < count:
                total, columns = ran(step(me, chunks[c], columns, total, shards, after, *wanted()[1:]), 0)
                loaded.append(columns)
            else:
                total = ran(step(me, chunks[c], columns, total, shards, after))

    inner = bits[1:]
    late = inner[:1] + inner[:0:-1]
    swapped = [inner[1], inner[0]] + inner[2:]
    half = tokens // 2
    routes = [
        [((0, half), swapped), ((half, tokens), late)],
        [((0, half), inner), ((half, tokens), swapped)],
    ][:parts]
    links = Links(bits)
    clock = 0.0
    kernels = 0
    pieces = []
    queue = []

    def send(x, bit, use):
        nonlocal clock
        clock += 0.9
        queue.append((links.send(bit, x.size, clock), kernels, swap(x, bit), use))

    def split(part, stage, pieces_of, left, keep, got):
        base = pieces_of[0][0][0]
        plans = [((begin - base, end - base), route[stage]) for (begin, end), route in pieces_of]
        outs = ran(halve(keep, got, left, plans, after))
        for i, (rows, route) in enumerate(pieces_of):
            rest = [d for d in left if not d & route[stage]]
            if stage + 1 < len(inner):
                use = functools.partial(split, part, stage + 1, [(rows, route)], rest, outs[2 * i])
            else:
                use = functools.partial(close, part, rows, outs[2 * i])
            send(outs[2 * i + 1], route[stage], use)

    def close(part, rows, keep, got):
        last = len(pieces) + 1 == parts * len(routes[0])
        held = pieces + [(rows, part, None)] if last else []
        pieces.append((rows, part, ran(finish(held, keep, got, tokens, width, parts, after))))

    factors = [(chunks[c], loaded[loads.index(c)], c == final[-1]) for c in final[count - DIRECT:]]
    sends = ran(product(me, factors, total, 0, distances[:len(near)], parts, after))
    clock += 0.9
    kernels += 1
    for x in sends:
        send(x, bits[0], None)
    keeps = ran(product(me, factors, total, len(near), near, parts, after))
    clock += 0.9
    kernels += 1
    queue[:] = [
        (when, at, got, functools.partial(split, part, 0, routes[part], near, keeps[part]))
        for part, (when, at, got, _) in enumerate(queue)
    ]
    while queue:
        item = min(queue, key=lambda item: item[0])
        queue.remove(item)
        when, at, got, use = item
        if at == kernels:
            ran(tick(after))
            kernels += 1
            clock += 0.1
        clock = max(clock, when) + 0.15
        kernels += 1
        use(got)
    return pieces[-1][2]


def solution(mesh):
    placed = (P("groups", "tensor"), P(), P("tensor", None))
    return jax.shard_map(
        body, mesh=mesh, in_specs=placed, out_specs=P("groups", "tensor"), check_vma=False
    )
```
